32 devices in a mesh: idx: 8 (over z, x), slab: 4 (over y, core).
Axes of the slice: x: 2, y: 2, z: 4, core: 2. Of those that a mesh axis runs over, the one named last changes fastest.
Arguments:
- amplitudes: bfloat16 [512, 2, 16384], P(('idx', 'slab')), may hold values from -6 to 6
- pair_irreps: int32 [512], replicated, may hold values from 0 to 7
- slab_irreps: int32 [2], replicated, may hold values from 0 to 7
- ladder_ints: bfloat16 [512, 512], P(None, 'slab'), may hold values from -0.75 to 0.75
- vv_blocks: bfloat16 [8, 128, 128], P(None, 'slab'), may hold values from -0.5 to 0.5
Outputs:
- residual: float32 [512, 2, 16384], P(('idx', 'slab'))
The draws below stay inside these ranges and needn't reach their ends.
Inputs may be any that keep to these rules, and one draw needn't show every extreme that they name: `pair_irreps`: irrep labels. `slab_irreps`: irrep labels.
All inputs are finite; a program needn't handle non-finite values.
Results may differ from the reference program's by a relative error of at most 0.0055.
Values may be sent and summed in bfloat16 or wider, within the bound.
A program may use at most 128 MiB of HBM per device.

```python
import jax
import jax.numpy as jnp

BLK = 128
IRREPS = 8
SLABS = 2
PAIR_DEV = 16
PAIRS = 512
N_IDX = 8
N_SLAB = 4


def place_ends(values, own_key, low, largest):
    longest = values.shape.index(max(values.shape))
    spots = []
    for shift in (0, 1):
        where = [jax.random.randint(jax.random.fold_in(own_key, axis), (), 0, length) for axis, length in enumerate(values.shape)]
        where[longest] = (where[longest] + shift) % values.shape[longest]
        spots.append(tuple(where))
    return values.at[spots[0]].set(low).at[spots[1]].set(largest)


def steps_of(stream_key, dims, cuts, least, top_value):
    def one(dim, parts):
        heights = jax.random.uniform(jax.random.fold_in(jax.random.fold_in(stream_key, 6), dim), (parts,), jnp.float32, least / len(cuts), top_value / len(cuts))
        return jnp.repeat(jnp.exp(heights), dims[dim] // parts).reshape((-1,) + (1,) * (len(dims) - dim - 1))

    factor_of = one(*cuts[0])
    for cut in cuts[1:]:
        factor_of = factor_of * one(*cut)
    return factor_of


def scatter_about(rng, dims, deviation, reach, cuts=(), kind=jnp.bfloat16):
    result = jax.random.normal(rng, dims, jnp.float32) * deviation
    if len(cuts) > 0:
        result = steps_of(rng, dims, cuts, -0.22, 0.18) * result
    return jnp.clip(result, min=-reach, max=reach).astype(kind)


def setup_inputs(seed: int = 0) -> dict:
    key_of = jax.random.split(jax.random.key(seed), 6)
    return {
        "amplitudes": scatter_about(key_of[0], (PAIRS, SLABS, BLK * BLK), 1.0, 6.0, ((0, 32),)),
        "pair_irreps": place_ends(jax.random.randint(key_of[1], (PAIRS,), 0, 8), jax.random.fold_in(key_of[1], 1), 0, 7).astype(jnp.int32),
        "slab_irreps": jax.random.randint(key_of[2], (SLABS,), 0, 8).astype(jnp.int32),
        "ladder_ints": scatter_about(key_of[3], (PAIRS, N_SLAB * N_IDX * PAIR_DEV), (PAIRS // 8) ** -0.5, 0.75, ((1, 4),)),
        "vv_blocks": scatter_about(key_of[4], (IRREPS, BLK, BLK), BLK ** -0.5, 0.5, ((1, 4),)),
    }


def reference(amplitudes, pair_irreps, slab_irreps, ladder_ints, vv_blocks):
    allowed = pair_irreps[:, None] == pair_irreps[None, :]
    ordered = ladder_ints.reshape(PAIRS, N_SLAB, N_IDX, PAIR_DEV).transpose(0, 2, 1, 3).reshape(PAIRS, PAIRS)
    weights = jnp.where(allowed, ordered, jnp.zeros((), jnp.bfloat16))
    flat = amplitudes.reshape(PAIRS, SLABS * BLK * BLK)
    hole = jnp.dot(weights, flat, preferred_element_type=jnp.float32).astype(jnp.bfloat16)
    block = jnp.bitwise_xor(pair_irreps[:, None], slab_irreps[None, :])
    onehot = (block[:, :, None] == jnp.arange(IRREPS, dtype=jnp.int32)[None, None, :]).astype(jnp.float32)
    chosen = jnp.einsum("psg,gac->psac", onehot, vv_blocks.astype(jnp.float32))
    blocks4 = amplitudes.reshape(PAIRS, SLABS, BLK, BLK).astype(jnp.float32)
    particle = jnp.einsum("psac,pscb->psab", chosen, blocks4)
    return hole.astype(jnp.float32).reshape(PAIRS, SLABS, BLK * BLK) + particle.reshape(PAIRS, SLABS, BLK * BLK)
```

```python
import functools

import jax
import jax.numpy as jnp
from jax import lax
from jax.experimental import pallas as pl
from jax.experimental.pallas import tpu as pltpu
from jax.sharding import PartitionSpec as P

MESH = pl.DeviceIdType.MESH


def exchange_kernel(
    n_idx, n_slab, cw, t_ref, labels_ref, slab_labels_ref, row_ref, w_ref, v_ref, out_ref,
    recv, wfull, res, hole, vfull, rows_in, rows_out, labels, slab_labels,
    send1, recv1, send2, recv2, wsend, wrecv, vsend, vrecv, own_sems,
):
    n_dev = n_idx * n_slab
    pair_dev = t_ref.shape[1]
    square = t_ref.shape[2]
    width = t_ref.shape[0] * square // n_dev
    chunks = width // cw
    w_cols = w_ref.shape[1]
    v_rows = v_ref.shape[1]
    e = lax.axis_index("idx")
    s = lax.axis_index("slab")
    me = e * n_slab + s
    my_block = (s * n_idx + e) * pair_dev
    others = n_dev - 1

    def where(peer):
        return (peer // n_slab, peer % n_slab)

    barrier = pltpu.get_barrier_semaphore()

    def greet(j, carry):
        pl.semaphore_signal(barrier, inc=1, device_id=where((me + j) % n_dev), device_id_type=MESH)
        return carry

    lax.fori_loop(1, n_dev, greet, 0)
    pl.semaphore_wait(barrier, others)

    locals_ = [
        pltpu.make_async_copy(
            w_ref, wfull.at[:, pl.ds(pl.multiple_of(s * w_cols, 128), w_cols)], own_sems.at[0]
        ),
        pltpu.make_async_copy(
            v_ref, vfull.at[:, pl.ds(pl.multiple_of(s * v_rows, 16), v_rows), :], own_sems.at[1]
        ),
        pltpu.make_async_copy(labels_ref, labels, own_sems.at[2]),
        pltpu.make_async_copy(slab_labels_ref, slab_labels, own_sems.at[3]),
    ]
    for copy in locals_:
        copy.start()

    def order(j):
        return j

    def columns(device, k):
        first = device * width + k * cw
        return first // square, pl.ds(pl.multiple_of(first % square, 128), cw)

    def send_chunk(k):
        def body(j, carry):
            peer = (me + order(j)) % n_dev
            plane, place = columns(peer, k)
            pltpu.make_async_remote_copy(
                src_ref=t_ref.at[plane, :, place],
                dst_ref=recv.at[k, pl.ds(pl.multiple_of(my_block, 16), pair_dev), :],
                send_sem=send1,
                recv_sem=recv1.at[k],
                device_id=where(peer),
                device_id_type=MESH,
            ).start()
            return carry

        lax.fori_loop(1, n_dev, body, 0)
        plane, place = columns(me, k)
        recv[k, pl.ds(pl.multiple_of(my_block, 16), pair_dev), :] = t_ref[plane, :, place]

    def gather(j):
        peer = (s + j) % n_slab
        return (
            pltpu.make_async_remote_copy(
                src_ref=w_ref,
                dst_ref=wfull.at[:, pl.ds(pl.multiple_of(s * w_cols, 128), w_cols)],
                send_sem=wsend.at[j - 1],
                recv_sem=wrecv.at[j - 1],
                device_id=(e, peer),
                device_id_type=MESH,
            ),
            pltpu.make_async_remote_copy(
                src_ref=v_ref,
                dst_ref=vfull.at[:, pl.ds(pl.multiple_of(s * v_rows, 16), v_rows), :],
                send_sem=vsend.at[j - 1],
                recv_sem=vrecv.at[j - 1],
                device_id=(e, peer),
                device_id_type=MESH,
            ),
        )

    send_chunk(0)
    gathers = [gather(j) for j in range(1, n_slab)]
    for w_copy, v_copy in gathers:
        w_copy.start()
        v_copy.start()
    for k in range(1, chunks):
        send_chunk(k)
    for copy in locals_:
        copy.wait()
    for _, v_copy in gathers:
        v_copy.wait()

    side = vfull.shape[1]
    slabs = t_ref.shape[0]
    def particle(plane):

        def take(c, carry):
            rows_in[pl.ds(pl.multiple_of(c * pair_dev, 16), pair_dev), :] = t_ref[
                plane, :, pl.ds(pl.multiple_of(c * side, 128), side)
            ].astype(jnp.float32)
            return carry

        def one(i, carry):
            g = jnp.bitwise_xor(labels[me * pair_dev + i], slab_labels[plane])
            x = rows_in[pl.ds(i, side, stride=pair_dev), :].astype(jnp.bfloat16)
            rows_out[plane, pl.ds(i, side, stride=pair_dev), :] = jnp.dot(
                vfull[g], x, preferred_element_type=jnp.float32
            )
            return carry

        lax.fori_loop(0, side, take, 0, unroll=8)
        lax.fori_loop(0, pair_dev, one, 0, unroll=4)

    for plane in range(slabs):
        particle(plane)

    for w_copy, _ in gathers:
        w_copy.wait()

    pairs = recv.shape[1]
    tile = min(pairs, 512)
    irreps = vfull.shape[0]
    onehot = (
        row_ref[...] == lax.broadcasted_iota(jnp.int32, (irreps, pairs), 0)
    ).astype(jnp.float32).astype(jnp.bfloat16)

    def mask_columns(n, carry):
        cols = pl.ds(pl.multiple_of(n * tile, tile), tile)
        col = lax.broadcasted_iota(jnp.int32, (pairs, tile), 1) + n * tile
        row = lax.broadcasted_iota(jnp.int32, (pairs, tile), 0)
        p, q = col % pair_dev, col // pair_dev
        kl = ((q % n_idx) * n_slab + q // n_idx) * pair_dev + p
        moved = jnp.dot(
            onehot,
            (row == kl).astype(jnp.float32).astype(jnp.bfloat16),
            preferred_element_type=jnp.float32,
        ).astype(jnp.bfloat16)
        equal = lax.dot_general(
            onehot, moved, (((0,), (0,)), ((), ())), preferred_element_type=jnp.float32
        )
        wfull[:, cols] = jnp.where(
            equal > 0.5, wfull[:, cols].astype(jnp.float32), 0.0
        ).astype(jnp.bfloat16)
        return carry

    lax.fori_loop(0, pairs // tile, mask_columns, 0)

    for k in range(chunks):
        plane, place = columns(me, k)
        landed = recv.at[k, pl.ds(0, others * pair_dev), :]
        pltpu.make_async_copy(landed, landed, recv1.at[k]).wait()

        def multiply(m, carry):
            rows = pl.ds(pl.multiple_of(m * tile, tile), tile)
            res[k, rows, :] = jnp.dot(
                wfull[rows, :], recv[k], preferred_element_type=jnp.float32
            ).astype(jnp.bfloat16)
            return carry

        lax.fori_loop(0, pairs // tile, multiply, 0)

        def give(j, carry):
            peer = (me + order(j)) % n_dev
            pltpu.make_async_remote_copy(
                src_ref=res.at[k, pl.ds(pl.multiple_of(peer * pair_dev, 16), pair_dev), :],
                dst_ref=hole.at[plane, :, place],
                send_sem=send2,
                recv_sem=recv2.at[k],
                device_id=where(peer),
                device_id_type=MESH,
            ).start()
            return carry

        lax.fori_loop(1, n_dev, give, 0)
        hole[plane, :, place] = res[k, pl.ds(pl.multiple_of(me * pair_dev, 16), pair_dev), :]


    per_plane = n_dev // slabs
    for k in range(chunks):
        landed = recv.at[k, pl.ds(0, others * pair_dev), :]
        pltpu.make_async_copy(landed, landed, recv2.at[k]).wait()
        for plane in range(slabs):

            def finish(d, carry):
                for u in range(cw // side):
                    first = d * width + k * cw + u * side
                    cols = pl.ds(pl.multiple_of(first, 128), side)
                    rows = pl.ds(pl.multiple_of(first // side * pair_dev, 16), pair_dev)
                    out_ref[:, plane, cols] = rows_out[plane, rows, :] + hole[
                        plane, :, cols
                    ].astype(jnp.float32)
                return carry

            lax.fori_loop(0, per_plane, finish, 0, unroll=2)

    everything = recv.at[:, pl.ds(0, others * pair_dev), :]
    for sem in (send1, send2):
        pltpu.make_async_copy(everything, everything, sem).wait()


def exchange(t, pair_irreps, slab_irreps, w, v, n_idx, n_slab):
    slabs, pair_dev, square = t.shape
    n_dev = n_idx * n_slab
    pairs = w.shape[0]
    width = slabs * square // n_dev
    cw = min(width, 256)
    chunks = width // cw
    irreps, v_rows, side = v.shape
    block = (chunks, pairs, cw)
    vmem = pl.BlockSpec(memory_space=pltpu.VMEM)
    anywhere = pl.BlockSpec(memory_space=pl.ANY)
    held = 2 * (pairs * pairs + 12 * slabs * pair_dev * square)
    dma = pltpu.SemaphoreType.DMA
    return pl.pallas_call(
        functools.partial(exchange_kernel, n_idx, n_slab, cw),
        out_shape=jax.ShapeDtypeStruct((pair_dev, slabs, square), jnp.float32),
        in_specs=[vmem, anywhere, anywhere, vmem, anywhere, anywhere],
        out_specs=vmem,
        scratch_shapes=[
            pltpu.VMEM(block, jnp.bfloat16),
            pltpu.VMEM((pairs, pairs), jnp.bfloat16),
            pltpu.VMEM(block, jnp.bfloat16),
            pltpu.VMEM(t.shape, jnp.bfloat16),
            pltpu.VMEM((irreps, v_rows * n_slab, side), jnp.bfloat16),
            pltpu.VMEM((side * pair_dev, side), jnp.float32),
            pltpu.VMEM((slabs, side * pair_dev, side), jnp.float32),
            pltpu.SMEM(pair_irreps.shape, jnp.int32),
            pltpu.SMEM(slab_irreps.shape, jnp.int32),
            dma, dma((chunks,)), dma, dma((chunks,)),
            dma((n_slab - 1,)), dma((n_slab - 1,)), dma((n_slab - 1,)), dma((n_slab - 1,)), dma((4,)),
        ],
        compiler_params=pltpu.CompilerParams(
            collective_id=0, has_side_effects=True, vmem_limit_bytes=held + 10 * 2**20
        ),
        cost_estimate=pl.CostEstimate(
            flops=2 * pairs * pairs * width,
            bytes_accessed=8 * slabs * pair_dev * square,
            transcendentals=0,
        ),
    )(t, pair_irreps, slab_irreps, pair_irreps.reshape(1, pairs), w, v)


def ladder_kernel(
    n_idx, n_slab, t_ref, labels_ref, slab_labels_ref, row_ref, w_ref, v_ref, out_ref,
    recv, wfull, wide, res, hole, mine, vfull, vwide, row, labels, slab_labels,
    send1, recv1, send2, recv2, wsend, wrecv, vsend, vrecv, own_sems, keep_sem,
):
    n_dev = n_idx * n_slab
    pair_dev, side, slabs, _ = t_ref.shape
    chunks = side // n_dev
    pairs = recv.shape[1]
    w_cols = w_ref.shape[1]
    irreps, v_rows, _ = v_ref.shape
    e = lax.axis_index("idx")
    s = lax.axis_index("slab")
    me = e * n_slab + s
    my_block = (s * n_idx + e) * pair_dev
    others = n_dev - 1

    def where(peer):
        return (peer // n_slab, peer % n_slab)

    barrier = pltpu.get_barrier_semaphore()

    def greet(j, carry):
        pl.semaphore_signal(barrier, inc=1, device_id=where((me + j) % n_dev), device_id_type=MESH)
        return carry

    lax.fori_loop(1, n_dev, greet, 0)

    keep = [
        pltpu.make_async_copy(
            t_ref.at[:, k * n_dev + me],
            recv.at[k, pl.ds(pl.multiple_of(my_block, 16), pair_dev)],
            keep_sem.at[k],
        )
        for k in range(chunks)
    ]
    locals_ = [
        pltpu.make_async_copy(
            w_ref, wfull.at[:, pl.ds(pl.multiple_of(s * w_cols, 128), w_cols)], own_sems.at[0]
        ),
        pltpu.make_async_copy(
            v_ref, vfull.at[:, pl.ds(pl.multiple_of(s * v_rows, 16), v_rows), :], own_sems.at[1]
        ),
        pltpu.make_async_copy(labels_ref, labels, own_sems.at[2]),
        pltpu.make_async_copy(slab_labels_ref, slab_labels, own_sems.at[3]),
        pltpu.make_async_copy(row_ref, row, own_sems.at[4]),
        pltpu.make_async_copy(t_ref, mine, own_sems.at[5]),
    ]
    for copy in keep + locals_:
        copy.start()

    pl.semaphore_wait(barrier, others)

    def send_chunk(k):
        def body(j, carry):
            peer = (me + j) % n_dev
            pltpu.make_async_remote_copy(
                src_ref=t_ref.at[:, k * n_dev + peer],
                dst_ref=recv.at[k, pl.ds(pl.multiple_of(my_block, 16), pair_dev)],
                send_sem=send1,
                recv_sem=recv1.at[k],
                device_id=where(peer),
                device_id_type=MESH,
            ).start()
            return carry

        lax.fori_loop(1, n_dev, body, 0)

    def gather(j):
        peer = (s + j) % n_slab
        return (
            pltpu.make_async_remote_copy(
                src_ref=w_ref,
                dst_ref=wfull.at[:, pl.ds(pl.multiple_of(s * w_cols, 128), w_cols)],
                send_sem=wsend.at[j - 1],
                recv_sem=wrecv.at[j - 1],
                device_id=(e, peer),
                device_id_type=MESH,
            ),
            pltpu.make_async_remote_copy(
                src_ref=v_ref,
                dst_ref=vfull.at[:, pl.ds(pl.multiple_of(s * v_rows, 16), v_rows), :],
                send_sem=vsend.at[j - 1],
                recv_sem=vrecv.at[j - 1],
                device_id=(e, peer),
                device_id_type=MESH,
            ),
        )

    send_chunk(0)
    gathers = [gather(j) for j in range(1, n_slab)]
    for w_copy, v_copy in gathers:
        w_copy.start()
        v_copy.start()
    for k in range(1, chunks):
        send_chunk(k)
    for copy in locals_:
        copy.wait()
    for w_copy, _ in gathers:
        w_copy.wait()

    def equal(shape, left, right):
        return (
            left(lax.broadcasted_iota(jnp.int32, shape, 0))
            == right(lax.broadcasted_iota(jnp.int32, shape, 1))
        )

    def ones(mask):
        return mask.astype(jnp.float32).astype(jnp.bfloat16)

    def same(x):
        return x

    def half(x):
        return x // slabs

    def rest(x):
        return x % slabs

    onehot = ones(row[...] == lax.broadcasted_iota(jnp.int32, (irreps, pairs), 0))

    def column_pair(q):
        p, q = q % pair_dev, q // pair_dev
        return ((q % n_idx) * n_slab + q // n_idx) * pair_dev + p

    moved = jnp.dot(
        onehot, ones(equal((pairs, pairs), same, column_pair)), preferred_element_type=jnp.float32
    ).astype(jnp.bfloat16)
    allowed = lax.dot_general(
        onehot, moved, (((0,), (0,)), ((), ())), preferred_element_type=jnp.float32
    )
    wfull[...] = jnp.where(allowed > 0.5, wfull[...].astype(jnp.float32), 0.0).astype(jnp.bfloat16)

    tile = 256
    spread = ones(equal((pairs, slabs * pairs), same, half))

    def widen(m, carry):
        down = ones(
            equal((tile, tile // slabs), half, same)
        )
        part = jnp.dot(
            down,
            wfull[pl.ds(pl.multiple_of(m * (tile // slabs), 16), tile // slabs), :],
            preferred_element_type=jnp.float32,
        ).astype(jnp.bfloat16)
        both = jnp.dot(part, spread, preferred_element_type=jnp.float32)
        wide[pl.ds(pl.multiple_of(m * tile, 16), tile), :] = jnp.where(
            equal(both.shape, rest, rest), both, 0.0
        ).astype(jnp.bfloat16)
        return carry

    lax.fori_loop(0, slabs * pairs // tile, widen, 0)

    for k in range(chunks):
        keep[k].wait()
        landed = recv.at[k, pl.ds(0, others * pair_dev)]
        pltpu.make_async_copy(landed, landed, recv1.at[k]).wait()
        right = recv[k].reshape(slabs * pairs, side)

        for m in range(slabs * pairs // tile):
            res[k, m * (tile // slabs) : (m + 1) * (tile // slabs)] = (
                jnp.dot(wide[m * tile : (m + 1) * tile, :], right, preferred_element_type=jnp.float32)
                .astype(jnp.bfloat16)
                .reshape(tile // slabs, slabs, side)
            )

        def give(j, carry):
            peer = (me + j) % n_dev
            pltpu.make_async_remote_copy(
                src_ref=res.at[k, pl.ds(pl.multiple_of(peer * pair_dev, 16), pair_dev)],
                dst_ref=hole.at[:, k * n_dev + me],
                send_sem=send2,
                recv_sem=recv2.at[k],
                device_id=where(peer),
                device_id_type=MESH,
            ).start()
            return carry

        lax.fori_loop(1, n_dev, give, 0)
        hole[:, k * n_dev + me] = res[k, pl.ds(pl.multiple_of(me * pair_dev, 16), pair_dev)]

    for _, v_copy in gathers:
        v_copy.wait()

    rows = slabs * side
    for g in range(irreps):
        tall = jnp.dot(
            ones(equal((rows, side), half, same)), vfull[g], preferred_element_type=jnp.float32
        ).astype(jnp.bfloat16)
        both = jnp.dot(
            tall, ones(equal((side, rows), same, half)), preferred_element_type=jnp.float32
        )
        together = equal((rows, rows), rest, rest)
        for plane in range(slabs):
            mask = together & (lax.broadcasted_iota(jnp.int32, (rows, rows), 0) % slabs == plane)
            vwide[plane, g] = jnp.where(mask, both, 0.0).astype(jnp.bfloat16)

    def particle(i, carry):
        x = mine[i].reshape(rows, side)
        total = jnp.zeros((rows, side), jnp.float32)
        for plane in range(slabs):
            g = jnp.bitwise_xor(labels[me * pair_dev + i], slab_labels[plane])
            total += jnp.dot(vwide[plane, g], x, preferred_element_type=jnp.float32)
        out_ref[i] = total
        return carry

    lax.fori_loop(0, pair_dev, particle, 0)

    for k in range(chunks):
        landed = recv.at[k, pl.ds(0, others * pair_dev)]
        pltpu.make_async_copy(landed, landed, recv2.at[k]).wait()

        def finish(i, carry):
            place = slice(k * n_dev * slabs, (k + 1) * n_dev * slabs)
            out_ref[i, place, :] += (
                hole[i, k * n_dev : (k + 1) * n_dev]
                .reshape(n_dev * slabs, side)
                .astype(jnp.float32)
            )
            return carry

        lax.fori_loop(0, pair_dev, finish, 0, unroll=4)

    everything = recv.at[:, pl.ds(0, others * pair_dev)]
    for sem in (send1, send2):
        pltpu.make_async_copy(everything, everything, sem).wait()


def ladder(amplitudes, pair_irreps, slab_irreps, w, v, n_idx, n_slab):
    pair_dev, slabs, square = amplitudes.shape
    n_dev = n_idx * n_slab
    pairs = w.shape[0]
    irreps, v_rows, side = v.shape
    chunks = side // n_dev
    t = amplitudes.reshape(pair_dev, slabs, side, side).transpose(0, 2, 1, 3)
    operands = (t, pair_irreps, slab_irreps, pair_irreps.reshape(1, pairs), w, v)
    hbm = pl.BlockSpec(memory_space=pltpu.HBM)
    dma = pltpu.SemaphoreType.DMA
    bf16 = jnp.bfloat16
    out = pl.pallas_call(
        functools.partial(ladder_kernel, n_idx, n_slab),
        out_shape=jax.ShapeDtypeStruct((pair_dev, side * slabs, side), jnp.float32),
        in_specs=[hbm] * 6,
        out_specs=pl.BlockSpec(memory_space=pltpu.VMEM),
        scratch_shapes=[
            pltpu.VMEM((chunks, pairs, slabs, side), bf16),
            pltpu.VMEM((pairs, pairs), bf16),
            pltpu.VMEM((slabs * pairs, slabs * pairs), bf16),
            pltpu.VMEM((chunks, pairs, slabs, side), bf16),
            pltpu.VMEM(t.shape, bf16),
            pltpu.VMEM(t.shape, bf16),
            pltpu.VMEM((irreps, side, side), bf16),
            pltpu.VMEM((slabs, irreps, slabs * side, slabs * side), bf16),
            pltpu.VMEM((1, pairs), jnp.int32),
            pltpu.SMEM(pair_irreps.shape, jnp.int32),
            pltpu.SMEM(slab_irreps.shape, jnp.int32),
            dma, dma((chunks,)), dma, dma((chunks,)),
            dma((n_slab - 1,)), dma((n_slab - 1,)), dma((n_slab - 1,)), dma((n_slab - 1,)),
            dma((6,)), dma((chunks,)),
        ],
        compiler_params=pltpu.CompilerParams(
            collective_id=0, has_side_effects=True, vmem_limit_bytes=40 * 2**20
        ),
        cost_estimate=pl.CostEstimate(
            flops=4 * pairs * pairs * slabs * square // n_dev,
            bytes_accessed=8 * slabs * pair_dev * square,
            transcendentals=0,
        ),
    )(*(pltpu.with_memory_space_constraint(x, pltpu.HBM) for x in operands))
    return out.reshape(pair_dev, side, slabs, side).transpose(0, 2, 1, 3).reshape(amplitudes.shape)


def body(amplitudes, pair_irreps, slab_irreps, ladder_ints, vv_blocks):
    n_idx = lax.axis_size("idx")
    n_slab = lax.axis_size("slab")
    whole = (amplitudes, pair_irreps, slab_irreps, ladder_ints, vv_blocks, n_idx, n_slab)
    if vv_blocks.shape[2] % (n_idx * n_slab) == 0:
        return ladder(*whole)
    return exchange(amplitudes.transpose(1, 0, 2), *whole[1:])


def solution(mesh):
    return jax.shard_map(
        body,
        mesh=mesh,
        in_specs=(P(("idx", "slab"), None, None), P(), P(), P(None, "slab"), P(None, "slab", None)),
        out_specs=P(("idx", "slab"), None, None),
        check_vma=False,
    )
```

```python
import functools

import jax
import jax.numpy as jnp
from jax import lax
from jax.experimental import pallas as pl
from jax.experimental.pallas import tpu as pltpu
from jax.sharding import PartitionSpec as P

MESH = pl.DeviceIdType.MESH


def exchange_kernel(
    n_idx, n_slab, cw, t_ref, labels_ref, slab_labels_ref, row_ref, w_ref, v_ref, out_ref,
    recv, wfull, res, hole, vfull, rows_in, rows_out, labels, slab_labels,
    send1, recv1, send2, recv2, wsend, wrecv, vsend, vrecv, own_sems,
):
    n_dev = n_idx * n_slab
    pair_dev = t_ref.shape[1]
    square = t_ref.shape[2]
    width = t_ref.shape[0] * square // n_dev
    chunks = width // cw
    w_cols = w_ref.shape[1]
    v_rows = v_ref.shape[1]
    e = lax.axis_index("idx")
    s = lax.axis_index("slab")
    me = e * n_slab + s
    my_block = (s * n_idx + e) * pair_dev
    others = n_dev - 1

    def where(peer):
        return (peer // n_slab, peer % n_slab)

    barrier = pltpu.get_barrier_semaphore()

    def greet(j, carry):
        pl.semaphore_signal(barrier, inc=1, device_id=where((me + j) % n_dev), device_id_type=MESH)
        return carry

    lax.fori_loop(1, n_dev, greet, 0)
    pl.semaphore_wait(barrier, others)

    locals_ = [
        pltpu.make_async_copy(
            w_ref, wfull.at[:, pl.ds(pl.multiple_of(s * w_cols, 128), w_cols)], own_sems.at[0]
        ),
        pltpu.make_async_copy(
            v_ref, vfull.at[:, pl.ds(pl.multiple_of(s * v_rows, 16), v_rows), :], own_sems.at[1]
        ),
        pltpu.make_async_copy(labels_ref, labels, own_sems.at[2]),
        pltpu.make_async_copy(slab_labels_ref, slab_labels, own_sems.at[3]),
    ]
    for copy in locals_:
        copy.start()

    def order(j):
        return j

    def columns(device, k):
        first = device * width + k * cw
        return first // square, pl.ds(pl.multiple_of(first % square, 128), cw)

    def send_chunk(k):
        def body(j, carry):
            peer = (me + order(j)) % n_dev
            plane, place = columns(peer, k)
            pltpu.make_async_remote_copy(
                src_ref=t_ref.at[plane, :, place],
                dst_ref=recv.at[k, pl.ds(pl.multiple_of(my_block, 16), pair_dev), :],
                send_sem=send1,
                recv_sem=recv1.at[k],
                device_id=where(peer),
                device_id_type=MESH,
            ).start()
            return carry

        lax.fori_loop(1, n_dev, body, 0)
        plane, place = columns(me, k)
        recv[k, pl.ds(pl.multiple_of(my_block, 16), pair_dev), :] = t_ref[plane, :, place]

    def gather(j):
        peer = (s + j) % n_slab
        return (
            pltpu.make_async_remote_copy(
                src_ref=w_ref,
                dst_ref=wfull.at[:, pl.ds(pl.multiple_of(s * w_cols, 128), w_cols)],
                send_sem=wsend.at[j - 1],
                recv_sem=wrecv.at[j - 1],
                device_id=(e, peer),
                device_id_type=MESH,
            ),
            pltpu.make_async_remote_copy(
                src_ref=v_ref,
                dst_ref=vfull.at[:, pl.ds(pl.multiple_of(s * v_rows, 16), v_rows), :],
                send_sem=vsend.at[j - 1],
                recv_sem=vrecv.at[j - 1],
                device_id=(e, peer),
                device_id_type=MESH,
            ),
        )

    send_chunk(0)
    gathers = [gather(j) for j in range(1, n_slab)]
    for w_copy, v_copy in gathers:
        w_copy.start()
        v_copy.start()
    for k in range(1, chunks):
        send_chunk(k)
    for copy in locals_:
        copy.wait()
    for _, v_copy in gathers:
        v_copy.wait()

    side = vfull.shape[1]
    slabs = t_ref.shape[0]
    def particle(plane):

        def take(c, carry):
            rows_in[pl.ds(pl.multiple_of(c * pair_dev, 16), pair_dev), :] = t_ref[
                plane, :, pl.ds(pl.multiple_of(c * side, 128), side)
            ].astype(jnp.float32)
            return carry

        def one(i, carry):
            g = jnp.bitwise_xor(labels[me * pair_dev + i], slab_labels[plane])
            x = rows_in[pl.ds(i, side, stride=pair_dev), :].astype(jnp.bfloat16)
            rows_out[plane, pl.ds(i, side, stride=pair_dev), :] = jnp.dot(
                vfull[g], x, preferred_element_type=jnp.float32
            )
            return carry

        lax.fori_loop(0, side, take, 0, unroll=8)
        lax.fori_loop(0, pair_dev, one, 0, unroll=4)

    for plane in range(slabs):
        particle(plane)

    for w_copy, _ in gathers:
        w_copy.wait()

    pairs = recv.shape[1]
    tile = min(pairs, 512)
    irreps = vfull.shape[0]
    onehot = (
        row_ref[...] == lax.broadcasted_iota(jnp.int32, (irreps, pairs), 0)
    ).astype(jnp.float32).astype(jnp.bfloat16)

    def mask_columns(n, carry):
        cols = pl.ds(pl.multiple_of(n * tile, tile), tile)
        col = lax.broadcasted_iota(jnp.int32, (pairs, tile), 1) + n * tile
        row = lax.broadcasted_iota(jnp.int32, (pairs, tile), 0)
        p, q = col % pair_dev, col // pair_dev
        kl = ((q % n_idx) * n_slab + q // n_idx) * pair_dev + p
        moved = jnp.dot(
            onehot,
            (row == kl).astype(jnp.float32).astype(jnp.bfloat16),
            preferred_element_type=jnp.float32,
        ).astype(jnp.bfloat16)
        equal = lax.dot_general(
            onehot, moved, (((0,), (0,)), ((), ())), preferred_element_type=jnp.float32
        )
        wfull[:, cols] = jnp.where(
            equal > 0.5, wfull[:, cols].astype(jnp.float32), 0.0
        ).astype(jnp.bfloat16)
        return carry

    lax.fori_loop(0, pairs // tile, mask_columns, 0)

    for k in range(chunks):
        plane, place = columns(me, k)
        landed = recv.at[k, pl.ds(0, others * pair_dev), :]
        pltpu.make_async_copy(landed, landed, recv1.at[k]).wait()

        def multiply(m, carry):
            rows = pl.ds(pl.multiple_of(m * tile, tile), tile)
            res[k, rows, :] = jnp.dot(
                wfull[rows, :], recv[k], preferred_element_type=jnp.float32
            ).astype(jnp.bfloat16)
            return carry

        lax.fori_loop(0, pairs // tile, multiply, 0)

        def give(j, carry):
            peer = (me + order(j)) % n_dev
            pltpu.make_async_remote_copy(
                src_ref=res.at[k, pl.ds(pl.multiple_of(peer * pair_dev, 16), pair_dev), :],
                dst_ref=hole.at[plane, :, place],
                send_sem=send2,
                recv_sem=recv2.at[k],
                device_id=where(peer),
                device_id_type=MESH,
            ).start()
            return carry

        lax.fori_loop(1, n_dev, give, 0)
        hole[plane, :, place] = res[k, pl.ds(pl.multiple_of(me * pair_dev, 16), pair_dev), :]


    per_plane = n_dev // slabs
    for k in range(chunks):
        landed = recv.at[k, pl.ds(0, others * pair_dev), :]
        pltpu.make_async_copy(landed, landed, recv2.at[k]).wait()
        for plane in range(slabs):

            def finish(d, carry):
                for u in range(cw // side):
                    first = d * width + k * cw + u * side
                    cols = pl.ds(pl.multiple_of(first, 128), side)
                    rows = pl.ds(pl.multiple_of(first // side * pair_dev, 16), pair_dev)
                    out_ref[:, plane, cols] = rows_out[plane, rows, :] + hole[
                        plane, :, cols
                    ].astype(jnp.float32)
                return carry

            lax.fori_loop(0, per_plane, finish, 0, unroll=2)

    everything = recv.at[:, pl.ds(0, others * pair_dev), :]
    for sem in (send1, send2):
        pltpu.make_async_copy(everything, everything, sem).wait()


def exchange(t, pair_irreps, slab_irreps, w, v, n_idx, n_slab):
    slabs, pair_dev, square = t.shape
    n_dev = n_idx * n_slab
    pairs = w.shape[0]
    width = slabs * square // n_dev
    cw = min(width, 256)
    chunks = width // cw
    irreps, v_rows, side = v.shape
    block = (chunks, pairs, cw)
    vmem = pl.BlockSpec(memory_space=pltpu.VMEM)
    anywhere = pl.BlockSpec(memory_space=pl.ANY)
    held = 2 * (pairs * pairs + 12 * slabs * pair_dev * square)
    dma = pltpu.SemaphoreType.DMA
    return pl.pallas_call(
        functools.partial(exchange_kernel, n_idx, n_slab, cw),
        out_shape=jax.ShapeDtypeStruct((pair_dev, slabs, square), jnp.float32),
        in_specs=[vmem, anywhere, anywhere, vmem, anywhere, anywhere],
        out_specs=vmem,
        scratch_shapes=[
            pltpu.VMEM(block, jnp.bfloat16),
            pltpu.VMEM((pairs, pairs), jnp.bfloat16),
            pltpu.VMEM(block, jnp.bfloat16),
            pltpu.VMEM(t.shape, jnp.bfloat16),
            pltpu.VMEM((irreps, v_rows * n_slab, side), jnp.bfloat16),
            pltpu.VMEM((side * pair_dev, side), jnp.float32),
            pltpu.VMEM((slabs, side * pair_dev, side), jnp.float32),
            pltpu.SMEM(pair_irreps.shape, jnp.int32),
            pltpu.SMEM(slab_irreps.shape, jnp.int32),
            dma, dma((chunks,)), dma, dma((chunks,)),
            dma((n_slab - 1,)), dma((n_slab - 1,)), dma((n_slab - 1,)), dma((n_slab - 1,)), dma((4,)),
        ],
        compiler_params=pltpu.CompilerParams(
            collective_id=0, has_side_effects=True, vmem_limit_bytes=held + 10 * 2**20
        ),
        cost_estimate=pl.CostEstimate(
            flops=2 * pairs * pairs * width,
            bytes_accessed=8 * slabs * pair_dev * square,
            transcendentals=0,
        ),
    )(t, pair_irreps, slab_irreps, pair_irreps.reshape(1, pairs), w, v)


def ladder_kernel(
    n_idx, n_slab, t_ref, labels_ref, slab_labels_ref, row_ref, w_ref, v_ref, out_ref,
    recv, wfull, wide, res, hole, mine, vfull, vwide, row, labels, slab_labels,
    send1, recv1, send2, recv2, wsend, wrecv, vsend, vrecv, own_sems, keep_sem, late,
):
    n_dev = n_idx * n_slab
    pair_dev, side, slabs, _ = t_ref.shape
    chunks, pairs, width = recv.shape[:3]
    w_cols = w_ref.shape[1]
    irreps, v_rows, _ = v_ref.shape
    e = lax.axis_index("idx")
    s = lax.axis_index("slab")
    z, x, y, core = e // 2, e % 2, s // 2, s % 2
    me = e * n_slab + s
    my_block = (s * n_idx + e) * pair_dev
    others = n_dev - 1
    plane_dev = n_dev // 4
    group = 2 * plane_dev
    inner = (z == 1) | (z == 2)
    outer = (z == 0) | (z == 3)

    def flip(bit, by):
        return bit + by - 2 * bit * by

    def partner(dz, q):
        pz = flip(z // 2, dz // 2) * 2 + flip(z % 2, dz % 2)
        return pz * 2 + flip(x, q // 4), flip(y, q // 2 % 2) * 2 + flip(core, q % 2)

    def of_kind(i):
        return partner(3 * (1 - i // plane_dev), plane_dev - 1 - i % plane_dev)

    def of_other_kind(i):
        return partner(2 - i // plane_dev, plane_dev - 1 - i % plane_dev)

    def of_all(i):
        return partner(3 - i // plane_dev, plane_dev - 1 - i % plane_dev)

    def signal(sem, count, peer_of):
        def body(i, carry):
            pl.semaphore_signal(sem, inc=1, device_id=peer_of(i), device_id_type=MESH)
            return carry

        lax.fori_loop(0, count, body, 0)

    def columns(k, device):
        return pl.ds(k * n_dev * width + device * width, width)

    keep = [
        pltpu.make_async_copy(
            t_ref.at[:, columns(k, me)],
            recv.at[k, pl.ds(pl.multiple_of(my_block, 16), pair_dev)],
            keep_sem.at[k],
        )
        for k in range(chunks)
    ]
    locals_ = [
        pltpu.make_async_copy(
            w_ref, wfull.at[:, pl.ds(pl.multiple_of(s * w_cols, 128), w_cols)], own_sems.at[0]
        ),
        pltpu.make_async_copy(
            v_ref, vfull.at[:, pl.ds(pl.multiple_of(s * v_rows, 16), v_rows), :], own_sems.at[1]
        ),
        pltpu.make_async_copy(labels_ref, labels, own_sems.at[2]),
        pltpu.make_async_copy(slab_labels_ref, slab_labels, own_sems.at[3]),
        pltpu.make_async_copy(row_ref, row, own_sems.at[4]),
        pltpu.make_async_copy(t_ref, mine, own_sems.at[5]),
    ]

    def send(k, count, peer_of):
        def body(i, carry):
            pe, ps = peer_of(i)
            pltpu.make_async_remote_copy(
                src_ref=t_ref.at[:, columns(k, pe * n_slab + ps)],
                dst_ref=recv.at[k, pl.ds(pl.multiple_of(my_block, 16), pair_dev)],
                send_sem=send1,
                recv_sem=recv1.at[k],
                device_id=(pe, ps),
                device_id_type=MESH,
            ).start()
            return carry

        lax.fori_loop(0, count, body, 0)

    barrier = pltpu.get_barrier_semaphore()
    signal(barrier, group - 1, of_kind)

    @pl.when(inner)
    def _():
        signal(barrier, group, of_other_kind)

    for copy in keep + locals_:
        copy.start()

    @pl.when(inner)
    def _():
        pl.semaphore_wait(barrier, group - 1)
        for k in range(chunks):
            send(k, group - 1, of_kind)
        pl.semaphore_wait(late, group)
        for k in range(chunks):
            send(k, group, of_other_kind)

    @pl.when(outer)
    def _():
        pl.semaphore_wait(barrier, others)
        signal(late, group, of_other_kind)
        for k in range(chunks):
            send(k, others, of_all)

    def gather(j):
        peer = (s + j) % n_slab
        return (
            pltpu.make_async_remote_copy(
                src_ref=w_ref,
                dst_ref=wfull.at[:, pl.ds(pl.multiple_of(s * w_cols, 128), w_cols)],
                send_sem=wsend.at[j - 1],
                recv_sem=wrecv.at[j - 1],
                device_id=(e, peer),
                device_id_type=MESH,
            ),
            pltpu.make_async_remote_copy(
                src_ref=v_ref,
                dst_ref=vfull.at[:, pl.ds(pl.multiple_of(s * v_rows, 16), v_rows), :],
                send_sem=vsend.at[j - 1],
                recv_sem=vrecv.at[j - 1],
                device_id=(e, peer),
                device_id_type=MESH,
            ),
        )

    gathers = [gather(j) for j in range(1, n_slab)]
    for w_copy, v_copy in gathers:
        w_copy.start()
        v_copy.start()
    for copy in locals_:
        copy.wait()
    for w_copy, _ in gathers:
        w_copy.wait()

    def equal(shape, left, right):
        return (
            left(lax.broadcasted_iota(jnp.int32, shape, 0))
            == right(lax.broadcasted_iota(jnp.int32, shape, 1))
        )

    def ones(mask):
        return mask.astype(jnp.float32).astype(jnp.bfloat16)

    def same(x):
        return x

    def half(x):
        return x // slabs

    def rest(x):
        return x % slabs

    onehot = ones(row[...] == lax.broadcasted_iota(jnp.int32, (irreps, pairs), 0))

    def column_pair(q):
        p, q = q % pair_dev, q // pair_dev
        return ((q % n_idx) * n_slab + q // n_idx) * pair_dev + p

    moved = jnp.dot(
        onehot, ones(equal((pairs, pairs), same, column_pair)), preferred_element_type=jnp.float32
    ).astype(jnp.bfloat16)
    allowed = lax.dot_general(
        onehot, moved, (((0,), (0,)), ((), ())), preferred_element_type=jnp.float32
    )
    wfull[...] = jnp.where(allowed > 0.5, wfull[...].astype(jnp.float32), 0.0).astype(jnp.bfloat16)

    tile = 256
    spread = ones(equal((pairs, slabs * pairs), same, half))

    def widen(m, carry):
        down = ones(
            equal((tile, tile // slabs), half, same)
        )
        part = jnp.dot(
            down,
            wfull[pl.ds(pl.multiple_of(m * (tile // slabs), 16), tile // slabs), :],
            preferred_element_type=jnp.float32,
        ).astype(jnp.bfloat16)
        both = jnp.dot(part, spread, preferred_element_type=jnp.float32)
        wide[pl.ds(pl.multiple_of(m * tile, 16), tile), :] = jnp.where(
            equal(both.shape, rest, rest), both, 0.0
        ).astype(jnp.bfloat16)
        return carry

    lax.fori_loop(0, slabs * pairs // tile, widen, 0)

    def give(k, far):
        def body(j, carry):
            t = j % 2
            q = j // 2 - 2 * t
            pe = (flip(z // 2, far) * 2 + t) * 2 + q // 4
            ps = q // 2 % 2 * 2 + flip(core, q % 2)
            peer = pe * n_slab + ps

            @pl.when((q >= 0) & (q < plane_dev) & (peer != me))
            def _():
                pltpu.make_async_remote_copy(
                    src_ref=res.at[k, pl.ds(pl.multiple_of(peer * pair_dev, 16), pair_dev)],
                    dst_ref=hole.at[:, columns(k, me)],
                    send_sem=send2,
                    recv_sem=recv2.at[k],
                    device_id=(pe, ps),
                    device_id_type=MESH,
                ).start()

            return carry

        lax.fori_loop(0, group + 4, body, 0)

    for k in range(chunks):
        keep[k].wait()
        landed = recv.at[k, pl.ds(0, others * pair_dev)]
        pltpu.make_async_copy(landed, landed, recv1.at[k]).wait()
        right = jnp.concatenate(
            [recv[k, :, u].reshape(slabs * pairs, side) for u in range(width)], axis=1
        )

        for m in range(slabs * pairs // tile):
            got = jnp.dot(
                wide[m * tile : (m + 1) * tile, :], right, preferred_element_type=jnp.float32
            ).astype(jnp.bfloat16)
            for u in range(width):
                res[k, m * (tile // slabs) : (m + 1) * (tile // slabs), u] = got[
                    :, u * side : (u + 1) * side
                ].reshape(tile // slabs, slabs, side)

        give(k, 0)
        give(k, 1)
        hole[:, columns(k, me)] = res[k, pl.ds(pl.multiple_of(me * pair_dev, 16), pair_dev)]

    for _, v_copy in gathers:
        v_copy.wait()

    rows = slabs * side
    for g in range(irreps):
        tall = jnp.dot(
            ones(equal((rows, side), half, same)), vfull[g], preferred_element_type=jnp.float32
        ).astype(jnp.bfloat16)
        both = jnp.dot(
            tall, ones(equal((side, rows), same, half)), preferred_element_type=jnp.float32
        )
        together = equal((rows, rows), rest, rest)
        for plane in range(slabs):
            mask = together & (lax.broadcasted_iota(jnp.int32, (rows, rows), 0) % slabs == plane)
            vwide[plane, g] = jnp.where(mask, both, 0.0).astype(jnp.bfloat16)

    def particle(i, carry):
        x = mine[i].reshape(rows, side)
        total = jnp.zeros((rows, side), jnp.float32)
        for plane in range(slabs):
            g = jnp.bitwise_xor(labels[me * pair_dev + i], slab_labels[plane])
            total += jnp.dot(vwide[plane, g], x, preferred_element_type=jnp.float32)
        out_ref[i] = total
        return carry

    lax.fori_loop(0, pair_dev, particle, 0)

    for k in range(chunks):
        landed = recv.at[k, pl.ds(0, others * pair_dev)]
        pltpu.make_async_copy(landed, landed, recv2.at[k]).wait()

        def finish(i, carry):
            part = side // chunks
            out_ref[i, k * part * slabs : (k + 1) * part * slabs, :] += (
                hole[i, k * part : (k + 1) * part].reshape(part * slabs, side).astype(jnp.float32)
            )
            return carry

        lax.fori_loop(0, pair_dev, finish, 0, unroll=4)

    everything = recv.at[:, pl.ds(0, others * pair_dev)]
    for sem in (send1, send2):
        pltpu.make_async_copy(everything, everything, sem).wait()


def ladder(amplitudes, pair_irreps, slab_irreps, w, v, n_idx, n_slab):
    pair_dev, slabs, square = amplitudes.shape
    n_dev = n_idx * n_slab
    pairs = w.shape[0]
    irreps, v_rows, side = v.shape
    width = 2
    chunks = side // n_dev // width
    t = amplitudes.reshape(pair_dev, slabs, side, side).transpose(0, 2, 1, 3)
    operands = (t, pair_irreps, slab_irreps, pair_irreps.reshape(1, pairs), w, v)
    hbm = pl.BlockSpec(memory_space=pltpu.HBM)
    dma = pltpu.SemaphoreType.DMA
    bf16 = jnp.bfloat16
    out = pl.pallas_call(
        functools.partial(ladder_kernel, n_idx, n_slab),
        out_shape=jax.ShapeDtypeStruct((pair_dev, side * slabs, side), jnp.float32),
        in_specs=[hbm] * 6,
        out_specs=pl.BlockSpec(memory_space=pltpu.VMEM),
        scratch_shapes=[
            pltpu.VMEM((chunks, pairs, width, slabs, side), bf16),
            pltpu.VMEM((pairs, pairs), bf16),
            pltpu.VMEM((slabs * pairs, slabs * pairs), bf16),
            pltpu.VMEM((chunks, pairs, width, slabs, side), bf16),
            pltpu.VMEM(t.shape, bf16),
            pltpu.VMEM(t.shape, bf16),
            pltpu.VMEM((irreps, side, side), bf16),
            pltpu.VMEM((slabs, irreps, slabs * side, slabs * side), bf16),
            pltpu.VMEM((1, pairs), jnp.int32),
            pltpu.SMEM(pair_irreps.shape, jnp.int32),
            pltpu.SMEM(slab_irreps.shape, jnp.int32),
            dma, dma((chunks,)), dma, dma((chunks,)),
            dma((n_slab - 1,)), dma((n_slab - 1,)), dma((n_slab - 1,)), dma((n_slab - 1,)),
            dma((6,)), dma((chunks,)), pltpu.SemaphoreType.REGULAR,
        ],
        compiler_params=pltpu.CompilerParams(
            collective_id=0, has_side_effects=True, vmem_limit_bytes=40 * 2**20
        ),
        cost_estimate=pl.CostEstimate(
            flops=4 * pairs * pairs * slabs * square // n_dev,
            bytes_accessed=8 * slabs * pair_dev * square,
            transcendentals=0,
        ),
    )(*(pltpu.with_memory_space_constraint(x, pltpu.HBM) for x in operands))
    return out.reshape(pair_dev, side, slabs, side).transpose(0, 2, 1, 3).reshape(amplitudes.shape)


def body(amplitudes, pair_irreps, slab_irreps, ladder_ints, vv_blocks):
    n_idx = lax.axis_size("idx")
    n_slab = lax.axis_size("slab")
    whole = (amplitudes, pair_irreps, slab_irreps, ladder_ints, vv_blocks, n_idx, n_slab)
    if (n_idx, n_slab) == (8, 4):
        return ladder(*whole)
    return exchange(amplitudes.transpose(1, 0, 2), *whole[1:])


def solution(mesh):
    return jax.shard_map(
        body,
        mesh=mesh,
        in_specs=(P(("idx", "slab"), None, None), P(), P(), P(None, "slab"), P(None, "slab", None)),
        out_specs=P(("idx", "slab"), None, None),
        check_vma=False,
    )
```

```python
import functools

import jax
import jax.numpy as jnp
from jax import lax
from jax.experimental import pallas as pl
from jax.experimental.pallas import tpu as pltpu
from jax.sharding import PartitionSpec as P

MESH = pl.DeviceIdType.MESH


def exchange_kernel(
    n_idx, n_slab, cw, t_ref, labels_ref, slab_labels_ref, row_ref, w_ref, v_ref, out_ref,
    recv, wfull, res, hole, vfull, rows_in, rows_out, labels, slab_labels,
    send1, recv1, send2, recv2, wsend, wrecv, vsend, vrecv, own_sems,
):
    n_dev = n_idx * n_slab
    pair_dev = t_ref.shape[1]
    square = t_ref.shape[2]
    width = t_ref.shape[0] * square // n_dev
    chunks = width // cw
    w_cols = w_ref.shape[1]
    v_rows = v_ref.shape[1]
    e = lax.axis_index("idx")
    s = lax.axis_index("slab")
    me = e * n_slab + s
    my_block = (s * n_idx + e) * pair_dev
    others = n_dev - 1

    def where(peer):
        return (peer // n_slab, peer % n_slab)

    barrier = pltpu.get_barrier_semaphore()

    def greet(j, carry):
        pl.semaphore_signal(barrier, inc=1, device_id=where((me + j) % n_dev), device_id_type=MESH)
        return carry

    lax.fori_loop(1, n_dev, greet, 0)
    pl.semaphore_wait(barrier, others)

    locals_ = [
        pltpu.make_async_copy(
            w_ref, wfull.at[:, pl.ds(pl.multiple_of(s * w_cols, 128), w_cols)], own_sems.at[0]
        ),
        pltpu.make_async_copy(
            v_ref, vfull.at[:, pl.ds(pl.multiple_of(s * v_rows, 16), v_rows), :], own_sems.at[1]
        ),
        pltpu.make_async_copy(labels_ref, labels, own_sems.at[2]),
        pltpu.make_async_copy(slab_labels_ref, slab_labels, own_sems.at[3]),
    ]
    for copy in locals_:
        copy.start()

    def order(j):
        return j

    def columns(device, k):
        first = device * width + k * cw
        return first // square, pl.ds(pl.multiple_of(first % square, 128), cw)

    def send_chunk(k):
        def body(j, carry):
            peer = (me + order(j)) % n_dev
            plane, place = columns(peer, k)
            pltpu.make_async_remote_copy(
                src_ref=t_ref.at[plane, :, place],
                dst_ref=recv.at[k, pl.ds(pl.multiple_of(my_block, 16), pair_dev), :],
                send_sem=send1,
                recv_sem=recv1.at[k],
                device_id=where(peer),
                device_id_type=MESH,
            ).start()
            return carry

        lax.fori_loop(1, n_dev, body, 0)
        plane, place = columns(me, k)
        recv[k, pl.ds(pl.multiple_of(my_block, 16), pair_dev), :] = t_ref[plane, :, place]

    def gather(j):
        peer = (s + j) % n_slab
        return (
            pltpu.make_async_remote_copy(
                src_ref=w_ref,
                dst_ref=wfull.at[:, pl.ds(pl.multiple_of(s * w_cols, 128), w_cols)],
                send_sem=wsend.at[j - 1],
                recv_sem=wrecv.at[j - 1],
                device_id=(e, peer),
                device_id_type=MESH,
            ),
            pltpu.make_async_remote_copy(
                src_ref=v_ref,
                dst_ref=vfull.at[:, pl.ds(pl.multiple_of(s * v_rows, 16), v_rows), :],
                send_sem=vsend.at[j - 1],
                recv_sem=vrecv.at[j - 1],
                device_id=(e, peer),
                device_id_type=MESH,
            ),
        )

    send_chunk(0)
    gathers = [gather(j) for j in range(1, n_slab)]
    for w_copy, v_copy in gathers:
        w_copy.start()
        v_copy.start()
    for k in range(1, chunks):
        send_chunk(k)
    for copy in locals_:
        copy.wait()
    for _, v_copy in gathers:
        v_copy.wait()

    side = vfull.shape[1]
    slabs = t_ref.shape[0]
    def particle(plane):

        def take(c, carry):
            rows_in[pl.ds(pl.multiple_of(c * pair_dev, 16), pair_dev), :] = t_ref[
                plane, :, pl.ds(pl.multiple_of(c * side, 128), side)
            ].astype(jnp.float32)
            return carry

        def one(i, carry):
            g = jnp.bitwise_xor(labels[me * pair_dev + i], slab_labels[plane])
            x = rows_in[pl.ds(i, side, stride=pair_dev), :].astype(jnp.bfloat16)
            rows_out[plane, pl.ds(i, side, stride=pair_dev), :] = jnp.dot(
                vfull[g], x, preferred_element_type=jnp.float32
            )
            return carry

        lax.fori_loop(0, side, take, 0, unroll=8)
        lax.fori_loop(0, pair_dev, one, 0, unroll=4)

    for plane in range(slabs):
        particle(plane)

    for w_copy, _ in gathers:
        w_copy.wait()

    pairs = recv.shape[1]
    tile = min(pairs, 512)
    irreps = vfull.shape[0]
    onehot = (
        row_ref[...] == lax.broadcasted_iota(jnp.int32, (irreps, pairs), 0)
    ).astype(jnp.float32).astype(jnp.bfloat16)

    def mask_columns(n, carry):
        cols = pl.ds(pl.multiple_of(n * tile, tile), tile)
        col = lax.broadcasted_iota(jnp.int32, (pairs, tile), 1) + n * tile
        row = lax.broadcasted_iota(jnp.int32, (pairs, tile), 0)
        p, q = col % pair_dev, col // pair_dev
        kl = ((q % n_idx) * n_slab + q // n_idx) * pair_dev + p
        moved = jnp.dot(
            onehot,
            (row == kl).astype(jnp.float32).astype(jnp.bfloat16),
            preferred_element_type=jnp.float32,
        ).astype(jnp.bfloat16)
        equal = lax.dot_general(
            onehot, moved, (((0,), (0,)), ((), ())), preferred_element_type=jnp.float32
        )
        wfull[:, cols] = jnp.where(
            equal > 0.5, wfull[:, cols].astype(jnp.float32), 0.0
        ).astype(jnp.bfloat16)
        return carry

    lax.fori_loop(0, pairs // tile, mask_columns, 0)

    for k in range(chunks):
        plane, place = columns(me, k)
        landed = recv.at[k, pl.ds(0, others * pair_dev), :]
        pltpu.make_async_copy(landed, landed, recv1.at[k]).wait()

        def multiply(m, carry):
            rows = pl.ds(pl.multiple_of(m * tile, tile), tile)
            res[k, rows, :] = jnp.dot(
                wfull[rows, :], recv[k], preferred_element_type=jnp.float32
            ).astype(jnp.bfloat16)
            return carry

        lax.fori_loop(0, pairs // tile, multiply, 0)

        def give(j, carry):
            peer = (me + order(j)) % n_dev
            pltpu.make_async_remote_copy(
                src_ref=res.at[k, pl.ds(pl.multiple_of(peer * pair_dev, 16), pair_dev), :],
                dst_ref=hole.at[plane, :, place],
                send_sem=send2,
                recv_sem=recv2.at[k],
                device_id=where(peer),
                device_id_type=MESH,
            ).start()
            return carry

        lax.fori_loop(1, n_dev, give, 0)
        hole[plane, :, place] = res[k, pl.ds(pl.multiple_of(me * pair_dev, 16), pair_dev), :]


    per_plane = n_dev // slabs
    for k in range(chunks):
        landed = recv.at[k, pl.ds(0, others * pair_dev), :]
        pltpu.make_async_copy(landed, landed, recv2.at[k]).wait()
        for plane in range(slabs):

            def finish(d, carry):
                for u in range(cw // side):
                    first = d * width + k * cw + u * side
                    cols = pl.ds(pl.multiple_of(first, 128), side)
                    rows = pl.ds(pl.multiple_of(first // side * pair_dev, 16), pair_dev)
                    out_ref[:, plane, cols] = rows_out[plane, rows, :] + hole[
                        plane, :, cols
                    ].astype(jnp.float32)
                return carry

            lax.fori_loop(0, per_plane, finish, 0, unroll=2)

    everything = recv.at[:, pl.ds(0, others * pair_dev), :]
    for sem in (send1, send2):
        pltpu.make_async_copy(everything, everything, sem).wait()


def exchange(t, pair_irreps, slab_irreps, w, v, n_idx, n_slab):
    slabs, pair_dev, square = t.shape
    n_dev = n_idx * n_slab
    pairs = w.shape[0]
    width = slabs * square // n_dev
    cw = min(width, 256)
    chunks = width // cw
    irreps, v_rows, side = v.shape
    block = (chunks, pairs, cw)
    vmem = pl.BlockSpec(memory_space=pltpu.VMEM)
    anywhere = pl.BlockSpec(memory_space=pl.ANY)
    held = 2 * (pairs * pairs + 12 * slabs * pair_dev * square)
    dma = pltpu.SemaphoreType.DMA
    return pl.pallas_call(
        functools.partial(exchange_kernel, n_idx, n_slab, cw),
        out_shape=jax.ShapeDtypeStruct((pair_dev, slabs, square), jnp.float32),
        in_specs=[vmem, anywhere, anywhere, vmem, anywhere, anywhere],
        out_specs=vmem,
        scratch_shapes=[
            pltpu.VMEM(block, jnp.bfloat16),
            pltpu.VMEM((pairs, pairs), jnp.bfloat16),
            pltpu.VMEM(block, jnp.bfloat16),
            pltpu.VMEM(t.shape, jnp.bfloat16),
            pltpu.VMEM((irreps, v_rows * n_slab, side), jnp.bfloat16),
            pltpu.VMEM((side * pair_dev, side), jnp.float32),
            pltpu.VMEM((slabs, side * pair_dev, side), jnp.float32),
            pltpu.SMEM(pair_irreps.shape, jnp.int32),
            pltpu.SMEM(slab_irreps.shape, jnp.int32),
            dma, dma((chunks,)), dma, dma((chunks,)),
            dma((n_slab - 1,)), dma((n_slab - 1,)), dma((n_slab - 1,)), dma((n_slab - 1,)), dma((4,)),
        ],
        compiler_params=pltpu.CompilerParams(
            collective_id=0, has_side_effects=True, vmem_limit_bytes=held + 10 * 2**20
        ),
        cost_estimate=pl.CostEstimate(
            flops=2 * pairs * pairs * width,
            bytes_accessed=8 * slabs * pair_dev * square,
            transcendentals=0,
        ),
    )(t, pair_irreps, slab_irreps, pair_irreps.reshape(1, pairs), w, v)


def ladder_kernel(
    n_idx, n_slab, t_ref, labels_ref, slab_labels_ref, row_ref, w_ref, v_ref, out_ref,
    recv, wfull, wide, res, hole, mine, vfull, vwide, row, labels, slab_labels,
    send1, recv1, send2, recv2, wsend, wrecv, vsend, vrecv, own_sems, keep_sem, late,
):
    n_dev = n_idx * n_slab
    pair_dev, side, slabs, _ = t_ref.shape
    chunks, pairs, width = recv.shape[:3]
    w_cols = w_ref.shape[1]
    irreps, v_rows, _ = v_ref.shape
    e = lax.axis_index("idx")
    s = lax.axis_index("slab")
    z, x, y, core = e // 2, e % 2, s // 2, s % 2
    me = e * n_slab + s
    my_block = (s * n_idx + e) * pair_dev
    others = n_dev - 1
    plane_dev = n_dev // 4
    group = 2 * plane_dev
    inner = (z == 1) | (z == 2)
    outer = (z == 0) | (z == 3)

    def flip(bit, by):
        return bit + by - 2 * bit * by

    def partner(dz, q):
        pz = flip(z // 2, dz // 2) * 2 + flip(z % 2, dz % 2)
        return pz * 2 + flip(x, q // 4), flip(y, q // 2 % 2) * 2 + flip(core, q % 2)

    def of_kind(i):
        return partner(3 * (1 - i // plane_dev), plane_dev - 1 - i % plane_dev)

    def of_other_kind(i):
        return partner(2 - i // plane_dev, plane_dev - 1 - i % plane_dev)

    def of_all(i):
        return partner(3 - i // plane_dev, plane_dev - 1 - i % plane_dev)

    def signal(sem, count, peer_of):
        def body(i, carry):
            pl.semaphore_signal(sem, inc=1, device_id=peer_of(i), device_id_type=MESH)
            return carry

        lax.fori_loop(0, count, body, 0)

    def columns(k, device):
        return pl.ds(k * n_dev * width + device * width, width)

    keep = [
        pltpu.make_async_copy(
            t_ref.at[:, columns(k, me)],
            recv.at[k, pl.ds(pl.multiple_of(my_block, 16), pair_dev)],
            keep_sem.at[k],
        )
        for k in range(chunks)
    ]
    locals_ = [
        pltpu.make_async_copy(
            w_ref, wfull.at[:, pl.ds(pl.multiple_of(s * w_cols, 128), w_cols)], own_sems.at[0]
        ),
        pltpu.make_async_copy(
            v_ref, vfull.at[:, pl.ds(pl.multiple_of(s * v_rows, 16), v_rows), :], own_sems.at[1]
        ),
        pltpu.make_async_copy(labels_ref, labels, own_sems.at[2]),
        pltpu.make_async_copy(slab_labels_ref, slab_labels, own_sems.at[3]),
        pltpu.make_async_copy(row_ref, row, own_sems.at[4]),
        pltpu.make_async_copy(t_ref, mine, own_sems.at[5]),
    ]

    def send(k, count, peer_of):
        def body(i, carry):
            pe, ps = peer_of(i)
            pltpu.make_async_remote_copy(
                src_ref=t_ref.at[:, columns(k, pe * n_slab + ps)],
                dst_ref=recv.at[k, pl.ds(pl.multiple_of(my_block, 16), pair_dev)],
                send_sem=send1,
                recv_sem=recv1.at[k],
                device_id=(pe, ps),
                device_id_type=MESH,
            ).start()
            return carry

        lax.fori_loop(0, count, body, 0)

    def gather(j):
        peer = (s + j) % n_slab
        return (
            pltpu.make_async_remote_copy(
                src_ref=w_ref,
                dst_ref=wfull.at[:, pl.ds(pl.multiple_of(s * w_cols, 128), w_cols)],
                send_sem=wsend.at[j - 1],
                recv_sem=wrecv.at[j - 1],
                device_id=(e, peer),
                device_id_type=MESH,
            ),
            pltpu.make_async_remote_copy(
                src_ref=v_ref,
                dst_ref=vfull.at[:, pl.ds(pl.multiple_of(s * v_rows, 16), v_rows), :],
                send_sem=vsend.at[j - 1],
                recv_sem=vrecv.at[j - 1],
                device_id=(e, peer),
                device_id_type=MESH,
            ),
        )

    gathers = [gather(j) for j in range(1, n_slab)]
    def start_gathers():
        for w_copy, v_copy in gathers:
            w_copy.start()
            v_copy.start()

    barrier = pltpu.get_barrier_semaphore()
    signal(barrier, group - 1, of_kind)

    @pl.when(inner)
    def _():
        signal(barrier, group, of_other_kind)

    for copy in keep + locals_:
        copy.start()

    @pl.when(inner)
    def _():
        pl.semaphore_wait(barrier, group - 1)
        start_gathers()
        send(0, group - 1, of_kind)
        pl.semaphore_wait(late, group)
        send(0, group, of_other_kind)
        for k in range(1, chunks):
            send(k, group - 1, of_kind)
            send(k, group, of_other_kind)

    @pl.when(outer)
    def _():
        pl.semaphore_wait(barrier, others)
        signal(late, group, of_other_kind)
        start_gathers()
        for k in range(chunks):
            send(k, others, of_all)

    for copy in locals_:
        copy.wait()
    for w_copy, _ in gathers:
        w_copy.wait()

    def equal(shape, left, right):
        return (
            left(lax.broadcasted_iota(jnp.int32, shape, 0))
            == right(lax.broadcasted_iota(jnp.int32, shape, 1))
        )

    def ones(mask):
        return mask.astype(jnp.float32).astype(jnp.bfloat16)

    def same(x):
        return x

    def half(x):
        return x // slabs

    def rest(x):
        return x % slabs

    onehot = ones(row[...] == lax.broadcasted_iota(jnp.int32, (irreps, pairs), 0))

    def column_pair(q):
        p, q = q % pair_dev, q // pair_dev
        return ((q % n_idx) * n_slab + q // n_idx) * pair_dev + p

    moved = jnp.dot(
        onehot, ones(equal((pairs, pairs), same, column_pair)), preferred_element_type=jnp.float32
    ).astype(jnp.bfloat16)
    allowed = lax.dot_general(
        onehot, moved, (((0,), (0,)), ((), ())), preferred_element_type=jnp.float32
    )
    wfull[...] = jnp.where(allowed > 0.5, wfull[...].astype(jnp.float32), 0.0).astype(jnp.bfloat16)

    tile = 256
    spread = ones(equal((pairs, slabs * pairs), same, half))

    def widen(m, carry):
        down = ones(
            equal((tile, tile // slabs), half, same)
        )
        part = jnp.dot(
            down,
            wfull[pl.ds(pl.multiple_of(m * (tile // slabs), 16), tile // slabs), :],
            preferred_element_type=jnp.float32,
        ).astype(jnp.bfloat16)
        both = jnp.dot(part, spread, preferred_element_type=jnp.float32)
        wide[pl.ds(pl.multiple_of(m * tile, 16), tile), :] = jnp.where(
            equal(both.shape, rest, rest), both, 0.0
        ).astype(jnp.bfloat16)
        return carry

    lax.fori_loop(0, slabs * pairs // tile, widen, 0)

    def give(k, far):
        def body(j, carry):
            t = j % 2
            q = j // 2 - 2 * t
            pe = (flip(z // 2, far) * 2 + t) * 2 + q // 4
            ps = q // 2 % 2 * 2 + flip(core, q % 2)
            peer = pe * n_slab + ps

            @pl.when((q >= 0) & (q < plane_dev) & (peer != me))
            def _():
                pltpu.make_async_remote_copy(
                    src_ref=res.at[k, pl.ds(pl.multiple_of(peer * pair_dev, 16), pair_dev)],
                    dst_ref=hole.at[:, columns(k, me)],
                    send_sem=send2,
                    recv_sem=recv2.at[k],
                    device_id=(pe, ps),
                    device_id_type=MESH,
                ).start()

            return carry

        lax.fori_loop(0, group + 4, body, 0)

    for k in range(chunks):
        keep[k].wait()
        landed = recv.at[k, pl.ds(0, others * pair_dev)]
        pltpu.make_async_copy(landed, landed, recv1.at[k]).wait()
        right = jnp.concatenate(
            [recv[k, :, u].reshape(slabs * pairs, side) for u in range(width)], axis=1
        )

        for m in range(slabs * pairs // tile):
            got = jnp.dot(
                wide[m * tile : (m + 1) * tile, :], right, preferred_element_type=jnp.float32
            ).astype(jnp.bfloat16)
            for u in range(width):
                res[k, m * (tile // slabs) : (m + 1) * (tile // slabs), u] = got[
                    :, u * side : (u + 1) * side
                ].reshape(tile // slabs, slabs, side)

        give(k, 0)
        give(k, 1)
        hole[:, columns(k, me)] = res[k, pl.ds(pl.multiple_of(me * pair_dev, 16), pair_dev)]

    for _, v_copy in gathers:
        v_copy.wait()

    rows = slabs * side
    for g in range(irreps):
        tall = jnp.dot(
            ones(equal((rows, side), half, same)), vfull[g], preferred_element_type=jnp.float32
        ).astype(jnp.bfloat16)
        both = jnp.dot(
            tall, ones(equal((side, rows), same, half)), preferred_element_type=jnp.float32
        )
        together = equal((rows, rows), rest, rest)
        for plane in range(slabs):
            mask = together & (lax.broadcasted_iota(jnp.int32, (rows, rows), 0) % slabs == plane)
            vwide[plane, g] = jnp.where(mask, both, 0.0).astype(jnp.bfloat16)

    def particle(i, carry):
        x = mine[i].reshape(rows, side)
        total = jnp.zeros((rows, side), jnp.float32)
        for plane in range(slabs):
            g = jnp.bitwise_xor(labels[me * pair_dev + i], slab_labels[plane])
            total += jnp.dot(vwide[plane, g], x, preferred_element_type=jnp.float32)
        out_ref[i] = total
        return carry

    lax.fori_loop(0, pair_dev, particle, 0)

    for k in range(chunks):
        landed = recv.at[k, pl.ds(0, others * pair_dev)]
        pltpu.make_async_copy(landed, landed, recv2.at[k]).wait()

        def finish(i, carry):
            part = side // chunks
            out_ref[i, k * part * slabs : (k + 1) * part * slabs, :] += (
                hole[i, k * part : (k + 1) * part].reshape(part * slabs, side).astype(jnp.float32)
            )
            return carry

        lax.fori_loop(0, pair_dev, finish, 0, unroll=4)

    everything = recv.at[:, pl.ds(0, others * pair_dev)]
    for sem in (send1, send2):
        pltpu.make_async_copy(everything, everything, sem).wait()


def ladder(amplitudes, pair_irreps, slab_irreps, w, v, n_idx, n_slab):
    pair_dev, slabs, square = amplitudes.shape
    n_dev = n_idx * n_slab
    pairs = w.shape[0]
    irreps, v_rows, side = v.shape
    width = 2
    chunks = side // n_dev // width
    t = amplitudes.reshape(pair_dev, slabs, side, side).transpose(0, 2, 1, 3)
    operands = (t, pair_irreps, slab_irreps, pair_irreps.reshape(1, pairs), w, v)
    hbm = pl.BlockSpec(memory_space=pltpu.HBM)
    dma = pltpu.SemaphoreType.DMA
    bf16 = jnp.bfloat16
    out = pl.pallas_call(
        functools.partial(ladder_kernel, n_idx, n_slab),
        out_shape=jax.ShapeDtypeStruct((pair_dev, side * slabs, side), jnp.float32),
        in_specs=[hbm] * 6,
        out_specs=pl.BlockSpec(memory_space=pltpu.VMEM),
        scratch_shapes=[
            pltpu.VMEM((chunks, pairs, width, slabs, side), bf16),
            pltpu.VMEM((pairs, pairs), bf16),
            pltpu.VMEM((slabs * pairs, slabs * pairs), bf16),
            pltpu.VMEM((chunks, pairs, width, slabs, side), bf16),
            pltpu.VMEM(t.shape, bf16),
            pltpu.VMEM(t.shape, bf16),
            pltpu.VMEM((irreps, side, side), bf16),
            pltpu.VMEM((slabs, irreps, slabs * side, slabs * side), bf16),
            pltpu.VMEM((1, pairs), jnp.int32),
            pltpu.SMEM(pair_irreps.shape, jnp.int32),
            pltpu.SMEM(slab_irreps.shape, jnp.int32),
            dma, dma((chunks,)), dma, dma((chunks,)),
            dma((n_slab - 1,)), dma((n_slab - 1,)), dma((n_slab - 1,)), dma((n_slab - 1,)),
            dma((6,)), dma((chunks,)), pltpu.SemaphoreType.REGULAR,
        ],
        compiler_params=pltpu.CompilerParams(
            collective_id=0, has_side_effects=True, vmem_limit_bytes=40 * 2**20
        ),
        cost_estimate=pl.CostEstimate(
            flops=4 * pairs * pairs * slabs * square // n_dev,
            bytes_accessed=8 * slabs * pair_dev * square,
            transcendentals=0,
        ),
    )(*(pltpu.with_memory_space_constraint(x, pltpu.HBM) for x in operands))
    return out.reshape(pair_dev, side, slabs, side).transpose(0, 2, 1, 3).reshape(amplitudes.shape)


def body(amplitudes, pair_irreps, slab_irreps, ladder_ints, vv_blocks):
    n_idx = lax.axis_size("idx")
    n_slab = lax.axis_size("slab")
    whole = (amplitudes, pair_irreps, slab_irreps, ladder_ints, vv_blocks, n_idx, n_slab)
    if (n_idx, n_slab) == (8, 4):
        return ladder(*whole)
    return exchange(amplitudes.transpose(1, 0, 2), *whole[1:])


def solution(mesh):
    return jax.shard_map(
        body,
        mesh=mesh,
        in_specs=(P(("idx", "slab"), None, None), P(), P(), P(None, "slab"), P(None, "slab", None)),
        out_specs=P(("idx", "slab"), None, None),
        check_vma=False,
    )
```

```python
import functools

import jax
import jax.numpy as jnp
from jax import lax
from jax.experimental import pallas as pl
from jax.experimental.pallas import tpu as pltpu
from jax.sharding import PartitionSpec as P

MESH = pl.DeviceIdType.MESH


def exchange_kernel(
    n_idx, n_slab, cw, t_ref, labels_ref, slab_labels_ref, row_ref, w_ref, v_ref, out_ref,
    recv, wfull, res, hole, vfull, rows_in, rows_out, labels, slab_labels,
    send1, recv1, send2, recv2, wsend, wrecv, vsend, vrecv, own_sems,
):
    n_dev = n_idx * n_slab
    pair_dev = t_ref.shape[1]
    square = t_ref.shape[2]
    width = t_ref.shape[0] * square // n_dev
    chunks = width // cw
    w_cols = w_ref.shape[1]
    v_rows = v_ref.shape[1]
    e = lax.axis_index("idx")
    s = lax.axis_index("slab")
    me = e * n_slab + s
    my_block = (s * n_idx + e) * pair_dev
    others = n_dev - 1

    def where(peer):
        return (peer // n_slab, peer % n_slab)

    barrier = pltpu.get_barrier_semaphore()

    def greet(j, carry):
        pl.semaphore_signal(barrier, inc=1, device_id=where((me + j) % n_dev), device_id_type=MESH)
        return carry

    lax.fori_loop(1, n_dev, greet, 0)
    pl.semaphore_wait(barrier, others)

    locals_ = [
        pltpu.make_async_copy(
            w_ref, wfull.at[:, pl.ds(pl.multiple_of(s * w_cols, 128), w_cols)], own_sems.at[0]
        ),
        pltpu.make_async_copy(
            v_ref, vfull.at[:, pl.ds(pl.multiple_of(s * v_rows, 16), v_rows), :], own_sems.at[1]
        ),
        pltpu.make_async_copy(labels_ref, labels, own_sems.at[2]),
        pltpu.make_async_copy(slab_labels_ref, slab_labels, own_sems.at[3]),
    ]
    for copy in locals_:
        copy.start()

    def order(j):
        return j

    def columns(device, k):
        first = device * width + k * cw
        return first // square, pl.ds(pl.multiple_of(first % square, 128), cw)

    def send_chunk(k):
        def body(j, carry):
            peer = (me + order(j)) % n_dev
            plane, place = columns(peer, k)
            pltpu.make_async_remote_copy(
                src_ref=t_ref.at[plane, :, place],
                dst_ref=recv.at[k, pl.ds(pl.multiple_of(my_block, 16), pair_dev), :],
                send_sem=send1,
                recv_sem=recv1.at[k],
                device_id=where(peer),
                device_id_type=MESH,
            ).start()
            return carry

        lax.fori_loop(1, n_dev, body, 0)
        plane, place = columns(me, k)
        recv[k, pl.ds(pl.multiple_of(my_block, 16), pair_dev), :] = t_ref[plane, :, place]

    def gather(j):
        peer = (s + j) % n_slab
        return (
            pltpu.make_async_remote_copy(
                src_ref=w_ref,
                dst_ref=wfull.at[:, pl.ds(pl.multiple_of(s * w_cols, 128), w_cols)],
                send_sem=wsend.at[j - 1],
                recv_sem=wrecv.at[j - 1],
                device_id=(e, peer),
                device_id_type=MESH,
            ),
            pltpu.make_async_remote_copy(
                src_ref=v_ref,
                dst_ref=vfull.at[:, pl.ds(pl.multiple_of(s * v_rows, 16), v_rows), :],
                send_sem=vsend.at[j - 1],
                recv_sem=vrecv.at[j - 1],
                device_id=(e, peer),
                device_id_type=MESH,
            ),
        )

    send_chunk(0)
    gathers = [gather(j) for j in range(1, n_slab)]
    for w_copy, v_copy in gathers:
        w_copy.start()
        v_copy.start()
    for k in range(1, chunks):
        send_chunk(k)
    for copy in locals_:
        copy.wait()
    for _, v_copy in gathers:
        v_copy.wait()

    side = vfull.shape[1]
    slabs = t_ref.shape[0]
    def particle(plane):

        def take(c, carry):
            rows_in[pl.ds(pl.multiple_of(c * pair_dev, 16), pair_dev), :] = t_ref[
                plane, :, pl.ds(pl.multiple_of(c * side, 128), side)
            ].astype(jnp.float32)
            return carry

        def one(i, carry):
            g = jnp.bitwise_xor(labels[me * pair_dev + i], slab_labels[plane])
            x = rows_in[pl.ds(i, side, stride=pair_dev), :].astype(jnp.bfloat16)
            rows_out[plane, pl.ds(i, side, stride=pair_dev), :] = jnp.dot(
                vfull[g], x, preferred_element_type=jnp.float32
            )
            return carry

        lax.fori_loop(0, side, take, 0, unroll=8)
        lax.fori_loop(0, pair_dev, one, 0, unroll=4)

    for plane in range(slabs):
        particle(plane)

    for w_copy, _ in gathers:
        w_copy.wait()

    pairs = recv.shape[1]
    tile = min(pairs, 512)
    irreps = vfull.shape[0]
    onehot = (
        row_ref[...] == lax.broadcasted_iota(jnp.int32, (irreps, pairs), 0)
    ).astype(jnp.float32).astype(jnp.bfloat16)

    def mask_columns(n, carry):
        cols = pl.ds(pl.multiple_of(n * tile, tile), tile)
        col = lax.broadcasted_iota(jnp.int32, (pairs, tile), 1) + n * tile
        row = lax.broadcasted_iota(jnp.int32, (pairs, tile), 0)
        p, q = col % pair_dev, col // pair_dev
        kl = ((q % n_idx) * n_slab + q // n_idx) * pair_dev + p
        moved = jnp.dot(
            onehot,
            (row == kl).astype(jnp.float32).astype(jnp.bfloat16),
            preferred_element_type=jnp.float32,
        ).astype(jnp.bfloat16)
        equal = lax.dot_general(
            onehot, moved, (((0,), (0,)), ((), ())), preferred_element_type=jnp.float32
        )
        wfull[:, cols] = jnp.where(
            equal > 0.5, wfull[:, cols].astype(jnp.float32), 0.0
        ).astype(jnp.bfloat16)
        return carry

    lax.fori_loop(0, pairs // tile, mask_columns, 0)

    for k in range(chunks):
        plane, place = columns(me, k)
        landed = recv.at[k, pl.ds(0, others * pair_dev), :]
        pltpu.make_async_copy(landed, landed, recv1.at[k]).wait()

        def multiply(m, carry):
            rows = pl.ds(pl.multiple_of(m * tile, tile), tile)
            res[k, rows, :] = jnp.dot(
                wfull[rows, :], recv[k], preferred_element_type=jnp.float32
            ).astype(jnp.bfloat16)
            return carry

        lax.fori_loop(0, pairs // tile, multiply, 0)

        def give(j, carry):
            peer = (me + order(j)) % n_dev
            pltpu.make_async_remote_copy(
                src_ref=res.at[k, pl.ds(pl.multiple_of(peer * pair_dev, 16), pair_dev), :],
                dst_ref=hole.at[plane, :, place],
                send_sem=send2,
                recv_sem=recv2.at[k],
                device_id=where(peer),
                device_id_type=MESH,
            ).start()
            return carry

        lax.fori_loop(1, n_dev, give, 0)
        hole[plane, :, place] = res[k, pl.ds(pl.multiple_of(me * pair_dev, 16), pair_dev), :]


    per_plane = n_dev // slabs
    for k in range(chunks):
        landed = recv.at[k, pl.ds(0, others * pair_dev), :]
        pltpu.make_async_copy(landed, landed, recv2.at[k]).wait()
        for plane in range(slabs):

            def finish(d, carry):
                for u in range(cw // side):
                    first = d * width + k * cw + u * side
                    cols = pl.ds(pl.multiple_of(first, 128), side)
                    rows = pl.ds(pl.multiple_of(first // side * pair_dev, 16), pair_dev)
                    out_ref[:, plane, cols] = rows_out[plane, rows, :] + hole[
                        plane, :, cols
                    ].astype(jnp.float32)
                return carry

            lax.fori_loop(0, per_plane, finish, 0, unroll=2)

    everything = recv.at[:, pl.ds(0, others * pair_dev), :]
    for sem in (send1, send2):
        pltpu.make_async_copy(everything, everything, sem).wait()


def exchange(t, pair_irreps, slab_irreps, w, v, n_idx, n_slab):
    slabs, pair_dev, square = t.shape
    n_dev = n_idx * n_slab
    pairs = w.shape[0]
    width = slabs * square // n_dev
    cw = min(width, 256)
    chunks = width // cw
    irreps, v_rows, side = v.shape
    block = (chunks, pairs, cw)
    vmem = pl.BlockSpec(memory_space=pltpu.VMEM)
    anywhere = pl.BlockSpec(memory_space=pl.ANY)
    held = 2 * (pairs * pairs + 12 * slabs * pair_dev * square)
    dma = pltpu.SemaphoreType.DMA
    return pl.pallas_call(
        functools.partial(exchange_kernel, n_idx, n_slab, cw),
        out_shape=jax.ShapeDtypeStruct((pair_dev, slabs, square), jnp.float32),
        in_specs=[vmem, anywhere, anywhere, vmem, anywhere, anywhere],
        out_specs=vmem,
        scratch_shapes=[
            pltpu.VMEM(block, jnp.bfloat16),
            pltpu.VMEM((pairs, pairs), jnp.bfloat16),
            pltpu.VMEM(block, jnp.bfloat16),
            pltpu.VMEM(t.shape, jnp.bfloat16),
            pltpu.VMEM((irreps, v_rows * n_slab, side), jnp.bfloat16),
            pltpu.VMEM((side * pair_dev, side), jnp.float32),
            pltpu.VMEM((slabs, side * pair_dev, side), jnp.float32),
            pltpu.SMEM(pair_irreps.shape, jnp.int32),
            pltpu.SMEM(slab_irreps.shape, jnp.int32),
            dma, dma((chunks,)), dma, dma((chunks,)),
            dma((n_slab - 1,)), dma((n_slab - 1,)), dma((n_slab - 1,)), dma((n_slab - 1,)), dma((4,)),
        ],
        compiler_params=pltpu.CompilerParams(
            collective_id=0, has_side_effects=True, vmem_limit_bytes=held + 10 * 2**20
        ),
        cost_estimate=pl.CostEstimate(
            flops=2 * pairs * pairs * width,
            bytes_accessed=8 * slabs * pair_dev * square,
            transcendentals=0,
        ),
    )(t, pair_irreps, slab_irreps, pair_irreps.reshape(1, pairs), w, v)


def ladder_kernel(
    n_idx, n_slab, t_ref, labels_ref, slab_labels_ref, row_ref, w_ref, v_ref, out_ref,
    recv, wfull, wide, res, hole, mine, vfull, vwide, row, labels, slab_labels,
    send1, recv1, send2, recv2, wsend, wrecv, vsend, vrecv, own_sems, keep_sem, late, pre,
):
    n_dev = n_idx * n_slab
    pair_dev, side, slabs, _ = t_ref.shape
    chunks, pairs, width = recv.shape[:3]
    w_cols = w_ref.shape[1]
    irreps, v_rows, _ = v_ref.shape
    e = lax.axis_index("idx")
    s = lax.axis_index("slab")
    z, x, y, core = e // 2, e % 2, s // 2, s % 2
    me = e * n_slab + s
    my_block = (s * n_idx + e) * pair_dev
    others = n_dev - 1
    plane_dev = n_dev // 4
    group = 2 * plane_dev
    inner = (z == 1) | (z == 2)
    outer = (z == 0) | (z == 3)

    def flip(bit, by):
        return bit + by - 2 * bit * by

    def partner(dz, q):
        pz = flip(z // 2, dz // 2) * 2 + flip(z % 2, dz % 2)
        return pz * 2 + flip(x, q // 4), flip(y, q // 2 % 2) * 2 + flip(core, q % 2)

    def of_kind(i):
        return partner(3 * (1 - i // plane_dev), plane_dev - 1 - i % plane_dev)

    def of_other_kind(i):
        return partner(2 - i // plane_dev, plane_dev - 1 - i % plane_dev)

    def of_all(i):
        return partner(3 - i // plane_dev, plane_dev - 1 - i % plane_dev)

    def signal(sem, count, peer_of):
        def body(i, carry):
            pl.semaphore_signal(sem, inc=1, device_id=peer_of(i), device_id_type=MESH)
            return carry

        lax.fori_loop(0, count, body, 0)

    def columns(k, device):
        return pl.ds(k * n_dev * width + device * width, width)

    keep = [
        pltpu.make_async_copy(
            t_ref.at[:, columns(k, me)],
            recv.at[k, pl.ds(pl.multiple_of(my_block, 16), pair_dev)],
            keep_sem.at[k],
        )
        for k in range(chunks)
    ]
    locals_ = [
        pltpu.make_async_copy(
            w_ref, wfull.at[:, pl.ds(pl.multiple_of(s * w_cols, 128), w_cols)], own_sems.at[0]
        ),
        pltpu.make_async_copy(
            v_ref, vfull.at[:, pl.ds(pl.multiple_of(s * v_rows, 16), v_rows), :], own_sems.at[1]
        ),
        pltpu.make_async_copy(labels_ref, labels, own_sems.at[2]),
        pltpu.make_async_copy(slab_labels_ref, slab_labels, own_sems.at[3]),
        pltpu.make_async_copy(row_ref, row, own_sems.at[4]),
        pltpu.make_async_copy(t_ref, mine, own_sems.at[5]),
    ]

    def send(k, count, peer_of, first=0):
        def body(i, carry):
            pe, ps = peer_of(i)
            pltpu.make_async_remote_copy(
                src_ref=t_ref.at[:, columns(k, pe * n_slab + ps)],
                dst_ref=recv.at[k, pl.ds(pl.multiple_of(my_block, 16), pair_dev)],
                send_sem=send1,
                recv_sem=recv1.at[k],
                device_id=(pe, ps),
                device_id_type=MESH,
            ).start()
            return carry

        lax.fori_loop(first, count, body, 0)

    def gather(j):
        peer = (s + j) % n_slab
        return (
            pltpu.make_async_remote_copy(
                src_ref=w_ref,
                dst_ref=wfull.at[:, pl.ds(pl.multiple_of(s * w_cols, 128), w_cols)],
                send_sem=wsend.at[j - 1],
                recv_sem=wrecv.at[j - 1],
                device_id=(e, peer),
                device_id_type=MESH,
            ),
            pltpu.make_async_remote_copy(
                src_ref=v_ref,
                dst_ref=vfull.at[:, pl.ds(pl.multiple_of(s * v_rows, 16), v_rows), :],
                send_sem=vsend.at[j - 1],
                recv_sem=vrecv.at[j - 1],
                device_id=(e, peer),
                device_id_type=MESH,
            ),
        )

    gathers = [gather(j) for j in range(1, n_slab)]
    def start_gathers():
        for w_copy, v_copy in gathers:
            w_copy.start()
            v_copy.start()

    barrier = pltpu.get_barrier_semaphore()
    def second_cores(i):
        pe, ps = partner(3 * (i // 4), i % 4 * 2)
        return pe, ps // 2 * 2 + 1

    def facing(i):
        return partner(3, i)

    def mate(i):
        return partner(0, 1)

    @pl.when(inner)
    def _():
        signal(barrier, 2, facing)

        def tell(i, carry):
            pe, ps = second_cores(i)

            @pl.when((pe % 2 != x) | (ps // 2 != y))
            def _():
                pl.semaphore_signal(barrier, inc=1, device_id=(pe, ps), device_id_type=MESH)

            return carry

        lax.fori_loop(0, plane_dev, tell, 0)
        signal(barrier, 1, mate)
        signal(barrier, group, of_other_kind)

    @pl.when(outer)
    def _():
        signal(barrier, group - 1, of_kind)

    for copy in keep + locals_:
        copy.start()

    def send_facing():
        for k in range(chunks):
            send(k, plane_dev, of_kind, plane_dev - 2)

    @pl.when(inner)
    def _():
        @pl.when(core == 0)
        def _():
            pl.semaphore_wait(barrier, 3)
            signal(pre, 1, mate)
            send_facing()
            pl.semaphore_wait(pre, 1)

        @pl.when(core == 1)
        def _():
            pl.semaphore_wait(pre, 1)
            send_facing()
            pl.semaphore_wait(barrier, group - 1)
            signal(pre, 1, mate)

        send(0, plane_dev - 2, of_kind)
        start_gathers()
        send(0, group - 1, of_kind, plane_dev)
        pl.semaphore_wait(late, group)
        send(0, group, of_other_kind)
        for k in range(1, chunks):
            send(k, plane_dev - 2, of_kind)
            send(k, group - 1, of_kind, plane_dev)
            send(k, group, of_other_kind)

    @pl.when(outer)
    def _():
        pl.semaphore_wait(barrier, others)
        send(0, plane_dev, of_all)
        signal(late, group, of_other_kind)
        send(0, group, of_all, plane_dev)
        start_gathers()
        send(0, others, of_all, group)
        for k in range(1, chunks):
            send(k, others, of_all)

    for copy in locals_:
        copy.wait()
    for w_copy, _ in gathers:
        w_copy.wait()

    def equal(shape, left, right):
        return (
            left(lax.broadcasted_iota(jnp.int32, shape, 0))
            == right(lax.broadcasted_iota(jnp.int32, shape, 1))
        )

    def ones(mask):
        return mask.astype(jnp.float32).astype(jnp.bfloat16)

    def same(x):
        return x

    def half(x):
        return x // slabs

    def rest(x):
        return x % slabs

    onehot = ones(row[...] == lax.broadcasted_iota(jnp.int32, (irreps, pairs), 0))

    def column_pair(q):
        p, q = q % pair_dev, q // pair_dev
        return ((q % n_idx) * n_slab + q // n_idx) * pair_dev + p

    moved = jnp.dot(
        onehot, ones(equal((pairs, pairs), same, column_pair)), preferred_element_type=jnp.float32
    ).astype(jnp.bfloat16)
    allowed = lax.dot_general(
        onehot, moved, (((0,), (0,)), ((), ())), preferred_element_type=jnp.float32
    )
    wfull[...] = jnp.where(allowed > 0.5, wfull[...].astype(jnp.float32), 0.0).astype(jnp.bfloat16)

    tile = 256
    spread = ones(equal((pairs, slabs * pairs), same, half))

    def widen(m, carry):
        down = ones(
            equal((tile, tile // slabs), half, same)
        )
        part = jnp.dot(
            down,
            wfull[pl.ds(pl.multiple_of(m * (tile // slabs), 16), tile // slabs), :],
            preferred_element_type=jnp.float32,
        ).astype(jnp.bfloat16)
        both = jnp.dot(part, spread, preferred_element_type=jnp.float32)
        wide[pl.ds(pl.multiple_of(m * tile, 16), tile), :] = jnp.where(
            equal(both.shape, rest, rest), both, 0.0
        ).astype(jnp.bfloat16)
        return carry

    lax.fori_loop(0, slabs * pairs // tile, widen, 0)

    def give(k, far):
        def body(j, carry):
            t = j % 2
            q = j // 2 - 4 * t
            pe = (flip(z // 2, far) * 2 + t) * 2 + q // 4
            ps = q // 2 % 2 * 2 + flip(core, q % 2)
            peer = pe * n_slab + ps

            @pl.when((q >= 0) & (q < plane_dev) & (peer != me))
            def _():
                pltpu.make_async_remote_copy(
                    src_ref=res.at[k, pl.ds(pl.multiple_of(peer * pair_dev, 16), pair_dev)],
                    dst_ref=hole.at[:, columns(k, me)],
                    send_sem=send2,
                    recv_sem=recv2.at[k],
                    device_id=(pe, ps),
                    device_id_type=MESH,
                ).start()

            return carry

        lax.fori_loop(0, group + 8, body, 0)

    for k in range(chunks):
        keep[k].wait()
        landed = recv.at[k, pl.ds(0, others * pair_dev)]
        pltpu.make_async_copy(landed, landed, recv1.at[k]).wait()
        right = jnp.concatenate(
            [recv[k, :, u].reshape(slabs * pairs, side) for u in range(width)], axis=1
        )

        for m in range(slabs * pairs // tile):
            got = jnp.dot(
                wide[m * tile : (m + 1) * tile, :], right, preferred_element_type=jnp.float32
            ).astype(jnp.bfloat16)
            for u in range(width):
                res[k, m * (tile // slabs) : (m + 1) * (tile // slabs), u] = got[
                    :, u * side : (u + 1) * side
                ].reshape(tile // slabs, slabs, side)

        give(k, 0)
        give(k, 1)
        hole[:, columns(k, me)] = res[k, pl.ds(pl.multiple_of(me * pair_dev, 16), pair_dev)]

    for _, v_copy in gathers:
        v_copy.wait()

    rows = slabs * side
    for g in range(irreps):
        tall = jnp.dot(
            ones(equal((rows, side), half, same)), vfull[g], preferred_element_type=jnp.float32
        ).astype(jnp.bfloat16)
        both = jnp.dot(
            tall, ones(equal((side, rows), same, half)), preferred_element_type=jnp.float32
        )
        together = equal((rows, rows), rest, rest)
        for plane in range(slabs):
            mask = together & (lax.broadcasted_iota(jnp.int32, (rows, rows), 0) % slabs == plane)
            vwide[plane, g] = jnp.where(mask, both, 0.0).astype(jnp.bfloat16)

    def particle(i, carry):
        x = mine[i].reshape(rows, side)
        total = jnp.zeros((rows, side), jnp.float32)
        for plane in range(slabs):
            g = jnp.bitwise_xor(labels[me * pair_dev + i], slab_labels[plane])
            total += jnp.dot(vwide[plane, g], x, preferred_element_type=jnp.float32)
        out_ref[i] = total
        return carry

    lax.fori_loop(0, pair_dev, particle, 0)

    for k in range(chunks):
        landed = recv.at[k, pl.ds(0, others * pair_dev)]
        pltpu.make_async_copy(landed, landed, recv2.at[k]).wait()

        def finish(i, carry):
            part = side // chunks
            out_ref[i, k * part * slabs : (k + 1) * part * slabs, :] += (
                hole[i, k * part : (k + 1) * part].reshape(part * slabs, side).astype(jnp.float32)
            )
            return carry

        lax.fori_loop(0, pair_dev, finish, 0, unroll=4)

    everything = recv.at[:, pl.ds(0, others * pair_dev)]
    for sem in (send1, send2):
        pltpu.make_async_copy(everything, everything, sem).wait()


def ladder(amplitudes, pair_irreps, slab_irreps, w, v, n_idx, n_slab):
    pair_dev, slabs, square = amplitudes.shape
    n_dev = n_idx * n_slab
    pairs = w.shape[0]
    irreps, v_rows, side = v.shape
    width = 2
    chunks = side // n_dev // width
    t = amplitudes.reshape(pair_dev, slabs, side, side).transpose(0, 2, 1, 3)
    operands = (t, pair_irreps, slab_irreps, pair_irreps.reshape(1, pairs), w, v)
    hbm = pl.BlockSpec(memory_space=pltpu.HBM)
    dma = pltpu.SemaphoreType.DMA
    bf16 = jnp.bfloat16
    out = pl.pallas_call(
        functools.partial(ladder_kernel, n_idx, n_slab),
        out_shape=jax.ShapeDtypeStruct((pair_dev, side * slabs, side), jnp.float32),
        in_specs=[hbm] * 6,
        out_specs=pl.BlockSpec(memory_space=pltpu.VMEM),
        scratch_shapes=[
            pltpu.VMEM((chunks, pairs, width, slabs, side), bf16),
            pltpu.VMEM((pairs, pairs), bf16),
            pltpu.VMEM((slabs * pairs, slabs * pairs), bf16),
            pltpu.VMEM((chunks, pairs, width, slabs, side), bf16),
            pltpu.VMEM(t.shape, bf16),
            pltpu.VMEM(t.shape, bf16),
            pltpu.VMEM((irreps, side, side), bf16),
            pltpu.VMEM((slabs, irreps, slabs * side, slabs * side), bf16),
            pltpu.VMEM((1, pairs), jnp.int32),
            pltpu.SMEM(pair_irreps.shape, jnp.int32),
            pltpu.SMEM(slab_irreps.shape, jnp.int32),
            dma, dma((chunks,)), dma, dma((chunks,)),
            dma((n_slab - 1,)), dma((n_slab - 1,)), dma((n_slab - 1,)), dma((n_slab - 1,)),
            dma((6,)), dma((chunks,)), pltpu.SemaphoreType.REGULAR,
            pltpu.SemaphoreType.REGULAR,
        ],
        compiler_params=pltpu.CompilerParams(
            collective_id=0, has_side_effects=True, vmem_limit_bytes=40 * 2**20
        ),
        cost_estimate=pl.CostEstimate(
            flops=4 * pairs * pairs * slabs * square // n_dev,
            bytes_accessed=8 * slabs * pair_dev * square,
            transcendentals=0,
        ),
    )(*(pltpu.with_memory_space_constraint(x, pltpu.HBM) for x in operands))
    return out.reshape(pair_dev, side, slabs, side).transpose(0, 2, 1, 3).reshape(amplitudes.shape)


def body(amplitudes, pair_irreps, slab_irreps, ladder_ints, vv_blocks):
    n_idx = lax.axis_size("idx")
    n_slab = lax.axis_size("slab")
    whole = (amplitudes, pair_irreps, slab_irreps, ladder_ints, vv_blocks, n_idx, n_slab)
    if (n_idx, n_slab) == (8, 4):
        return ladder(*whole)
    return exchange(amplitudes.transpose(1, 0, 2), *whole[1:])


def solution(mesh):
    return jax.shard_map(
        body,
        mesh=mesh,
        in_specs=(P(("idx", "slab"), None, None), P(), P(), P(None, "slab"), P(None, "slab", None)),
        out_specs=P(("idx", "slab"), None, None),
        check_vma=False,
    )
```

```python
import functools

import jax
import jax.numpy as jnp
from jax import lax
from jax.experimental import pallas as pl
from jax.experimental.pallas import tpu as pltpu
from jax.sharding import PartitionSpec as P

MESH = pl.DeviceIdType.MESH


def exchange_kernel(
    n_idx, n_slab, cw, t_ref, labels_ref, slab_labels_ref, row_ref, w_ref, v_ref, out_ref,
    recv, wfull, res, hole, vfull, rows_in, rows_out, labels, slab_labels,
    send1, recv1, send2, recv2, wsend, wrecv, vsend, vrecv, own_sems,
):
    n_dev = n_idx * n_slab
    pair_dev = t_ref.shape[1]
    square = t_ref.shape[2]
    width = t_ref.shape[0] * square // n_dev
    chunks = width // cw
    w_cols = w_ref.shape[1]
    v_rows = v_ref.shape[1]
    e = lax.axis_index("idx")
    s = lax.axis_index("slab")
    me = e * n_slab + s
    my_block = (s * n_idx + e) * pair_dev
    others = n_dev - 1

    def where(peer):
        return (peer // n_slab, peer % n_slab)

    barrier = pltpu.get_barrier_semaphore()

    def greet(j, carry):
        pl.semaphore_signal(barrier, inc=1, device_id=where((me + j) % n_dev), device_id_type=MESH)
        return carry

    lax.fori_loop(1, n_dev, greet, 0)
    pl.semaphore_wait(barrier, others)

    locals_ = [
        pltpu.make_async_copy(
            w_ref, wfull.at[:, pl.ds(pl.multiple_of(s * w_cols, 128), w_cols)], own_sems.at[0]
        ),
        pltpu.make_async_copy(
            v_ref, vfull.at[:, pl.ds(pl.multiple_of(s * v_rows, 16), v_rows), :], own_sems.at[1]
        ),
        pltpu.make_async_copy(labels_ref, labels, own_sems.at[2]),
        pltpu.make_async_copy(slab_labels_ref, slab_labels, own_sems.at[3]),
    ]
    for copy in locals_:
        copy.start()

    def order(j):
        return j

    def columns(device, k):
        first = device * width + k * cw
        return first // square, pl.ds(pl.multiple_of(first % square, 128), cw)

    def send_chunk(k):
        def body(j, carry):
            peer = (me + order(j)) % n_dev
            plane, place = columns(peer, k)
            pltpu.make_async_remote_copy(
                src_ref=t_ref.at[plane, :, place],
                dst_ref=recv.at[k, pl.ds(pl.multiple_of(my_block, 16), pair_dev), :],
                send_sem=send1,
                recv_sem=recv1.at[k],
                device_id=where(peer),
                device_id_type=MESH,
            ).start()
            return carry

        lax.fori_loop(1, n_dev, body, 0)
        plane, place = columns(me, k)
        recv[k, pl.ds(pl.multiple_of(my_block, 16), pair_dev), :] = t_ref[plane, :, place]

    def gather(j):
        peer = (s + j) % n_slab
        return (
            pltpu.make_async_remote_copy(
                src_ref=w_ref,
                dst_ref=wfull.at[:, pl.ds(pl.multiple_of(s * w_cols, 128), w_cols)],
                send_sem=wsend.at[j - 1],
                recv_sem=wrecv.at[j - 1],
                device_id=(e, peer),
                device_id_type=MESH,
            ),
            pltpu.make_async_remote_copy(
                src_ref=v_ref,
                dst_ref=vfull.at[:, pl.ds(pl.multiple_of(s * v_rows, 16), v_rows), :],
                send_sem=vsend.at[j - 1],
                recv_sem=vrecv.at[j - 1],
                device_id=(e, peer),
                device_id_type=MESH,
            ),
        )

    send_chunk(0)
    gathers = [gather(j) for j in range(1, n_slab)]
    for w_copy, v_copy in gathers:
        w_copy.start()
        v_copy.start()
    for k in range(1, chunks):
        send_chunk(k)
    for copy in locals_:
        copy.wait()
    for _, v_copy in gathers:
        v_copy.wait()

    side = vfull.shape[1]
    slabs = t_ref.shape[0]
    def particle(plane):

        def take(c, carry):
            rows_in[pl.ds(pl.multiple_of(c * pair_dev, 16), pair_dev), :] = t_ref[
                plane, :, pl.ds(pl.multiple_of(c * side, 128), side)
            ].astype(jnp.float32)
            return carry

        def one(i, carry):
            g = jnp.bitwise_xor(labels[me * pair_dev + i], slab_labels[plane])
            x = rows_in[pl.ds(i, side, stride=pair_dev), :].astype(jnp.bfloat16)
            rows_out[plane, pl.ds(i, side, stride=pair_dev), :] = jnp.dot(
                vfull[g], x, preferred_element_type=jnp.float32
            )
            return carry

        lax.fori_loop(0, side, take, 0, unroll=8)
        lax.fori_loop(0, pair_dev, one, 0, unroll=4)

    for plane in range(slabs):
        particle(plane)

    for w_copy, _ in gathers:
        w_copy.wait()

    pairs = recv.shape[1]
    tile = min(pairs, 512)
    irreps = vfull.shape[0]
    onehot = (
        row_ref[...] == lax.broadcasted_iota(jnp.int32, (irreps, pairs), 0)
    ).astype(jnp.float32).astype(jnp.bfloat16)

    def mask_columns(n, carry):
        cols = pl.ds(pl.multiple_of(n * tile, tile), tile)
        col = lax.broadcasted_iota(jnp.int32, (pairs, tile), 1) + n * tile
        row = lax.broadcasted_iota(jnp.int32, (pairs, tile), 0)
        p, q = col % pair_dev, col // pair_dev
        kl = ((q % n_idx) * n_slab + q // n_idx) * pair_dev + p
        moved = jnp.dot(
            onehot,
            (row == kl).astype(jnp.float32).astype(jnp.bfloat16),
            preferred_element_type=jnp.float32,
        ).astype(jnp.bfloat16)
        equal = lax.dot_general(
            onehot, moved, (((0,), (0,)), ((), ())), preferred_element_type=jnp.float32
        )
        wfull[:, cols] = jnp.where(
            equal > 0.5, wfull[:, cols].astype(jnp.float32), 0.0
        ).astype(jnp.bfloat16)
        return carry

    lax.fori_loop(0, pairs // tile, mask_columns, 0)

    for k in range(chunks):
        plane, place = columns(me, k)
        landed = recv.at[k, pl.ds(0, others * pair_dev), :]
        pltpu.make_async_copy(landed, landed, recv1.at[k]).wait()

        def multiply(m, carry):
            rows = pl.ds(pl.multiple_of(m * tile, tile), tile)
            res[k, rows, :] = jnp.dot(
                wfull[rows, :], recv[k], preferred_element_type=jnp.float32
            ).astype(jnp.bfloat16)
            return carry

        lax.fori_loop(0, pairs // tile, multiply, 0)

        def give(j, carry):
            peer = (me + order(j)) % n_dev
            pltpu.make_async_remote_copy(
                src_ref=res.at[k, pl.ds(pl.multiple_of(peer * pair_dev, 16), pair_dev), :],
                dst_ref=hole.at[plane, :, place],
                send_sem=send2,
                recv_sem=recv2.at[k],
                device_id=where(peer),
                device_id_type=MESH,
            ).start()
            return carry

        lax.fori_loop(1, n_dev, give, 0)
        hole[plane, :, place] = res[k, pl.ds(pl.multiple_of(me * pair_dev, 16), pair_dev), :]


    per_plane = n_dev // slabs
    for k in range(chunks):
        landed = recv.at[k, pl.ds(0, others * pair_dev), :]
        pltpu.make_async_copy(landed, landed, recv2.at[k]).wait()
        for plane in range(slabs):

            def finish(d, carry):
                for u in range(cw // side):
                    first = d * width + k * cw + u * side
                    cols = pl.ds(pl.multiple_of(first, 128), side)
                    rows = pl.ds(pl.multiple_of(first // side * pair_dev, 16), pair_dev)
                    out_ref[:, plane, cols] = rows_out[plane, rows, :] + hole[
                        plane, :, cols
                    ].astype(jnp.float32)
                return carry

            lax.fori_loop(0, per_plane, finish, 0, unroll=2)

    everything = recv.at[:, pl.ds(0, others * pair_dev), :]
    for sem in (send1, send2):
        pltpu.make_async_copy(everything, everything, sem).wait()


def exchange(t, pair_irreps, slab_irreps, w, v, n_idx, n_slab):
    slabs, pair_dev, square = t.shape
    n_dev = n_idx * n_slab
    pairs = w.shape[0]
    width = slabs * square // n_dev
    cw = min(width, 256)
    chunks = width // cw
    irreps, v_rows, side = v.shape
    block = (chunks, pairs, cw)
    vmem = pl.BlockSpec(memory_space=pltpu.VMEM)
    anywhere = pl.BlockSpec(memory_space=pl.ANY)
    held = 2 * (pairs * pairs + 12 * slabs * pair_dev * square)
    dma = pltpu.SemaphoreType.DMA
    return pl.pallas_call(
        functools.partial(exchange_kernel, n_idx, n_slab, cw),
        out_shape=jax.ShapeDtypeStruct((pair_dev, slabs, square), jnp.float32),
        in_specs=[vmem, anywhere, anywhere, vmem, anywhere, anywhere],
        out_specs=vmem,
        scratch_shapes=[
            pltpu.VMEM(block, jnp.bfloat16),
            pltpu.VMEM((pairs, pairs), jnp.bfloat16),
            pltpu.VMEM(block, jnp.bfloat16),
            pltpu.VMEM(t.shape, jnp.bfloat16),
            pltpu.VMEM((irreps, v_rows * n_slab, side), jnp.bfloat16),
            pltpu.VMEM((side * pair_dev, side), jnp.float32),
            pltpu.VMEM((slabs, side * pair_dev, side), jnp.float32),
            pltpu.SMEM(pair_irreps.shape, jnp.int32),
            pltpu.SMEM(slab_irreps.shape, jnp.int32),
            dma, dma((chunks,)), dma, dma((chunks,)),
            dma((n_slab - 1,)), dma((n_slab - 1,)), dma((n_slab - 1,)), dma((n_slab - 1,)), dma((4,)),
        ],
        compiler_params=pltpu.CompilerParams(
            collective_id=0, has_side_effects=True, vmem_limit_bytes=held + 10 * 2**20
        ),
        cost_estimate=pl.CostEstimate(
            flops=2 * pairs * pairs * width,
            bytes_accessed=8 * slabs * pair_dev * square,
            transcendentals=0,
        ),
    )(t, pair_irreps, slab_irreps, pair_irreps.reshape(1, pairs), w, v)


def ladder_kernel(
    n_idx, n_slab, t_ref, labels_ref, slab_labels_ref, row_ref, w_ref, v_ref, out_ref,
    recv, wfull, wide, res, hole, mine, vfull, vwide, row, labels, slab_labels,
    send1, recv1, send2, recv2, wsend, wrecv, vsend, vrecv, own_sems, keep_sem, late, pre,
):
    n_dev = n_idx * n_slab
    pair_dev, side, slabs, _ = t_ref.shape
    chunks, pairs, width = recv.shape[:3]
    w_cols = w_ref.shape[1]
    irreps, v_rows, _ = v_ref.shape
    e = lax.axis_index("idx")
    s = lax.axis_index("slab")
    z, x, y, core = e // 2, e % 2, s // 2, s % 2
    me = e * n_slab + s
    my_block = (s * n_idx + e) * pair_dev
    others = n_dev - 1
    plane_dev = n_dev // 4
    group = 2 * plane_dev
    inner = (z == 1) | (z == 2)
    outer = (z == 0) | (z == 3)

    def flip(bit, by):
        return bit + by - 2 * bit * by

    def partner(dz, q):
        pz = flip(z // 2, dz // 2) * 2 + flip(z % 2, dz % 2)
        return pz * 2 + flip(x, q // 4), flip(y, q // 2 % 2) * 2 + flip(core, q % 2)

    def of_kind(i):
        return partner(3 * (1 - i // plane_dev), plane_dev - 1 - i % plane_dev)

    def of_other_kind(i):
        return partner(2 - i // plane_dev, plane_dev - 1 - i % plane_dev)

    def of_all(i):
        return partner(3 - i // plane_dev, plane_dev - 1 - i % plane_dev)

    def signal(sem, count, peer_of):
        def body(i, carry):
            pl.semaphore_signal(sem, inc=1, device_id=peer_of(i), device_id_type=MESH)
            return carry

        lax.fori_loop(0, count, body, 0)

    def columns(k, device):
        return pl.ds(k * n_dev * width + device * width, width)

    keep = [
        pltpu.make_async_copy(
            t_ref.at[:, columns(k, me)],
            recv.at[k, pl.ds(pl.multiple_of(my_block, 16), pair_dev)],
            keep_sem.at[k],
        )
        for k in range(chunks)
    ]
    locals_ = [
        pltpu.make_async_copy(
            w_ref, wfull.at[:, pl.ds(pl.multiple_of(s * w_cols, 128), w_cols)], own_sems.at[0]
        ),
        pltpu.make_async_copy(
            v_ref, vfull.at[:, pl.ds(pl.multiple_of(s * v_rows, 16), v_rows), :], own_sems.at[1]
        ),
        pltpu.make_async_copy(labels_ref, labels, own_sems.at[2]),
        pltpu.make_async_copy(slab_labels_ref, slab_labels, own_sems.at[3]),
        pltpu.make_async_copy(row_ref, row, own_sems.at[4]),
        pltpu.make_async_copy(t_ref, mine, own_sems.at[5]),
    ]

    def send(k, count, peer_of, first=0):
        def body(i, carry):
            pe, ps = peer_of(i)
            pltpu.make_async_remote_copy(
                src_ref=t_ref.at[:, columns(k, pe * n_slab + ps)],
                dst_ref=recv.at[k, pl.ds(pl.multiple_of(my_block, 16), pair_dev)],
                send_sem=send1,
                recv_sem=recv1.at[k],
                device_id=(pe, ps),
                device_id_type=MESH,
            ).start()
            return carry

        lax.fori_loop(first, count, body, 0)

    def gather(j):
        peer = (s + j) % n_slab
        return (
            pltpu.make_async_remote_copy(
                src_ref=w_ref,
                dst_ref=wfull.at[:, pl.ds(pl.multiple_of(s * w_cols, 128), w_cols)],
                send_sem=wsend.at[j - 1],
                recv_sem=wrecv.at[j - 1],
                device_id=(e, peer),
                device_id_type=MESH,
            ),
            pltpu.make_async_remote_copy(
                src_ref=v_ref,
                dst_ref=vfull.at[:, pl.ds(pl.multiple_of(s * v_rows, 16), v_rows), :],
                send_sem=vsend.at[j - 1],
                recv_sem=vrecv.at[j - 1],
                device_id=(e, peer),
                device_id_type=MESH,
            ),
        )

    gathers = [gather(j) for j in range(1, n_slab)]
    def start_gathers():
        for w_copy, v_copy in gathers:
            w_copy.start()
            v_copy.start()

    barrier = pltpu.get_barrier_semaphore()
    def second_cores(i):
        pe, ps = partner(3 * (i // 4), i % 4 * 2)
        return pe, ps // 2 * 2 + 1

    def facing(i):
        return partner(3, i)

    def mate(i):
        return partner(0, 1)

    @pl.when(inner)
    def _():
        signal(barrier, 2, facing)

        def tell(i, carry):
            pe, ps = second_cores(i)

            @pl.when((pe % 2 != x) | (ps // 2 != y))
            def _():
                pl.semaphore_signal(barrier, inc=1, device_id=(pe, ps), device_id_type=MESH)

            return carry

        lax.fori_loop(0, plane_dev, tell, 0)
        signal(barrier, 1, mate)
        signal(barrier, group, of_other_kind)

    @pl.when(outer)
    def _():
        signal(barrier, group - 1, of_kind)

    for copy in keep + locals_:
        copy.start()

    def send_facing():
        for k in range(chunks):
            send(k, plane_dev, of_kind, plane_dev - 2)

    @pl.when(inner)
    def _():
        @pl.when(core == 0)
        def _():
            pl.semaphore_wait(barrier, 3)
            signal(pre, 1, mate)
            send_facing()
            pl.semaphore_wait(pre, 1)

        @pl.when(core == 1)
        def _():
            pl.semaphore_wait(pre, 1)
            send_facing()
            pl.semaphore_wait(barrier, group - 1)
            signal(pre, 1, mate)

        send(0, plane_dev - 2, of_kind)
        start_gathers()
        send(0, group - 1, of_kind, plane_dev)
        pl.semaphore_wait(late, group)
        send(0, group, of_other_kind)
        for k in range(1, chunks):
            send(k, plane_dev - 2, of_kind)
            send(k, group - 1, of_kind, plane_dev)
            send(k, group, of_other_kind)

    @pl.when(outer)
    def _():
        pl.semaphore_wait(barrier, others)
        send(0, plane_dev, of_all)
        signal(late, group, of_other_kind)
        send(0, group, of_all, plane_dev)
        start_gathers()
        send(0, others, of_all, group)
        for k in range(1, chunks):
            send(k, others, of_all)

    for copy in locals_:
        copy.wait()
    for w_copy, _ in gathers:
        w_copy.wait()

    def equal(shape, left, right):
        return (
            left(lax.broadcasted_iota(jnp.int32, shape, 0))
            == right(lax.broadcasted_iota(jnp.int32, shape, 1))
        )

    def ones(mask):
        return mask.astype(jnp.float32).astype(jnp.bfloat16)

    def same(x):
        return x

    def half(x):
        return x // slabs

    def rest(x):
        return x % slabs

    onehot = ones(row[...] == lax.broadcasted_iota(jnp.int32, (irreps, pairs), 0))

    def column_pair(q):
        p, q = q % pair_dev, q // pair_dev
        return ((q % n_idx) * n_slab + q // n_idx) * pair_dev + p

    moved = jnp.dot(
        onehot, ones(equal((pairs, pairs), same, column_pair)), preferred_element_type=jnp.float32
    ).astype(jnp.bfloat16)
    allowed = lax.dot_general(
        onehot, moved, (((0,), (0,)), ((), ())), preferred_element_type=jnp.float32
    )
    wfull[...] = jnp.where(allowed > 0.5, wfull[...].astype(jnp.float32), 0.0).astype(jnp.bfloat16)

    tile = 256
    spread = ones(equal((pairs, slabs * pairs), same, half))

    def widen(m, carry):
        down = ones(
            equal((tile, tile // slabs), half, same)
        )
        part = jnp.dot(
            down,
            wfull[pl.ds(pl.multiple_of(m * (tile // slabs), 16), tile // slabs), :],
            preferred_element_type=jnp.float32,
        ).astype(jnp.bfloat16)
        both = jnp.dot(part, spread, preferred_element_type=jnp.float32)
        wide[pl.ds(pl.multiple_of(m * tile, 16), tile), :] = jnp.where(
            equal(both.shape, rest, rest), both, 0.0
        ).astype(jnp.bfloat16)
        return carry

    lax.fori_loop(0, slabs * pairs // tile, widen, 0)

    def give(k, far):
        def body(j, carry):
            t = j % 2
            q = j // 2 - 2 * t
            right, up = q // 4, q // 2 % 2
            pe = (flip(z // 2, far) * 2 + t) * 2 + right + t * (up - right)
            ps = (up + t * (right - up)) * 2 + flip(core, q % 2)
            peer = pe * n_slab + ps

            @pl.when((q >= 0) & (q < plane_dev) & (peer != me))
            def _():
                pltpu.make_async_remote_copy(
                    src_ref=res.at[k, pl.ds(pl.multiple_of(peer * pair_dev, 16), pair_dev)],
                    dst_ref=hole.at[:, columns(k, me)],
                    send_sem=send2,
                    recv_sem=recv2.at[k],
                    device_id=(pe, ps),
                    device_id_type=MESH,
                ).start()

            return carry

        lax.fori_loop(0, group + 8, body, 0)

    for k in range(chunks):
        keep[k].wait()
        landed = recv.at[k, pl.ds(0, others * pair_dev)]
        pltpu.make_async_copy(landed, landed, recv1.at[k]).wait()
        right = jnp.concatenate(
            [recv[k, :, u].reshape(slabs * pairs, side) for u in range(width)], axis=1
        )

        for m in range(slabs * pairs // tile):
            got = jnp.dot(
                wide[m * tile : (m + 1) * tile, :], right, preferred_element_type=jnp.float32
            ).astype(jnp.bfloat16)
            for u in range(width):
                res[k, m * (tile // slabs) : (m + 1) * (tile // slabs), u] = got[
                    :, u * side : (u + 1) * side
                ].reshape(tile // slabs, slabs, side)

        give(k, 1)
        give(k, 0)
        hole[:, columns(k, me)] = res[k, pl.ds(pl.multiple_of(me * pair_dev, 16), pair_dev)]

    for _, v_copy in gathers:
        v_copy.wait()

    rows = slabs * side
    for g in range(irreps):
        tall = jnp.dot(
            ones(equal((rows, side), half, same)), vfull[g], preferred_element_type=jnp.float32
        ).astype(jnp.bfloat16)
        both = jnp.dot(
            tall, ones(equal((side, rows), same, half)), preferred_element_type=jnp.float32
        )
        together = equal((rows, rows), rest, rest)
        for plane in range(slabs):
            mask = together & (lax.broadcasted_iota(jnp.int32, (rows, rows), 0) % slabs == plane)
            vwide[plane, g] = jnp.where(mask, both, 0.0).astype(jnp.bfloat16)

    def particle(i, carry):
        x = mine[i].reshape(rows, side)
        total = jnp.zeros((rows, side), jnp.float32)
        for plane in range(slabs):
            g = jnp.bitwise_xor(labels[me * pair_dev + i], slab_labels[plane])
            total += jnp.dot(vwide[plane, g], x, preferred_element_type=jnp.float32)
        out_ref[i] = total
        return carry

    lax.fori_loop(0, pair_dev, particle, 0)

    for k in range(chunks):
        landed = recv.at[k, pl.ds(0, others * pair_dev)]
        pltpu.make_async_copy(landed, landed, recv2.at[k]).wait()

        def finish(i, carry):
            part = side // chunks
            out_ref[i, k * part * slabs : (k + 1) * part * slabs, :] += (
                hole[i, k * part : (k + 1) * part].reshape(part * slabs, side).astype(jnp.float32)
            )
            return carry

        lax.fori_loop(0, pair_dev, finish, 0, unroll=4)

    everything = recv.at[:, pl.ds(0, others * pair_dev)]
    for sem in (send1, send2):
        pltpu.make_async_copy(everything, everything, sem).wait()


def ladder(amplitudes, pair_irreps, slab_irreps, w, v, n_idx, n_slab):
    pair_dev, slabs, square = amplitudes.shape
    n_dev = n_idx * n_slab
    pairs = w.shape[0]
    irreps, v_rows, side = v.shape
    width = 2
    chunks = side // n_dev // width
    t = amplitudes.reshape(pair_dev, slabs, side, side).transpose(0, 2, 1, 3)
    operands = (t, pair_irreps, slab_irreps, pair_irreps.reshape(1, pairs), w, v)
    hbm = pl.BlockSpec(memory_space=pltpu.HBM)
    dma = pltpu.SemaphoreType.DMA
    bf16 = jnp.bfloat16
    out = pl.pallas_call(
        functools.partial(ladder_kernel, n_idx, n_slab),
        out_shape=jax.ShapeDtypeStruct((pair_dev, side * slabs, side), jnp.float32),
        in_specs=[hbm] * 6,
        out_specs=pl.BlockSpec(memory_space=pltpu.VMEM),
        scratch_shapes=[
            pltpu.VMEM((chunks, pairs, width, slabs, side), bf16),
            pltpu.VMEM((pairs, pairs), bf16),
            pltpu.VMEM((slabs * pairs, slabs * pairs), bf16),
            pltpu.VMEM((chunks, pairs, width, slabs, side), bf16),
            pltpu.VMEM(t.shape, bf16),
            pltpu.VMEM(t.shape, bf16),
            pltpu.VMEM((irreps, side, side), bf16),
            pltpu.VMEM((slabs, irreps, slabs * side, slabs * side), bf16),
            pltpu.VMEM((1, pairs), jnp.int32),
            pltpu.SMEM(pair_irreps.shape, jnp.int32),
            pltpu.SMEM(slab_irreps.shape, jnp.int32),
            dma, dma((chunks,)), dma, dma((chunks,)),
            dma((n_slab - 1,)), dma((n_slab - 1,)), dma((n_slab - 1,)), dma((n_slab - 1,)),
            dma((6,)), dma((chunks,)), pltpu.SemaphoreType.REGULAR,
            pltpu.SemaphoreType.REGULAR,
        ],
        compiler_params=pltpu.CompilerParams(
            collective_id=0, has_side_effects=True, vmem_limit_bytes=40 * 2**20
        ),
        cost_estimate=pl.CostEstimate(
            flops=4 * pairs * pairs * slabs * square // n_dev,
            bytes_accessed=8 * slabs * pair_dev * square,
            transcendentals=0,
        ),
    )(*(pltpu.with_memory_space_constraint(x, pltpu.HBM) for x in operands))
    return out.reshape(pair_dev, side, slabs, side).transpose(0, 2, 1, 3).reshape(amplitudes.shape)


def body(amplitudes, pair_irreps, slab_irreps, ladder_ints, vv_blocks):
    n_idx = lax.axis_size("idx")
    n_slab = lax.axis_size("slab")
    whole = (amplitudes, pair_irreps, slab_irreps, ladder_ints, vv_blocks, n_idx, n_slab)
    if (n_idx, n_slab) == (8, 4):
        return ladder(*whole)
    return exchange(amplitudes.transpose(1, 0, 2), *whole[1:])


def solution(mesh):
    return jax.shard_map(
        body,
        mesh=mesh,
        in_specs=(P(("idx", "slab"), None, None), P(), P(), P(None, "slab"), P(None, "slab", None)),
        out_specs=P(("idx", "slab"), None, None),
        check_vma=False,
    )
```

```python
import functools

import jax
import jax.numpy as jnp
from jax import lax
from jax.experimental import pallas as pl
from jax.experimental.pallas import tpu as pltpu
from jax.sharding import PartitionSpec as P

MESH = pl.DeviceIdType.MESH


def exchange_kernel(
    n_idx, n_slab, cw, t_ref, labels_ref, slab_labels_ref, row_ref, w_ref, v_ref, out_ref,
    recv, wfull, res, hole, vfull, rows_in, rows_out, labels, slab_labels,
    send1, recv1, send2, recv2, wsend, wrecv, vsend, vrecv, own_sems,
):
    n_dev = n_idx * n_slab
    pair_dev = t_ref.shape[1]
    square = t_ref.shape[2]
    width = t_ref.shape[0] * square // n_dev
    chunks = width // cw
    w_cols = w_ref.shape[1]
    v_rows = v_ref.shape[1]
    e = lax.axis_index("idx")
    s = lax.axis_index("slab")
    me = e * n_slab + s
    my_block = (s * n_idx + e) * pair_dev
    others = n_dev - 1

    def where(peer):
        return (peer // n_slab, peer % n_slab)

    barrier = pltpu.get_barrier_semaphore()

    def greet(j, carry):
        pl.semaphore_signal(barrier, inc=1, device_id=where((me + j) % n_dev), device_id_type=MESH)
        return carry

    lax.fori_loop(1, n_dev, greet, 0)
    pl.semaphore_wait(barrier, others)

    locals_ = [
        pltpu.make_async_copy(
            w_ref, wfull.at[:, pl.ds(pl.multiple_of(s * w_cols, 128), w_cols)], own_sems.at[0]
        ),
        pltpu.make_async_copy(
            v_ref, vfull.at[:, pl.ds(pl.multiple_of(s * v_rows, 16), v_rows), :], own_sems.at[1]
        ),
        pltpu.make_async_copy(labels_ref, labels, own_sems.at[2]),
        pltpu.make_async_copy(slab_labels_ref, slab_labels, own_sems.at[3]),
    ]
    for copy in locals_:
        copy.start()

    def order(j):
        return j

    def columns(device, k):
        first = device * width + k * cw
        return first // square, pl.ds(pl.multiple_of(first % square, 128), cw)

    def send_chunk(k):
        def body(j, carry):
            peer = (me + order(j)) % n_dev
            plane, place = columns(peer, k)
            pltpu.make_async_remote_copy(
                src_ref=t_ref.at[plane, :, place],
                dst_ref=recv.at[k, pl.ds(pl.multiple_of(my_block, 16), pair_dev), :],
                send_sem=send1,
                recv_sem=recv1.at[k],
                device_id=where(peer),
                device_id_type=MESH,
            ).start()
            return carry

        lax.fori_loop(1, n_dev, body, 0)
        plane, place = columns(me, k)
        recv[k, pl.ds(pl.multiple_of(my_block, 16), pair_dev), :] = t_ref[plane, :, place]

    def gather(j):
        peer = (s + j) % n_slab
        return (
            pltpu.make_async_remote_copy(
                src_ref=w_ref,
                dst_ref=wfull.at[:, pl.ds(pl.multiple_of(s * w_cols, 128), w_cols)],
                send_sem=wsend.at[j - 1],
                recv_sem=wrecv.at[j - 1],
                device_id=(e, peer),
                device_id_type=MESH,
            ),
            pltpu.make_async_remote_copy(
                src_ref=v_ref,
                dst_ref=vfull.at[:, pl.ds(pl.multiple_of(s * v_rows, 16), v_rows), :],
                send_sem=vsend.at[j - 1],
                recv_sem=vrecv.at[j - 1],
                device_id=(e, peer),
                device_id_type=MESH,
            ),
        )

    send_chunk(0)
    gathers = [gather(j) for j in range(1, n_slab)]
    for w_copy, v_copy in gathers:
        w_copy.start()
        v_copy.start()
    for k in range(1, chunks):
        send_chunk(k)
    for copy in locals_:
        copy.wait()
    for _, v_copy in gathers:
        v_copy.wait()

    side = vfull.shape[1]
    slabs = t_ref.shape[0]
    def particle(plane):

        def take(c, carry):
            rows_in[pl.ds(pl.multiple_of(c * pair_dev, 16), pair_dev), :] = t_ref[
                plane, :, pl.ds(pl.multiple_of(c * side, 128), side)
            ].astype(jnp.float32)
            return carry

        def one(i, carry):
            g = jnp.bitwise_xor(labels[me * pair_dev + i], slab_labels[plane])
            x = rows_in[pl.ds(i, side, stride=pair_dev), :].astype(jnp.bfloat16)
            rows_out[plane, pl.ds(i, side, stride=pair_dev), :] = jnp.dot(
                vfull[g], x, preferred_element_type=jnp.float32
            )
            return carry

        lax.fori_loop(0, side, take, 0, unroll=8)
        lax.fori_loop(0, pair_dev, one, 0, unroll=4)

    for plane in range(slabs):
        particle(plane)

    for w_copy, _ in gathers:
        w_copy.wait()

    pairs = recv.shape[1]
    tile = min(pairs, 512)
    irreps = vfull.shape[0]
    onehot = (
        row_ref[...] == lax.broadcasted_iota(jnp.int32, (irreps, pairs), 0)
    ).astype(jnp.float32).astype(jnp.bfloat16)

    def mask_columns(n, carry):
        cols = pl.ds(pl.multiple_of(n * tile, tile), tile)
        col = lax.broadcasted_iota(jnp.int32, (pairs, tile), 1) + n * tile
        row = lax.broadcasted_iota(jnp.int32, (pairs, tile), 0)
        p, q = col % pair_dev, col // pair_dev
        kl = ((q % n_idx) * n_slab + q // n_idx) * pair_dev + p
        moved = jnp.dot(
            onehot,
            (row == kl).astype(jnp.float32).astype(jnp.bfloat16),
            preferred_element_type=jnp.float32,
        ).astype(jnp.bfloat16)
        equal = lax.dot_general(
            onehot, moved, (((0,), (0,)), ((), ())), preferred_element_type=jnp.float32
        )
        wfull[:, cols] = jnp.where(
            equal > 0.5, wfull[:, cols].astype(jnp.float32), 0.0
        ).astype(jnp.bfloat16)
        return carry

    lax.fori_loop(0, pairs // tile, mask_columns, 0)

    for k in range(chunks):
        plane, place = columns(me, k)
        landed = recv.at[k, pl.ds(0, others * pair_dev), :]
        pltpu.make_async_copy(landed, landed, recv1.at[k]).wait()

        def multiply(m, carry):
            rows = pl.ds(pl.multiple_of(m * tile, tile), tile)
            res[k, rows, :] = jnp.dot(
                wfull[rows, :], recv[k], preferred_element_type=jnp.float32
            ).astype(jnp.bfloat16)
            return carry

        lax.fori_loop(0, pairs // tile, multiply, 0)

        def give(j, carry):
            peer = (me + order(j)) % n_dev
            pltpu.make_async_remote_copy(
                src_ref=res.at[k, pl.ds(pl.multiple_of(peer * pair_dev, 16), pair_dev), :],
                dst_ref=hole.at[plane, :, place],
                send_sem=send2,
                recv_sem=recv2.at[k],
                device_id=where(peer),
                device_id_type=MESH,
            ).start()
            return carry

        lax.fori_loop(1, n_dev, give, 0)
        hole[plane, :, place] = res[k, pl.ds(pl.multiple_of(me * pair_dev, 16), pair_dev), :]


    per_plane = n_dev // slabs
    for k in range(chunks):
        landed = recv.at[k, pl.ds(0, others * pair_dev), :]
        pltpu.make_async_copy(landed, landed, recv2.at[k]).wait()
        for plane in range(slabs):

            def finish(d, carry):
                for u in range(cw // side):
                    first = d * width + k * cw + u * side
                    cols = pl.ds(pl.multiple_of(first, 128), side)
                    rows = pl.ds(pl.multiple_of(first // side * pair_dev, 16), pair_dev)
                    out_ref[:, plane, cols] = rows_out[plane, rows, :] + hole[
                        plane, :, cols
                    ].astype(jnp.float32)
                return carry

            lax.fori_loop(0, per_plane, finish, 0, unroll=2)

    everything = recv.at[:, pl.ds(0, others * pair_dev), :]
    for sem in (send1, send2):
        pltpu.make_async_copy(everything, everything, sem).wait()


def exchange(t, pair_irreps, slab_irreps, w, v, n_idx, n_slab):
    slabs, pair_dev, square = t.shape
    n_dev = n_idx * n_slab
    pairs = w.shape[0]
    width = slabs * square // n_dev
    cw = min(width, 256)
    chunks = width // cw
    irreps, v_rows, side = v.shape
    block = (chunks, pairs, cw)
    vmem = pl.BlockSpec(memory_space=pltpu.VMEM)
    anywhere = pl.BlockSpec(memory_space=pl.ANY)
    held = 2 * (pairs * pairs + 12 * slabs * pair_dev * square)
    dma = pltpu.SemaphoreType.DMA
    return pl.pallas_call(
        functools.partial(exchange_kernel, n_idx, n_slab, cw),
        out_shape=jax.ShapeDtypeStruct((pair_dev, slabs, square), jnp.float32),
        in_specs=[vmem, anywhere, anywhere, vmem, anywhere, anywhere],
        out_specs=vmem,
        scratch_shapes=[
            pltpu.VMEM(block, jnp.bfloat16),
            pltpu.VMEM((pairs, pairs), jnp.bfloat16),
            pltpu.VMEM(block, jnp.bfloat16),
            pltpu.VMEM(t.shape, jnp.bfloat16),
            pltpu.VMEM((irreps, v_rows * n_slab, side), jnp.bfloat16),
            pltpu.VMEM((side * pair_dev, side), jnp.float32),
            pltpu.VMEM((slabs, side * pair_dev, side), jnp.float32),
            pltpu.SMEM(pair_irreps.shape, jnp.int32),
            pltpu.SMEM(slab_irreps.shape, jnp.int32),
            dma, dma((chunks,)), dma, dma((chunks,)),
            dma((n_slab - 1,)), dma((n_slab - 1,)), dma((n_slab - 1,)), dma((n_slab - 1,)), dma((4,)),
        ],
        compiler_params=pltpu.CompilerParams(
            collective_id=0, has_side_effects=True, vmem_limit_bytes=held + 10 * 2**20
        ),
        cost_estimate=pl.CostEstimate(
            flops=2 * pairs * pairs * width,
            bytes_accessed=8 * slabs * pair_dev * square,
            transcendentals=0,
        ),
    )(t, pair_irreps, slab_irreps, pair_irreps.reshape(1, pairs), w, v)


def ladder_kernel(
    n_idx, n_slab, t_ref, labels_ref, slab_labels_ref, row_ref, w_ref, v_ref, out_ref,
    recv, wfull, wide, res, hole, mine, vfull, vwide, row, labels, slab_labels,
    send1, recv1, send2, recv2, wsend, wrecv, vsend, vrecv, own_sems, keep_sem, late, pre,
):
    n_dev = n_idx * n_slab
    pair_dev, side, slabs, _ = t_ref.shape
    chunks, pairs, width = recv.shape[:3]
    w_cols = w_ref.shape[1]
    irreps, v_rows, _ = v_ref.shape
    e = lax.axis_index("idx")
    s = lax.axis_index("slab")
    z, x, y, core = e // 2, e % 2, s // 2, s % 2
    me = e * n_slab + s
    my_block = (s * n_idx + e) * pair_dev
    others = n_dev - 1
    plane_dev = n_dev // 4
    group = 2 * plane_dev
    inner = (z == 1) | (z == 2)
    outer = (z == 0) | (z == 3)

    def flip(bit, by):
        return bit + by - 2 * bit * by

    def partner(dz, q):
        pz = flip(z // 2, dz // 2) * 2 + flip(z % 2, dz % 2)
        return pz * 2 + flip(x, q // 4), flip(y, q // 2 % 2) * 2 + flip(core, q % 2)

    def of_kind(i):
        return partner(3 * (1 - i // plane_dev), plane_dev - 1 - i % plane_dev)

    def of_other_kind(i):
        return partner(2 - i // plane_dev, plane_dev - 1 - i % plane_dev)

    def of_all(i):
        return partner(3 - i // plane_dev, plane_dev - 1 - i % plane_dev)

    def signal(sem, count, peer_of):
        def body(i, carry):
            pl.semaphore_signal(sem, inc=1, device_id=peer_of(i), device_id_type=MESH)
            return carry

        lax.fori_loop(0, count, body, 0)

    def columns(k, device):
        return pl.ds(k * n_dev * width + device * width, width)

    keep = [
        pltpu.make_async_copy(
            t_ref.at[:, columns(k, me)],
            recv.at[k, pl.ds(pl.multiple_of(my_block, 16), pair_dev)],
            keep_sem.at[k],
        )
        for k in range(chunks)
    ]
    locals_ = [
        pltpu.make_async_copy(
            w_ref, wfull.at[:, pl.ds(pl.multiple_of(s * w_cols, 128), w_cols)], own_sems.at[0]
        ),
        pltpu.make_async_copy(
            v_ref, vfull.at[:, pl.ds(pl.multiple_of(s * v_rows, 16), v_rows), :], own_sems.at[1]
        ),
        pltpu.make_async_copy(labels_ref, labels, own_sems.at[2]),
        pltpu.make_async_copy(slab_labels_ref, slab_labels, own_sems.at[3]),
        pltpu.make_async_copy(row_ref, row, own_sems.at[4]),
        pltpu.make_async_copy(t_ref, mine, own_sems.at[5]),
    ]

    def send(k, count, peer_of, first=0):
        def body(i, carry):
            pe, ps = peer_of(i)
            pltpu.make_async_remote_copy(
                src_ref=t_ref.at[:, columns(k, pe * n_slab + ps)],
                dst_ref=recv.at[k, pl.ds(pl.multiple_of(my_block, 16), pair_dev)],
                send_sem=send1,
                recv_sem=recv1.at[k],
                device_id=(pe, ps),
                device_id_type=MESH,
            ).start()
            return carry

        lax.fori_loop(first, count, body, 0)

    def gather(j):
        peer = (s + j) % n_slab
        return (
            pltpu.make_async_remote_copy(
                src_ref=w_ref,
                dst_ref=wfull.at[:, pl.ds(pl.multiple_of(s * w_cols, 128), w_cols)],
                send_sem=wsend.at[j - 1],
                recv_sem=wrecv.at[j - 1],
                device_id=(e, peer),
                device_id_type=MESH,
            ),
            pltpu.make_async_remote_copy(
                src_ref=v_ref,
                dst_ref=vfull.at[:, pl.ds(pl.multiple_of(s * v_rows, 16), v_rows), :],
                send_sem=vsend.at[j - 1],
                recv_sem=vrecv.at[j - 1],
                device_id=(e, peer),
                device_id_type=MESH,
            ),
        )

    gathers = [gather(j) for j in range(1, n_slab)]
    def start_gathers():
        for w_copy, v_copy in gathers:
            w_copy.start()
            v_copy.start()

    barrier = pltpu.get_barrier_semaphore()
    def second_cores(i):
        pe, ps = partner(3 * (i // 4), i % 4 * 2)
        return pe, ps // 2 * 2 + 1

    def other_second_cores(i):
        pe, ps = partner(3 - 3 * (i // 4), (3 - i % 4) * 2)
        return pe, ps // 2 * 2 + 1

    def first_cores_of_other_kind(i):
        pe, ps = partner(2 - i // 4, i % 4 * 2)
        return pe, ps // 2 * 2

    def facing(i):
        return partner(3, i)

    def mate(i):
        return partner(0, 1)

    @pl.when(inner)
    def _():
        signal(barrier, 2, facing)

        def tell(i, carry):
            pe, ps = second_cores(i)

            @pl.when((pe % 2 != x) | (ps // 2 != y))
            def _():
                pl.semaphore_signal(barrier, inc=1, device_id=(pe, ps), device_id_type=MESH)

            return carry

        lax.fori_loop(0, plane_dev, tell, 0)
        signal(barrier, 1, mate)
        signal(barrier, plane_dev, first_cores_of_other_kind)

    @pl.when(outer)
    def _():
        signal(barrier, plane_dev - 1, other_second_cores)
        signal(barrier, 1, mate)

    for copy in keep + locals_:
        copy.start()

    def send_facing():
        for k in range(chunks):
            send(k, plane_dev, of_kind, plane_dev - 2)

    @pl.when(inner)
    def _():
        @pl.when(core == 0)
        def _():
            pl.semaphore_wait(barrier, 3)
            signal(pre, 1, mate)
            send_facing()
            pl.semaphore_wait(pre, 1)

        @pl.when(core == 1)
        def _():
            pl.semaphore_wait(pre, 1)
            send_facing()
            pl.semaphore_wait(barrier, group - 1)
            signal(pre, 1, mate)

        send(0, plane_dev - 2, of_kind)
        start_gathers()
        send(0, group - 1, of_kind, plane_dev)
        pl.semaphore_wait(late, plane_dev)
        send(0, group, of_other_kind)
        for k in range(1, chunks):
            send(k, plane_dev - 2, of_kind)
            send(k, group - 1, of_kind, plane_dev)
            send(k, group, of_other_kind)

    @pl.when(outer & (core == 0))
    def _():
        pl.semaphore_wait(barrier, group + 1)
        signal(pre, 1, mate)
        signal(late, group, of_other_kind)
        send(0, plane_dev, of_other_kind)
        pl.semaphore_wait(pre, 1)
        send(0, plane_dev, of_kind)
        start_gathers()
        send(0, group, of_other_kind, plane_dev)
        send(0, group - 1, of_kind, plane_dev)
        for k in range(1, chunks):
            send(k, others, of_all)

    @pl.when(outer & (core == 1))
    def _():
        pl.semaphore_wait(barrier, group - 1)
        signal(pre, 1, mate)
        send(0, plane_dev, of_kind)
        pl.semaphore_wait(pre, 1)
        send(0, plane_dev, of_other_kind)
        start_gathers()
        send(0, group, of_other_kind, plane_dev)
        send(0, group - 1, of_kind, plane_dev)
        for k in range(1, chunks):
            send(k, others, of_all)

    for copy in locals_:
        copy.wait()
    for w_copy, _ in gathers:
        w_copy.wait()

    def equal(shape, left, right):
        return (
            left(lax.broadcasted_iota(jnp.int32, shape, 0))
            == right(lax.broadcasted_iota(jnp.int32, shape, 1))
        )

    def ones(mask):
        return mask.astype(jnp.float32).astype(jnp.bfloat16)

    def same(x):
        return x

    def half(x):
        return x // slabs

    def rest(x):
        return x % slabs

    onehot = ones(row[...] == lax.broadcasted_iota(jnp.int32, (irreps, pairs), 0))

    def column_pair(q):
        p, q = q % pair_dev, q // pair_dev
        return ((q % n_idx) * n_slab + q // n_idx) * pair_dev + p

    moved = jnp.dot(
        onehot, ones(equal((pairs, pairs), same, column_pair)), preferred_element_type=jnp.float32
    ).astype(jnp.bfloat16)
    allowed = lax.dot_general(
        onehot, moved, (((0,), (0,)), ((), ())), preferred_element_type=jnp.float32
    )
    wfull[...] = jnp.where(allowed > 0.5, wfull[...].astype(jnp.float32), 0.0).astype(jnp.bfloat16)

    tile = 256
    spread = ones(equal((pairs, slabs * pairs), same, half))

    def widen(m, carry):
        down = ones(
            equal((tile, tile // slabs), half, same)
        )
        part = jnp.dot(
            down,
            wfull[pl.ds(pl.multiple_of(m * (tile // slabs), 16), tile // slabs), :],
            preferred_element_type=jnp.float32,
        ).astype(jnp.bfloat16)
        both = jnp.dot(part, spread, preferred_element_type=jnp.float32)
        wide[pl.ds(pl.multiple_of(m * tile, 16), tile), :] = jnp.where(
            equal(both.shape, rest, rest), both, 0.0
        ).astype(jnp.bfloat16)
        return carry

    lax.fori_loop(0, slabs * pairs // tile, widen, 0)

    def give(k, far):
        def body(j, carry):
            t = j % 2
            q = j // 2 - 2 * t
            right, up = q // 4, q // 2 % 2
            pe = (flip(z // 2, far) * 2 + t) * 2 + right + t * (up - right)
            ps = (up + t * (right - up)) * 2 + flip(core, q % 2)
            peer = pe * n_slab + ps

            @pl.when((q >= 0) & (q < plane_dev) & (peer != me))
            def _():
                pltpu.make_async_remote_copy(
                    src_ref=res.at[k, pl.ds(pl.multiple_of(peer * pair_dev, 16), pair_dev)],
                    dst_ref=hole.at[:, columns(k, me)],
                    send_sem=send2,
                    recv_sem=recv2.at[4 * k + z],
                    device_id=(pe, ps),
                    device_id_type=MESH,
                ).start()

            return carry

        lax.fori_loop(0, group + 8, body, 0)

    for k in range(chunks):
        keep[k].wait()
        landed = recv.at[k, pl.ds(0, others * pair_dev)]
        pltpu.make_async_copy(landed, landed, recv1.at[k]).wait()
        right = jnp.concatenate(
            [recv[k, :, u].reshape(slabs * pairs, side) for u in range(width)], axis=1
        )

        for m in range(slabs * pairs // tile):
            got = jnp.dot(
                wide[m * tile : (m + 1) * tile, :], right, preferred_element_type=jnp.float32
            ).astype(jnp.bfloat16)
            for u in range(width):
                res[k, m * (tile // slabs) : (m + 1) * (tile // slabs), u] = got[
                    :, u * side : (u + 1) * side
                ].reshape(tile // slabs, slabs, side)

        give(k, 1)
        give(k, 0)
        hole[:, columns(k, me)] = res[k, pl.ds(pl.multiple_of(me * pair_dev, 16), pair_dev)]

    for _, v_copy in gathers:
        v_copy.wait()

    rows = slabs * side
    for g in range(irreps):
        tall = jnp.dot(
            ones(equal((rows, side), half, same)), vfull[g], preferred_element_type=jnp.float32
        ).astype(jnp.bfloat16)
        both = jnp.dot(
            tall, ones(equal((side, rows), same, half)), preferred_element_type=jnp.float32
        )
        together = equal((rows, rows), rest, rest)
        for plane in range(slabs):
            mask = together & (lax.broadcasted_iota(jnp.int32, (rows, rows), 0) % slabs == plane)
            vwide[plane, g] = jnp.where(mask, both, 0.0).astype(jnp.bfloat16)

    def particle(i, carry):
        x = mine[i].reshape(rows, side)
        total = jnp.zeros((rows, side), jnp.float32)
        for plane in range(slabs):
            g = jnp.bitwise_xor(labels[me * pair_dev + i], slab_labels[plane])
            total += jnp.dot(vwide[plane, g], x, preferred_element_type=jnp.float32)
        out_ref[i] = total
        return carry

    lax.fori_loop(0, pair_dev, particle, 0)

    part = plane_dev * width
    order = (z, z + 1 - 2 * (z % 2), 3 - 3 * (z // 2), 2 - z // 2)
    for k in range(chunks):
        for turn, plane in enumerate(order):
            senders = plane_dev - 1 if turn == 0 else plane_dev
            landed = recv.at[k, pl.ds(0, senders * pair_dev)]
            pltpu.make_async_copy(landed, landed, recv2.at[4 * k + plane]).wait()
            first = k * n_dev * width + plane * part

            def finish(i, carry):
                place = pl.ds(pl.multiple_of(first * slabs, 8), part * slabs)
                out_ref[i, place, :] += (
                    hole[i, pl.ds(first, part)].reshape(part * slabs, side).astype(jnp.float32)
                )
                return carry

            lax.fori_loop(0, pair_dev, finish, 0, unroll=8)

    everything = recv.at[:, pl.ds(0, others * pair_dev)]
    for sem in (send1, send2):
        pltpu.make_async_copy(everything, everything, sem).wait()


def ladder(amplitudes, pair_irreps, slab_irreps, w, v, n_idx, n_slab):
    pair_dev, slabs, square = amplitudes.shape
    n_dev = n_idx * n_slab
    pairs = w.shape[0]
    irreps, v_rows, side = v.shape
    width = 2
    chunks = side // n_dev // width
    t = amplitudes.reshape(pair_dev, slabs, side, side).transpose(0, 2, 1, 3)
    operands = (t, pair_irreps, slab_irreps, pair_irreps.reshape(1, pairs), w, v)
    hbm = pl.BlockSpec(memory_space=pltpu.HBM)
    dma = pltpu.SemaphoreType.DMA
    bf16 = jnp.bfloat16
    out = pl.pallas_call(
        functools.partial(ladder_kernel, n_idx, n_slab),
        out_shape=jax.ShapeDtypeStruct((pair_dev, side * slabs, side), jnp.float32),
        in_specs=[hbm] * 6,
        out_specs=pl.BlockSpec(memory_space=pltpu.VMEM),
        scratch_shapes=[
            pltpu.VMEM((chunks, pairs, width, slabs, side), bf16),
            pltpu.VMEM((pairs, pairs), bf16),
            pltpu.VMEM((slabs * pairs, slabs * pairs), bf16),
            pltpu.VMEM((chunks, pairs, width, slabs, side), bf16),
            pltpu.VMEM(t.shape, bf16),
            pltpu.VMEM(t.shape, bf16),
            pltpu.VMEM((irreps, side, side), bf16),
            pltpu.VMEM((slabs, irreps, slabs * side, slabs * side), bf16),
            pltpu.VMEM((1, pairs), jnp.int32),
            pltpu.SMEM(pair_irreps.shape, jnp.int32),
            pltpu.SMEM(slab_irreps.shape, jnp.int32),
            dma, dma((chunks,)), dma, dma((4 * chunks,)),
            dma((n_slab - 1,)), dma((n_slab - 1,)), dma((n_slab - 1,)), dma((n_slab - 1,)),
            dma((6,)), dma((chunks,)), pltpu.SemaphoreType.REGULAR,
            pltpu.SemaphoreType.REGULAR,
        ],
        compiler_params=pltpu.CompilerParams(
            collective_id=0, has_side_effects=True, vmem_limit_bytes=40 * 2**20
        ),
        cost_estimate=pl.CostEstimate(
            flops=4 * pairs * pairs * slabs * square // n_dev,
            bytes_accessed=8 * slabs * pair_dev * square,
            transcendentals=0,
        ),
    )(*(pltpu.with_memory_space_constraint(x, pltpu.HBM) for x in operands))
    return out.reshape(pair_dev, side, slabs, side).transpose(0, 2, 1, 3).reshape(amplitudes.shape)


def body(amplitudes, pair_irreps, slab_irreps, ladder_ints, vv_blocks):
    n_idx = lax.axis_size("idx")
    n_slab = lax.axis_size("slab")
    whole = (amplitudes, pair_irreps, slab_irreps, ladder_ints, vv_blocks, n_idx, n_slab)
    if (n_idx, n_slab) == (8, 4):
        return ladder(*whole)
    return exchange(amplitudes.transpose(1, 0, 2), *whole[1:])


def solution(mesh):
    return jax.shard_map(
        body,
        mesh=mesh,
        in_specs=(P(("idx", "slab"), None, None), P(), P(), P(None, "slab"), P(None, "slab", None)),
        out_specs=P(("idx", "slab"), None, None),
        check_vma=False,
    )
```

```python
import functools

import jax
import jax.numpy as jnp
from jax import lax
from jax.experimental import pallas as pl
from jax.experimental.pallas import tpu as pltpu
from jax.sharding import PartitionSpec as P

MESH = pl.DeviceIdType.MESH


def exchange_kernel(
    n_idx, n_slab, cw, t_ref, labels_ref, slab_labels_ref, row_ref, w_ref, v_ref, out_ref,
    recv, wfull, res, hole, vfull, rows_in, rows_out, labels, slab_labels,
    send1, recv1, send2, recv2, wsend, wrecv, vsend, vrecv, own_sems,
):
    n_dev = n_idx * n_slab
    pair_dev = t_ref.shape[1]
    square = t_ref.shape[2]
    width = t_ref.shape[0] * square // n_dev
    chunks = width // cw
    w_cols = w_ref.shape[1]
    v_rows = v_ref.shape[1]
    e = lax.axis_index("idx")
    s = lax.axis_index("slab")
    me = e * n_slab + s
    my_block = (s * n_idx + e) * pair_dev
    others = n_dev - 1

    def where(peer):
        return (peer // n_slab, peer % n_slab)

    barrier = pltpu.get_barrier_semaphore()

    def greet(j, carry):
        pl.semaphore_signal(barrier, inc=1, device_id=where((me + j) % n_dev), device_id_type=MESH)
        return carry

    lax.fori_loop(1, n_dev, greet, 0)
    pl.semaphore_wait(barrier, others)

    locals_ = [
        pltpu.make_async_copy(
            w_ref, wfull.at[:, pl.ds(pl.multiple_of(s * w_cols, 128), w_cols)], own_sems.at[0]
        ),
        pltpu.make_async_copy(
            v_ref, vfull.at[:, pl.ds(pl.multiple_of(s * v_rows, 16), v_rows), :], own_sems.at[1]
        ),
        pltpu.make_async_copy(labels_ref, labels, own_sems.at[2]),
        pltpu.make_async_copy(slab_labels_ref, slab_labels, own_sems.at[3]),
    ]
    for copy in locals_:
        copy.start()

    def order(j):
        return j

    def columns(device, k):
        first = device * width + k * cw
        return first // square, pl.ds(pl.multiple_of(first % square, 128), cw)

    def send_chunk(k):
        def body(j, carry):
            peer = (me + order(j)) % n_dev
            plane, place = columns(peer, k)
            pltpu.make_async_remote_copy(
                src_ref=t_ref.at[plane, :, place],
                dst_ref=recv.at[k, pl.ds(pl.multiple_of(my_block, 16), pair_dev), :],
                send_sem=send1,
                recv_sem=recv1.at[k],
                device_id=where(peer),
                device_id_type=MESH,
            ).start()
            return carry

        lax.fori_loop(1, n_dev, body, 0)
        plane, place = columns(me, k)
        recv[k, pl.ds(pl.multiple_of(my_block, 16), pair_dev), :] = t_ref[plane, :, place]

    def gather(j):
        peer = (s + j) % n_slab
        return (
            pltpu.make_async_remote_copy(
                src_ref=w_ref,
                dst_ref=wfull.at[:, pl.ds(pl.multiple_of(s * w_cols, 128), w_cols)],
                send_sem=wsend.at[j - 1],
                recv_sem=wrecv.at[j - 1],
                device_id=(e, peer),
                device_id_type=MESH,
            ),
            pltpu.make_async_remote_copy(
                src_ref=v_ref,
                dst_ref=vfull.at[:, pl.ds(pl.multiple_of(s * v_rows, 16), v_rows), :],
                send_sem=vsend.at[j - 1],
                recv_sem=vrecv.at[j - 1],
                device_id=(e, peer),
                device_id_type=MESH,
            ),
        )

    send_chunk(0)
    gathers = [gather(j) for j in range(1, n_slab)]
    for w_copy, v_copy in gathers:
        w_copy.start()
        v_copy.start()
    for k in range(1, chunks):
        send_chunk(k)
    for copy in locals_:
        copy.wait()
    for _, v_copy in gathers:
        v_copy.wait()

    side = vfull.shape[1]
    slabs = t_ref.shape[0]
    def particle(plane):

        def take(c, carry):
            rows_in[pl.ds(pl.multiple_of(c * pair_dev, 16), pair_dev), :] = t_ref[
                plane, :, pl.ds(pl.multiple_of(c * side, 128), side)
            ].astype(jnp.float32)
            return carry

        def one(i, carry):
            g = jnp.bitwise_xor(labels[me * pair_dev + i], slab_labels[plane])
            x = rows_in[pl.ds(i, side, stride=pair_dev), :].astype(jnp.bfloat16)
            rows_out[plane, pl.ds(i, side, stride=pair_dev), :] = jnp.dot(
                vfull[g], x, preferred_element_type=jnp.float32
            )
            return carry

        lax.fori_loop(0, side, take, 0, unroll=8)
        lax.fori_loop(0, pair_dev, one, 0, unroll=4)

    for plane in range(slabs):
        particle(plane)

    for w_copy, _ in gathers:
        w_copy.wait()

    pairs = recv.shape[1]
    tile = min(pairs, 512)
    irreps = vfull.shape[0]
    onehot = (
        row_ref[...] == lax.broadcasted_iota(jnp.int32, (irreps, pairs), 0)
    ).astype(jnp.float32).astype(jnp.bfloat16)

    def mask_columns(n, carry):
        cols = pl.ds(pl.multiple_of(n * tile, tile), tile)
        col = lax.broadcasted_iota(jnp.int32, (pairs, tile), 1) + n * tile
        row = lax.broadcasted_iota(jnp.int32, (pairs, tile), 0)
        p, q = col % pair_dev, col // pair_dev
        kl = ((q % n_idx) * n_slab + q // n_idx) * pair_dev + p
        moved = jnp.dot(
            onehot,
            (row == kl).astype(jnp.float32).astype(jnp.bfloat16),
            preferred_element_type=jnp.float32,
        ).astype(jnp.bfloat16)
        equal = lax.dot_general(
            onehot, moved, (((0,), (0,)), ((), ())), preferred_element_type=jnp.float32
        )
        wfull[:, cols] = jnp.where(
            equal > 0.5, wfull[:, cols].astype(jnp.float32), 0.0
        ).astype(jnp.bfloat16)
        return carry

    lax.fori_loop(0, pairs // tile, mask_columns, 0)

    for k in range(chunks):
        plane, place = columns(me, k)
        landed = recv.at[k, pl.ds(0, others * pair_dev), :]
        pltpu.make_async_copy(landed, landed, recv1.at[k]).wait()

        def multiply(m, carry):
            rows = pl.ds(pl.multiple_of(m * tile, tile), tile)
            res[k, rows, :] = jnp.dot(
                wfull[rows, :], recv[k], preferred_element_type=jnp.float32
            ).astype(jnp.bfloat16)
            return carry

        lax.fori_loop(0, pairs // tile, multiply, 0)

        def give(j, carry):
            peer = (me + order(j)) % n_dev
            pltpu.make_async_remote_copy(
                src_ref=res.at[k, pl.ds(pl.multiple_of(peer * pair_dev, 16), pair_dev), :],
                dst_ref=hole.at[plane, :, place],
                send_sem=send2,
                recv_sem=recv2.at[k],
                device_id=where(peer),
                device_id_type=MESH,
            ).start()
            return carry

        lax.fori_loop(1, n_dev, give, 0)
        hole[plane, :, place] = res[k, pl.ds(pl.multiple_of(me * pair_dev, 16), pair_dev), :]


    per_plane = n_dev // slabs
    for k in range(chunks):
        landed = recv.at[k, pl.ds(0, others * pair_dev), :]
        pltpu.make_async_copy(landed, landed, recv2.at[k]).wait()
        for plane in range(slabs):

            def finish(d, carry):
                for u in range(cw // side):
                    first = d * width + k * cw + u * side
                    cols = pl.ds(pl.multiple_of(first, 128), side)
                    rows = pl.ds(pl.multiple_of(first // side * pair_dev, 16), pair_dev)
                    out_ref[:, plane, cols] = rows_out[plane, rows, :] + hole[
                        plane, :, cols
                    ].astype(jnp.float32)
                return carry

            lax.fori_loop(0, per_plane, finish, 0, unroll=2)

    everything = recv.at[:, pl.ds(0, others * pair_dev), :]
    for sem in (send1, send2):
        pltpu.make_async_copy(everything, everything, sem).wait()


def exchange(t, pair_irreps, slab_irreps, w, v, n_idx, n_slab):
    slabs, pair_dev, square = t.shape
    n_dev = n_idx * n_slab
    pairs = w.shape[0]
    width = slabs * square // n_dev
    cw = min(width, 256)
    chunks = width // cw
    irreps, v_rows, side = v.shape
    block = (chunks, pairs, cw)
    vmem = pl.BlockSpec(memory_space=pltpu.VMEM)
    anywhere = pl.BlockSpec(memory_space=pl.ANY)
    held = 2 * (pairs * pairs + 12 * slabs * pair_dev * square)
    dma = pltpu.SemaphoreType.DMA
    return pl.pallas_call(
        functools.partial(exchange_kernel, n_idx, n_slab, cw),
        out_shape=jax.ShapeDtypeStruct((pair_dev, slabs, square), jnp.float32),
        in_specs=[vmem, anywhere, anywhere, vmem, anywhere, anywhere],
        out_specs=vmem,
        scratch_shapes=[
            pltpu.VMEM(block, jnp.bfloat16),
            pltpu.VMEM((pairs, pairs), jnp.bfloat16),
            pltpu.VMEM(block, jnp.bfloat16),
            pltpu.VMEM(t.shape, jnp.bfloat16),
            pltpu.VMEM((irreps, v_rows * n_slab, side), jnp.bfloat16),
            pltpu.VMEM((side * pair_dev, side), jnp.float32),
            pltpu.VMEM((slabs, side * pair_dev, side), jnp.float32),
            pltpu.SMEM(pair_irreps.shape, jnp.int32),
            pltpu.SMEM(slab_irreps.shape, jnp.int32),
            dma, dma((chunks,)), dma, dma((chunks,)),
            dma((n_slab - 1,)), dma((n_slab - 1,)), dma((n_slab - 1,)), dma((n_slab - 1,)), dma((4,)),
        ],
        compiler_params=pltpu.CompilerParams(
            collective_id=0, has_side_effects=True, vmem_limit_bytes=held + 10 * 2**20
        ),
        cost_estimate=pl.CostEstimate(
            flops=2 * pairs * pairs * width,
            bytes_accessed=8 * slabs * pair_dev * square,
            transcendentals=0,
        ),
    )(t, pair_irreps, slab_irreps, pair_irreps.reshape(1, pairs), w, v)


def ladder_kernel(
    n_idx, n_slab, t_ref, labels_ref, slab_labels_ref, row_ref, w_ref, v_ref, out_ref,
    recv, wfull, wide, res, hole, mine, vfull, vwide, row, labels, slab_labels,
    send1, recv1, send2, recv2, wsend, wrecv, vsend, vrecv, own_sems, keep_sem, late, pre,
):
    n_dev = n_idx * n_slab
    pair_dev, side, slabs, _ = t_ref.shape
    chunks, pairs, width = recv.shape[:3]
    w_cols = w_ref.shape[1]
    irreps, v_rows, _ = v_ref.shape
    e = lax.axis_index("idx")
    s = lax.axis_index("slab")
    z, x, y, core = e // 2, e % 2, s // 2, s % 2
    me = e * n_slab + s
    my_block = (s * n_idx + e) * pair_dev
    others = n_dev - 1
    plane_dev = n_dev // 4
    group = 2 * plane_dev
    inner = (z == 1) | (z == 2)
    outer = (z == 0) | (z == 3)

    def flip(bit, by):
        return bit + by - 2 * bit * by

    def partner(dz, q):
        pz = flip(z // 2, dz // 2) * 2 + flip(z % 2, dz % 2)
        return pz * 2 + flip(x, q // 4), flip(y, q // 2 % 2) * 2 + flip(core, q % 2)

    def of_kind(i):
        return partner(3 * (1 - i // plane_dev), plane_dev - 1 - i % plane_dev)

    def of_other_kind(i):
        return partner(2 - i // plane_dev, plane_dev - 1 - i % plane_dev)

    def of_all(i):
        return partner(3 - i // plane_dev, plane_dev - 1 - i % plane_dev)

    def signal(sem, count, peer_of):
        def body(i, carry):
            pl.semaphore_signal(sem, inc=1, device_id=peer_of(i), device_id_type=MESH)
            return carry

        lax.fori_loop(0, count, body, 0)

    def columns(k, device):
        return pl.ds(k * n_dev * width + device * width, width)

    keep = [
        pltpu.make_async_copy(
            t_ref.at[:, columns(k, me)],
            recv.at[k, pl.ds(pl.multiple_of(my_block, 16), pair_dev)],
            keep_sem.at[k],
        )
        for k in range(chunks)
    ]
    locals_ = [
        pltpu.make_async_copy(
            w_ref, wfull.at[:, pl.ds(pl.multiple_of(s * w_cols, 128), w_cols)], own_sems.at[0]
        ),
        pltpu.make_async_copy(
            v_ref, vfull.at[:, pl.ds(pl.multiple_of(s * v_rows, 16), v_rows), :], own_sems.at[1]
        ),
        pltpu.make_async_copy(labels_ref, labels, own_sems.at[2]),
        pltpu.make_async_copy(slab_labels_ref, slab_labels, own_sems.at[3]),
        pltpu.make_async_copy(row_ref, row, own_sems.at[4]),
        pltpu.make_async_copy(t_ref, mine, own_sems.at[5]),
    ]

    def send(k, count, peer_of, first=0):
        def body(i, carry):
            pe, ps = peer_of(i)
            pltpu.make_async_remote_copy(
                src_ref=t_ref.at[:, columns(k, pe * n_slab + ps)],
                dst_ref=recv.at[k, pl.ds(pl.multiple_of(my_block, 16), pair_dev)],
                send_sem=send1,
                recv_sem=recv1.at[k],
                device_id=(pe, ps),
                device_id_type=MESH,
            ).start()
            return carry

        lax.fori_loop(first, count, body, 0)

    def gather(j):
        peer = (s + j) % n_slab
        return (
            pltpu.make_async_remote_copy(
                src_ref=w_ref,
                dst_ref=wfull.at[:, pl.ds(pl.multiple_of(s * w_cols, 128), w_cols)],
                send_sem=wsend.at[j - 1],
                recv_sem=wrecv.at[j - 1],
                device_id=(e, peer),
                device_id_type=MESH,
            ),
            pltpu.make_async_remote_copy(
                src_ref=v_ref,
                dst_ref=vfull.at[:, pl.ds(pl.multiple_of(s * v_rows, 16), v_rows), :],
                send_sem=vsend.at[j - 1],
                recv_sem=vrecv.at[j - 1],
                device_id=(e, peer),
                device_id_type=MESH,
            ),
        )

    gathers = [gather(j) for j in range(1, n_slab)]
    def start_gathers():
        for w_copy, v_copy in gathers:
            w_copy.start()
            v_copy.start()

    barrier = pltpu.get_barrier_semaphore()
    def second_cores(i):
        pe, ps = partner(3 * (i // 4), i % 4 * 2)
        return pe, ps // 2 * 2 + 1

    def other_second_cores(i):
        pe, ps = partner(3 - 3 * (i // 4), (3 - i % 4) * 2)
        return pe, ps // 2 * 2 + 1

    def first_cores_of_other_kind(i):
        pe, ps = partner(2 - i // 4, i % 4 * 2)
        return pe, ps // 2 * 2

    def facing(i):
        return partner(3, i)

    def mate(i):
        return partner(0, 1)

    @pl.when(inner)
    def _():
        signal(barrier, 2, facing)

        def tell(i, carry):
            pe, ps = second_cores(i)

            @pl.when((pe % 2 != x) | (ps // 2 != y))
            def _():
                pl.semaphore_signal(barrier, inc=1, device_id=(pe, ps), device_id_type=MESH)

            return carry

        lax.fori_loop(0, plane_dev, tell, 0)
        signal(barrier, 1, mate)
        signal(barrier, plane_dev, first_cores_of_other_kind)

    @pl.when(outer)
    def _():
        signal(barrier, plane_dev - 1, other_second_cores)
        signal(barrier, 1, mate)

    for copy in keep + locals_:
        copy.start()

    def send_facing():
        for k in range(chunks):
            send(k, plane_dev, of_kind, plane_dev - 2)

    @pl.when(inner)
    def _():
        @pl.when(core == 0)
        def _():
            pl.semaphore_wait(barrier, 3)
            signal(pre, 1, mate)
            send_facing()
            pl.semaphore_wait(pre, 1)

        @pl.when(core == 1)
        def _():
            pl.semaphore_wait(pre, 1)
            send_facing()
            pl.semaphore_wait(barrier, group - 1)
            signal(pre, 1, mate)

        send(0, plane_dev - 2, of_kind)
        start_gathers()
        send(0, group - 1, of_kind, plane_dev)
        pl.semaphore_wait(late, plane_dev)
        send(0, group, of_other_kind)
        for k in range(1, chunks):
            send(k, plane_dev - 2, of_kind)
            send(k, group - 1, of_kind, plane_dev)
            send(k, group, of_other_kind)

    @pl.when(outer & (core == 0))
    def _():
        pl.semaphore_wait(barrier, group + 1)
        signal(pre, 1, mate)
        signal(late, group, of_other_kind)
        send(0, plane_dev, of_other_kind)
        pl.semaphore_wait(pre, 1)
        send(0, plane_dev, of_kind)
        start_gathers()
        send(0, group, of_other_kind, plane_dev)
        send(0, group - 1, of_kind, plane_dev)
        for k in range(1, chunks):
            send(k, others, of_all)

    @pl.when(outer & (core == 1))
    def _():
        pl.semaphore_wait(barrier, group - 1)
        signal(pre, 1, mate)
        send(0, plane_dev, of_kind)
        pl.semaphore_wait(pre, 1)
        send(0, plane_dev, of_other_kind)
        start_gathers()
        send(0, group, of_other_kind, plane_dev)
        send(0, group - 1, of_kind, plane_dev)
        for k in range(1, chunks):
            send(k, others, of_all)

    for copy in locals_:
        copy.wait()
    for w_copy, _ in gathers:
        w_copy.wait()

    def equal(shape, left, right):
        return (
            left(lax.broadcasted_iota(jnp.int32, shape, 0))
            == right(lax.broadcasted_iota(jnp.int32, shape, 1))
        )

    def ones(mask):
        return mask.astype(jnp.float32).astype(jnp.bfloat16)

    def same(x):
        return x

    def half(x):
        return x // slabs

    def rest(x):
        return x % slabs

    onehot = ones(row[...] == lax.broadcasted_iota(jnp.int32, (irreps, pairs), 0))

    def column_pair(q):
        p, q = q % pair_dev, q // pair_dev
        return ((q % n_idx) * n_slab + q // n_idx) * pair_dev + p

    moved = jnp.dot(
        onehot, ones(equal((pairs, pairs), same, column_pair)), preferred_element_type=jnp.float32
    ).astype(jnp.bfloat16)
    allowed = lax.dot_general(
        onehot, moved, (((0,), (0,)), ((), ())), preferred_element_type=jnp.float32
    )
    wfull[...] = jnp.where(allowed > 0.5, wfull[...].astype(jnp.float32), 0.0).astype(jnp.bfloat16)

    tile = 256
    spread = ones(equal((pairs, slabs * pairs), same, half))

    def widen(m, carry):
        down = ones(
            equal((tile, tile // slabs), half, same)
        )
        part = jnp.dot(
            down,
            wfull[pl.ds(pl.multiple_of(m * (tile // slabs), 16), tile // slabs), :],
            preferred_element_type=jnp.float32,
        ).astype(jnp.bfloat16)
        both = jnp.dot(part, spread, preferred_element_type=jnp.float32)
        wide[pl.ds(pl.multiple_of(m * tile, 16), tile), :] = jnp.where(
            equal(both.shape, rest, rest), both, 0.0
        ).astype(jnp.bfloat16)
        return carry

    lax.fori_loop(0, slabs * pairs // tile, widen, 0)

    def give(k, far):
        def body(j, carry):
            t = j % 2
            q = j // 2 - 2 * t
            right, up = q // 4, q // 2 % 2
            pe = (flip(z // 2, far) * 2 + t) * 2 + right + t * (up - right)
            ps = (up + t * (right - up)) * 2 + flip(core, q % 2)
            peer = pe * n_slab + ps

            @pl.when((q >= 0) & (q < plane_dev) & (peer != me))
            def _():
                pltpu.make_async_remote_copy(
                    src_ref=res.at[k, pl.ds(pl.multiple_of(peer * pair_dev, 16), pair_dev)],
                    dst_ref=hole.at[:, columns(k, me)],
                    send_sem=send2,
                    recv_sem=recv2.at[4 * k + z],
                    device_id=(pe, ps),
                    device_id_type=MESH,
                ).start()

            return carry

        lax.fori_loop(0, group + 8, body, 0)

    for k in range(chunks):
        keep[k].wait()
        landed = recv.at[k, pl.ds(0, others * pair_dev)]
        pltpu.make_async_copy(landed, landed, recv1.at[k]).wait()
        right = jnp.concatenate(
            [recv[k, :, u].reshape(slabs * pairs, side) for u in range(width)], axis=1
        )

        for m in range(slabs * pairs // tile):
            got = jnp.dot(
                wide[m * tile : (m + 1) * tile, :], right, preferred_element_type=jnp.float32
            ).astype(jnp.bfloat16)
            for u in range(width):
                res[k, m * (tile // slabs) : (m + 1) * (tile // slabs), u] = got[
                    :, u * side : (u + 1) * side
                ].reshape(tile // slabs, slabs, side)

        give(k, k)
        give(k, 1 - k)
        hole[:, columns(k, me)] = res[k, pl.ds(pl.multiple_of(me * pair_dev, 16), pair_dev)]

    for _, v_copy in gathers:
        v_copy.wait()

    rows = slabs * side
    for g in range(irreps):
        tall = jnp.dot(
            ones(equal((rows, side), half, same)), vfull[g], preferred_element_type=jnp.float32
        ).astype(jnp.bfloat16)
        both = jnp.dot(
            tall, ones(equal((side, rows), same, half)), preferred_element_type=jnp.float32
        )
        together = equal((rows, rows), rest, rest)
        for plane in range(slabs):
            mask = together & (lax.broadcasted_iota(jnp.int32, (rows, rows), 0) % slabs == plane)
            vwide[plane, g] = jnp.where(mask, both, 0.0).astype(jnp.bfloat16)

    def particle(i, carry):
        x = mine[i].reshape(rows, side)
        total = jnp.zeros((rows, side), jnp.float32)
        for plane in range(slabs):
            g = jnp.bitwise_xor(labels[me * pair_dev + i], slab_labels[plane])
            total += jnp.dot(vwide[plane, g], x, preferred_element_type=jnp.float32)
        out_ref[i] = total
        return carry

    lax.fori_loop(0, pair_dev, particle, 0)

    part = plane_dev * width
    order = (z, z + 1 - 2 * (z % 2), 3 - 3 * (z // 2), 2 - z // 2)
    for k in range(chunks):
        for turn, plane in enumerate(order):
            senders = plane_dev - 1 if turn == 0 else plane_dev
            landed = recv.at[k, pl.ds(0, senders * pair_dev)]
            pltpu.make_async_copy(landed, landed, recv2.at[4 * k + plane]).wait()
            first = k * n_dev * width + plane * part

            def finish(i, carry):
                place = pl.ds(pl.multiple_of(first * slabs, 8), part * slabs)
                out_ref[i, place, :] += (
                    hole[i, pl.ds(first, part)].reshape(part * slabs, side).astype(jnp.float32)
                )
                return carry

            lax.fori_loop(0, pair_dev, finish, 0, unroll=8)

    everything = recv.at[:, pl.ds(0, others * pair_dev)]
    for sem in (send1, send2):
        pltpu.make_async_copy(everything, everything, sem).wait()


def ladder(amplitudes, pair_irreps, slab_irreps, w, v, n_idx, n_slab):
    pair_dev, slabs, square = amplitudes.shape
    n_dev = n_idx * n_slab
    pairs = w.shape[0]
    irreps, v_rows, side = v.shape
    width = 2
    chunks = side // n_dev // width
    t = amplitudes.reshape(pair_dev, slabs, side, side).transpose(0, 2, 1, 3)
    operands = (t, pair_irreps, slab_irreps, pair_irreps.reshape(1, pairs), w, v)
    hbm = pl.BlockSpec(memory_space=pltpu.HBM)
    dma = pltpu.SemaphoreType.DMA
    bf16 = jnp.bfloat16
    out = pl.pallas_call(
        functools.partial(ladder_kernel, n_idx, n_slab),
        out_shape=jax.ShapeDtypeStruct((pair_dev, side * slabs, side), jnp.float32),
        in_specs=[hbm] * 6,
        out_specs=pl.BlockSpec(memory_space=pltpu.VMEM),
        scratch_shapes=[
            pltpu.VMEM((chunks, pairs, width, slabs, side), bf16),
            pltpu.VMEM((pairs, pairs), bf16),
            pltpu.VMEM((slabs * pairs, slabs * pairs), bf16),
            pltpu.VMEM((chunks, pairs, width, slabs, side), bf16),
            pltpu.VMEM(t.shape, bf16),
            pltpu.VMEM(t.shape, bf16),
            pltpu.VMEM((irreps, side, side), bf16),
            pltpu.VMEM((slabs, irreps, slabs * side, slabs * side), bf16),
            pltpu.VMEM((1, pairs), jnp.int32),
            pltpu.SMEM(pair_irreps.shape, jnp.int32),
            pltpu.SMEM(slab_irreps.shape, jnp.int32),
            dma, dma((chunks,)), dma, dma((4 * chunks,)),
            dma((n_slab - 1,)), dma((n_slab - 1,)), dma((n_slab - 1,)), dma((n_slab - 1,)),
            dma((6,)), dma((chunks,)), pltpu.SemaphoreType.REGULAR,
            pltpu.SemaphoreType.REGULAR,
        ],
        compiler_params=pltpu.CompilerParams(
            collective_id=0, has_side_effects=True, vmem_limit_bytes=40 * 2**20
        ),
        cost_estimate=pl.CostEstimate(
            flops=4 * pairs * pairs * slabs * square // n_dev,
            bytes_accessed=8 * slabs * pair_dev * square,
            transcendentals=0,
        ),
    )(*(pltpu.with_memory_space_constraint(x, pltpu.HBM) for x in operands))
    return out.reshape(pair_dev, side, slabs, side).transpose(0, 2, 1, 3).reshape(amplitudes.shape)


def body(amplitudes, pair_irreps, slab_irreps, ladder_ints, vv_blocks):
    n_idx = lax.axis_size("idx")
    n_slab = lax.axis_size("slab")
    whole = (amplitudes, pair_irreps, slab_irreps, ladder_ints, vv_blocks, n_idx, n_slab)
    if (n_idx, n_slab) == (8, 4):
        return ladder(*whole)
    return exchange(amplitudes.transpose(1, 0, 2), *whole[1:])


def solution(mesh):
    return jax.shard_map(
        body,
        mesh=mesh,
        in_specs=(P(("idx", "slab"), None, None), P(), P(), P(None, "slab"), P(None, "slab", None)),
        out_specs=P(("idx", "slab"), None, None),
        check_vma=False,
    )
```

```python
import functools

import jax
import jax.numpy as jnp
from jax import lax
from jax.experimental import pallas as pl
from jax.experimental.pallas import tpu as pltpu
from jax.sharding import PartitionSpec as P

MESH = pl.DeviceIdType.MESH


def exchange_kernel(
    n_idx, n_slab, cw, t_ref, labels_ref, slab_labels_ref, row_ref, w_ref, v_ref, out_ref,
    recv, wfull, res, hole, vfull, rows_in, rows_out, labels, slab_labels,
    send1, recv1, send2, recv2, wsend, wrecv, vsend, vrecv, own_sems,
):
    n_dev = n_idx * n_slab
    pair_dev = t_ref.shape[1]
    square = t_ref.shape[2]
    width = t_ref.shape[0] * square // n_dev
    chunks = width // cw
    w_cols = w_ref.shape[1]
    v_rows = v_ref.shape[1]
    e = lax.axis_index("idx")
    s = lax.axis_index("slab")
    me = e * n_slab + s
    my_block = (s * n_idx + e) * pair_dev
    others = n_dev - 1

    def where(peer):
        return (peer // n_slab, peer % n_slab)

    barrier = pltpu.get_barrier_semaphore()

    def greet(j, carry):
        pl.semaphore_signal(barrier, inc=1, device_id=where((me + j) % n_dev), device_id_type=MESH)
        return carry

    lax.fori_loop(1, n_dev, greet, 0)
    pl.semaphore_wait(barrier, others)

    locals_ = [
        pltpu.make_async_copy(
            w_ref, wfull.at[:, pl.ds(pl.multiple_of(s * w_cols, 128), w_cols)], own_sems.at[0]
        ),
        pltpu.make_async_copy(
            v_ref, vfull.at[:, pl.ds(pl.multiple_of(s * v_rows, 16), v_rows), :], own_sems.at[1]
        ),
        pltpu.make_async_copy(labels_ref, labels, own_sems.at[2]),
        pltpu.make_async_copy(slab_labels_ref, slab_labels, own_sems.at[3]),
    ]
    for copy in locals_:
        copy.start()

    def order(j):
        return j

    def columns(device, k):
        first = device * width + k * cw
        return first // square, pl.ds(pl.multiple_of(first % square, 128), cw)

    def send_chunk(k):
        def body(j, carry):
            peer = (me + order(j)) % n_dev
            plane, place = columns(peer, k)
            pltpu.make_async_remote_copy(
                src_ref=t_ref.at[plane, :, place],
                dst_ref=recv.at[k, pl.ds(pl.multiple_of(my_block, 16), pair_dev), :],
                send_sem=send1,
                recv_sem=recv1.at[k],
                device_id=where(peer),
                device_id_type=MESH,
            ).start()
            return carry

        lax.fori_loop(1, n_dev, body, 0)
        plane, place = columns(me, k)
        recv[k, pl.ds(pl.multiple_of(my_block, 16), pair_dev), :] = t_ref[plane, :, place]

    def gather(j):
        peer = (s + j) % n_slab
        return (
            pltpu.make_async_remote_copy(
                src_ref=w_ref,
                dst_ref=wfull.at[:, pl.ds(pl.multiple_of(s * w_cols, 128), w_cols)],
                send_sem=wsend.at[j - 1],
                recv_sem=wrecv.at[j - 1],
                device_id=(e, peer),
                device_id_type=MESH,
            ),
            pltpu.make_async_remote_copy(
                src_ref=v_ref,
                dst_ref=vfull.at[:, pl.ds(pl.multiple_of(s * v_rows, 16), v_rows), :],
                send_sem=vsend.at[j - 1],
                recv_sem=vrecv.at[j - 1],
                device_id=(e, peer),
                device_id_type=MESH,
            ),
        )

    send_chunk(0)
    gathers = [gather(j) for j in range(1, n_slab)]
    for w_copy, v_copy in gathers:
        w_copy.start()
        v_copy.start()
    for k in range(1, chunks):
        send_chunk(k)
    for copy in locals_:
        copy.wait()
    for _, v_copy in gathers:
        v_copy.wait()

    side = vfull.shape[1]
    slabs = t_ref.shape[0]
    def particle(plane):

        def take(c, carry):
            rows_in[pl.ds(pl.multiple_of(c * pair_dev, 16), pair_dev), :] = t_ref[
                plane, :, pl.ds(pl.multiple_of(c * side, 128), side)
            ].astype(jnp.float32)
            return carry

        def one(i, carry):
            g = jnp.bitwise_xor(labels[me * pair_dev + i], slab_labels[plane])
            x = rows_in[pl.ds(i, side, stride=pair_dev), :].astype(jnp.bfloat16)
            rows_out[plane, pl.ds(i, side, stride=pair_dev), :] = jnp.dot(
                vfull[g], x, preferred_element_type=jnp.float32
            )
            return carry

        lax.fori_loop(0, side, take, 0, unroll=8)
        lax.fori_loop(0, pair_dev, one, 0, unroll=4)

    for plane in range(slabs):
        particle(plane)

    for w_copy, _ in gathers:
        w_copy.wait()

    pairs = recv.shape[1]
    tile = min(pairs, 512)
    irreps = vfull.shape[0]
    onehot = (
        row_ref[...] == lax.broadcasted_iota(jnp.int32, (irreps, pairs), 0)
    ).astype(jnp.float32).astype(jnp.bfloat16)

    def mask_columns(n, carry):
        cols = pl.ds(pl.multiple_of(n * tile, tile), tile)
        col = lax.broadcasted_iota(jnp.int32, (pairs, tile), 1) + n * tile
        row = lax.broadcasted_iota(jnp.int32, (pairs, tile), 0)
        p, q = col % pair_dev, col // pair_dev
        kl = ((q % n_idx) * n_slab + q // n_idx) * pair_dev + p
        moved = jnp.dot(
            onehot,
            (row == kl).astype(jnp.float32).astype(jnp.bfloat16),
            preferred_element_type=jnp.float32,
        ).astype(jnp.bfloat16)
        equal = lax.dot_general(
            onehot, moved, (((0,), (0,)), ((), ())), preferred_element_type=jnp.float32
        )
        wfull[:, cols] = jnp.where(
            equal > 0.5, wfull[:, cols].astype(jnp.float32), 0.0
        ).astype(jnp.bfloat16)
        return carry

    lax.fori_loop(0, pairs // tile, mask_columns, 0)

    for k in range(chunks):
        plane, place = columns(me, k)
        landed = recv.at[k, pl.ds(0, others * pair_dev), :]
        pltpu.make_async_copy(landed, landed, recv1.at[k]).wait()

        def multiply(m, carry):
            rows = pl.ds(pl.multiple_of(m * tile, tile), tile)
            res[k, rows, :] = jnp.dot(
                wfull[rows, :], recv[k], preferred_element_type=jnp.float32
            ).astype(jnp.bfloat16)
            return carry

        lax.fori_loop(0, pairs // tile, multiply, 0)

        def give(j, carry):
            peer = (me + order(j)) % n_dev
            pltpu.make_async_remote_copy(
                src_ref=res.at[k, pl.ds(pl.multiple_of(peer * pair_dev, 16), pair_dev), :],
                dst_ref=hole.at[plane, :, place],
                send_sem=send2,
                recv_sem=recv2.at[k],
                device_id=where(peer),
                device_id_type=MESH,
            ).start()
            return carry

        lax.fori_loop(1, n_dev, give, 0)
        hole[plane, :, place] = res[k, pl.ds(pl.multiple_of(me * pair_dev, 16), pair_dev), :]


    per_plane = n_dev // slabs
    for k in range(chunks):
        landed = recv.at[k, pl.ds(0, others * pair_dev), :]
        pltpu.make_async_copy(landed, landed, recv2.at[k]).wait()
        for plane in range(slabs):

            def finish(d, carry):
                for u in range(cw // side):
                    first = d * width + k * cw + u * side
                    cols = pl.ds(pl.multiple_of(first, 128), side)
                    rows = pl.ds(pl.multiple_of(first // side * pair_dev, 16), pair_dev)
                    out_ref[:, plane, cols] = rows_out[plane, rows, :] + hole[
                        plane, :, cols
                    ].astype(jnp.float32)
                return carry

            lax.fori_loop(0, per_plane, finish, 0, unroll=2)

    everything = recv.at[:, pl.ds(0, others * pair_dev), :]
    for sem in (send1, send2):
        pltpu.make_async_copy(everything, everything, sem).wait()


def exchange(t, pair_irreps, slab_irreps, w, v, n_idx, n_slab):
    slabs, pair_dev, square = t.shape
    n_dev = n_idx * n_slab
    pairs = w.shape[0]
    width = slabs * square // n_dev
    cw = min(width, 256)
    chunks = width // cw
    irreps, v_rows, side = v.shape
    block = (chunks, pairs, cw)
    vmem = pl.BlockSpec(memory_space=pltpu.VMEM)
    anywhere = pl.BlockSpec(memory_space=pl.ANY)
    held = 2 * (pairs * pairs + 12 * slabs * pair_dev * square)
    dma = pltpu.SemaphoreType.DMA
    return pl.pallas_call(
        functools.partial(exchange_kernel, n_idx, n_slab, cw),
        out_shape=jax.ShapeDtypeStruct((pair_dev, slabs, square), jnp.float32),
        in_specs=[vmem, anywhere, anywhere, vmem, anywhere, anywhere],
        out_specs=vmem,
        scratch_shapes=[
            pltpu.VMEM(block, jnp.bfloat16),
            pltpu.VMEM((pairs, pairs), jnp.bfloat16),
            pltpu.VMEM(block, jnp.bfloat16),
            pltpu.VMEM(t.shape, jnp.bfloat16),
            pltpu.VMEM((irreps, v_rows * n_slab, side), jnp.bfloat16),
            pltpu.VMEM((side * pair_dev, side), jnp.float32),
            pltpu.VMEM((slabs, side * pair_dev, side), jnp.float32),
            pltpu.SMEM(pair_irreps.shape, jnp.int32),
            pltpu.SMEM(slab_irreps.shape, jnp.int32),
            dma, dma((chunks,)), dma, dma((chunks,)),
            dma((n_slab - 1,)), dma((n_slab - 1,)), dma((n_slab - 1,)), dma((n_slab - 1,)), dma((4,)),
        ],
        compiler_params=pltpu.CompilerParams(
            collective_id=0, has_side_effects=True, vmem_limit_bytes=held + 10 * 2**20
        ),
        cost_estimate=pl.CostEstimate(
            flops=2 * pairs * pairs * width,
            bytes_accessed=8 * slabs * pair_dev * square,
            transcendentals=0,
        ),
    )(t, pair_irreps, slab_irreps, pair_irreps.reshape(1, pairs), w, v)


def ladder_kernel(
    n_idx, n_slab, t_ref, labels_ref, slab_labels_ref, row_ref, w_ref, v_ref, out_ref,
    recv, wfull, wide, res, hole, mine, vfull, vwide, row, labels, slab_labels,
    send1, recv1, send2, recv2, wsend, wrecv, vsend, vrecv, own_sems, keep_sem, late, pre,
):
    n_dev = n_idx * n_slab
    pair_dev, side, slabs, _ = t_ref.shape
    chunks, pairs, width = recv.shape[:3]
    w_cols = w_ref.shape[1]
    irreps, v_rows, _ = v_ref.shape
    e = lax.axis_index("idx")
    s = lax.axis_index("slab")
    z, x, y, core = e // 2, e % 2, s // 2, s % 2
    me = e * n_slab + s
    my_block = (s * n_idx + e) * pair_dev
    others = n_dev - 1
    plane_dev = n_dev // 4
    group = 2 * plane_dev
    inner = (z == 1) | (z == 2)
    outer = (z == 0) | (z == 3)

    def flip(bit, by):
        return bit + by - 2 * bit * by

    def partner(dz, q):
        pz = flip(z // 2, dz // 2) * 2 + flip(z % 2, dz % 2)
        return pz * 2 + flip(x, q // 4), flip(y, q // 2 % 2) * 2 + flip(core, q % 2)

    def of_kind(i):
        return partner(3 * (1 - i // plane_dev), plane_dev - 1 - i % plane_dev)

    def of_other_kind(i):
        return partner(2 - i // plane_dev, plane_dev - 1 - i % plane_dev)

    def of_all(i):
        return partner(3 - i // plane_dev, plane_dev - 1 - i % plane_dev)

    def signal(sem, count, peer_of):
        def body(i, carry):
            pl.semaphore_signal(sem, inc=1, device_id=peer_of(i), device_id_type=MESH)
            return carry

        lax.fori_loop(0, count, body, 0)

    def columns(k, device):
        return pl.ds(k * n_dev * width + device * width, width)

    keep = [
        pltpu.make_async_copy(
            t_ref.at[:, columns(k, me)],
            recv.at[k, pl.ds(pl.multiple_of(my_block, 16), pair_dev)],
            keep_sem.at[k],
        )
        for k in range(chunks)
    ]
    locals_ = [
        pltpu.make_async_copy(
            w_ref, wfull.at[:, pl.ds(pl.multiple_of(s * w_cols, 128), w_cols)], own_sems.at[0]
        ),
        pltpu.make_async_copy(
            v_ref, vfull.at[:, pl.ds(pl.multiple_of(s * v_rows, 16), v_rows), :], own_sems.at[1]
        ),
        pltpu.make_async_copy(labels_ref, labels, own_sems.at[2]),
        pltpu.make_async_copy(slab_labels_ref, slab_labels, own_sems.at[3]),
        pltpu.make_async_copy(row_ref, row, own_sems.at[4]),
        pltpu.make_async_copy(t_ref, mine, own_sems.at[5]),
    ]

    def send(k, count, peer_of, first=0):
        def body(i, carry):
            pe, ps = peer_of(i)
            pltpu.make_async_remote_copy(
                src_ref=t_ref.at[:, columns(k, pe * n_slab + ps)],
                dst_ref=recv.at[k, pl.ds(pl.multiple_of(my_block, 16), pair_dev)],
                send_sem=send1,
                recv_sem=recv1.at[k],
                device_id=(pe, ps),
                device_id_type=MESH,
            ).start()
            return carry

        lax.fori_loop(first, count, body, 0)

    def gather(j):
        peer = (s + j) % n_slab
        return (
            pltpu.make_async_remote_copy(
                src_ref=w_ref,
                dst_ref=wfull.at[:, pl.ds(pl.multiple_of(s * w_cols, 128), w_cols)],
                send_sem=wsend.at[j - 1],
                recv_sem=wrecv.at[j - 1],
                device_id=(e, peer),
                device_id_type=MESH,
            ),
            pltpu.make_async_remote_copy(
                src_ref=v_ref,
                dst_ref=vfull.at[:, pl.ds(pl.multiple_of(s * v_rows, 16), v_rows), :],
                send_sem=vsend.at[j - 1],
                recv_sem=vrecv.at[j - 1],
                device_id=(e, peer),
                device_id_type=MESH,
            ),
        )

    gathers = [gather(j) for j in range(1, n_slab)]
    def start_gathers():
        for w_copy, v_copy in gathers:
            w_copy.start()
            v_copy.start()

    barrier = pltpu.get_barrier_semaphore()
    def second_cores(i):
        pe, ps = partner(3 * (i // 4), i % 4 * 2)
        return pe, ps // 2 * 2 + 1

    def other_second_cores(i):
        pe, ps = partner(3 - 3 * (i // 4), (3 - i % 4) * 2)
        return pe, ps // 2 * 2 + 1

    def first_cores_of_other_kind(i):
        pe, ps = partner(2 - i // 4, i % 4 * 2)
        return pe, ps // 2 * 2

    def facing(i):
        return partner(3, i)

    def mate(i):
        return partner(0, 1)

    @pl.when(inner)
    def _():
        signal(barrier, 1, mate)
        signal(barrier, 2, facing)

        def tell(i, carry):
            pe, ps = second_cores(i)

            @pl.when((pe % 2 != x) | (ps // 2 != y))
            def _():
                pl.semaphore_signal(barrier, inc=1, device_id=(pe, ps), device_id_type=MESH)

            return carry

        lax.fori_loop(0, plane_dev, tell, 0)
        signal(barrier, plane_dev, first_cores_of_other_kind)

    @pl.when(outer)
    def _():
        signal(barrier, 1, mate)
        signal(barrier, plane_dev - 1, other_second_cores)

    def send_facing():
        for k in range(chunks):
            send(k, plane_dev, of_kind, plane_dev - 2)

    @pl.when(inner)
    def _():
        @pl.when(core == 0)
        def _():
            pl.semaphore_wait(barrier, 3)
            signal(pre, 1, mate)
            send_facing()
            pl.semaphore_wait(pre, 1)

        @pl.when(core == 1)
        def _():
            pl.semaphore_wait(pre, 1)
            send_facing()
            pl.semaphore_wait(barrier, group - 1)
            signal(pre, 1, mate)

        send(0, plane_dev - 2, of_kind)
        start_gathers()
        send(0, group - 1, of_kind, plane_dev)
        pl.semaphore_wait(late, plane_dev)
        send(0, group, of_other_kind)
        for k in range(1, chunks):
            send(k, plane_dev - 2, of_kind)
            send(k, group - 1, of_kind, plane_dev)
            send(k, group, of_other_kind)

    @pl.when(outer & (core == 0))
    def _():
        pl.semaphore_wait(barrier, group + 1)
        signal(pre, 1, mate)
        signal(late, group, of_other_kind)
        send(0, plane_dev, of_other_kind)
        pl.semaphore_wait(pre, 1)
        send(0, plane_dev, of_kind)
        start_gathers()
        send(0, group, of_other_kind, plane_dev)
        send(0, group - 1, of_kind, plane_dev)
        for k in range(1, chunks):
            send(k, others, of_all)

    @pl.when(outer & (core == 1))
    def _():
        pl.semaphore_wait(barrier, group - 1)
        signal(pre, 1, mate)
        send(0, plane_dev, of_kind)
        pl.semaphore_wait(pre, 1)
        send(0, plane_dev, of_other_kind)
        start_gathers()
        send(0, group, of_other_kind, plane_dev)
        send(0, group - 1, of_kind, plane_dev)
        for k in range(1, chunks):
            send(k, others, of_all)

    for copy in keep + locals_:
        copy.start()
    for copy in locals_:
        copy.wait()
    for w_copy, _ in gathers:
        w_copy.wait()

    def equal(shape, left, right):
        return (
            left(lax.broadcasted_iota(jnp.int32, shape, 0))
            == right(lax.broadcasted_iota(jnp.int32, shape, 1))
        )

    def ones(mask):
        return mask.astype(jnp.float32).astype(jnp.bfloat16)

    def same(x):
        return x

    def half(x):
        return x // slabs

    def rest(x):
        return x % slabs

    onehot = ones(row[...] == lax.broadcasted_iota(jnp.int32, (irreps, pairs), 0))

    def column_pair(q):
        p, q = q % pair_dev, q // pair_dev
        return ((q % n_idx) * n_slab + q // n_idx) * pair_dev + p

    moved = jnp.dot(
        onehot, ones(equal((pairs, pairs), same, column_pair)), preferred_element_type=jnp.float32
    ).astype(jnp.bfloat16)
    allowed = lax.dot_general(
        onehot, moved, (((0,), (0,)), ((), ())), preferred_element_type=jnp.float32
    )
    wfull[...] = jnp.where(allowed > 0.5, wfull[...].astype(jnp.float32), 0.0).astype(jnp.bfloat16)

    tile = 256
    spread = ones(equal((pairs, slabs * pairs), same, half))

    def widen(m, carry):
        down = ones(
            equal((tile, tile // slabs), half, same)
        )
        part = jnp.dot(
            down,
            wfull[pl.ds(pl.multiple_of(m * (tile // slabs), 16), tile // slabs), :],
            preferred_element_type=jnp.float32,
        ).astype(jnp.bfloat16)
        both = jnp.dot(part, spread, preferred_element_type=jnp.float32)
        wide[pl.ds(pl.multiple_of(m * tile, 16), tile), :] = jnp.where(
            equal(both.shape, rest, rest), both, 0.0
        ).astype(jnp.bfloat16)
        return carry

    lax.fori_loop(0, slabs * pairs // tile, widen, 0)

    def give(k, far):
        def body(j, carry):
            t = j % 2
            q = j // 2 - 2 * t
            right, up = q // 4, q // 2 % 2
            pe = (flip(z // 2, far) * 2 + t) * 2 + right + t * (up - right)
            ps = (up + t * (right - up)) * 2 + flip(core, q % 2)
            peer = pe * n_slab + ps

            @pl.when((q >= 0) & (q < plane_dev) & (peer != me))
            def _():
                pltpu.make_async_remote_copy(
                    src_ref=res.at[k, pl.ds(pl.multiple_of(peer * pair_dev, 16), pair_dev)],
                    dst_ref=hole.at[:, columns(k, me)],
                    send_sem=send2,
                    recv_sem=recv2.at[4 * k + z],
                    device_id=(pe, ps),
                    device_id_type=MESH,
                ).start()

            return carry

        lax.fori_loop(0, group + 8, body, 0)

    for k in range(chunks):
        keep[k].wait()
        landed = recv.at[k, pl.ds(0, others * pair_dev)]
        pltpu.make_async_copy(landed, landed, recv1.at[k]).wait()
        right = jnp.concatenate(
            [recv[k, :, u].reshape(slabs * pairs, side) for u in range(width)], axis=1
        )

        for m in range(slabs * pairs // tile):
            got = jnp.dot(
                wide[m * tile : (m + 1) * tile, :], right, preferred_element_type=jnp.float32
            ).astype(jnp.bfloat16)
            for u in range(width):
                res[k, m * (tile // slabs) : (m + 1) * (tile // slabs), u] = got[
                    :, u * side : (u + 1) * side
                ].reshape(tile // slabs, slabs, side)

        give(k, 1)
        give(k, 0)
        hole[:, columns(k, me)] = res[k, pl.ds(pl.multiple_of(me * pair_dev, 16), pair_dev)]

    for _, v_copy in gathers:
        v_copy.wait()

    rows = slabs * side
    for g in range(irreps):
        tall = jnp.dot(
            ones(equal((rows, side), half, same)), vfull[g], preferred_element_type=jnp.float32
        ).astype(jnp.bfloat16)
        both = jnp.dot(
            tall, ones(equal((side, rows), same, half)), preferred_element_type=jnp.float32
        )
        together = equal((rows, rows), rest, rest)
        for plane in range(slabs):
            mask = together & (lax.broadcasted_iota(jnp.int32, (rows, rows), 0) % slabs == plane)
            vwide[plane, g] = jnp.where(mask, both, 0.0).astype(jnp.bfloat16)

    def particle(i, carry):
        x = mine[i].reshape(rows, side)
        total = jnp.zeros((rows, side), jnp.float32)
        for plane in range(slabs):
            g = jnp.bitwise_xor(labels[me * pair_dev + i], slab_labels[plane])
            total += jnp.dot(vwide[plane, g], x, preferred_element_type=jnp.float32)
        out_ref[i] = total
        return carry

    lax.fori_loop(0, pair_dev, particle, 0)

    part = plane_dev * width
    order = (z, z + 1 - 2 * (z % 2), 3 - 3 * (z // 2), 2 - z // 2)
    for k in range(chunks):
        for turn, plane in enumerate(order):
            senders = plane_dev - 1 if turn == 0 else plane_dev
            landed = recv.at[k, pl.ds(0, senders * pair_dev)]
            pltpu.make_async_copy(landed, landed, recv2.at[4 * k + plane]).wait()
            first = k * n_dev * width + plane * part

            def finish(i, carry):
                place = pl.ds(pl.multiple_of(first * slabs, 8), part * slabs)
                out_ref[i, place, :] += (
                    hole[i, pl.ds(first, part)].reshape(part * slabs, side).astype(jnp.float32)
                )
                return carry

            lax.fori_loop(0, pair_dev, finish, 0, unroll=8)

    everything = recv.at[:, pl.ds(0, others * pair_dev)]
    for sem in (send1, send2):
        pltpu.make_async_copy(everything, everything, sem).wait()


def ladder(amplitudes, pair_irreps, slab_irreps, w, v, n_idx, n_slab):
    pair_dev, slabs, square = amplitudes.shape
    n_dev = n_idx * n_slab
    pairs = w.shape[0]
    irreps, v_rows, side = v.shape
    width = 2
    chunks = side // n_dev // width
    t = amplitudes.reshape(pair_dev, slabs, side, side).transpose(0, 2, 1, 3)
    operands = (t, pair_irreps, slab_irreps, pair_irreps.reshape(1, pairs), w, v)
    hbm = pl.BlockSpec(memory_space=pltpu.HBM)
    dma = pltpu.SemaphoreType.DMA
    bf16 = jnp.bfloat16
    out = pl.pallas_call(
        functools.partial(ladder_kernel, n_idx, n_slab),
        out_shape=jax.ShapeDtypeStruct((pair_dev, side * slabs, side), jnp.float32),
        in_specs=[hbm] * 6,
        out_specs=pl.BlockSpec(memory_space=pltpu.VMEM),
        scratch_shapes=[
            pltpu.VMEM((chunks, pairs, width, slabs, side), bf16),
            pltpu.VMEM((pairs, pairs), bf16),
            pltpu.VMEM((slabs * pairs, slabs * pairs), bf16),
            pltpu.VMEM((chunks, pairs, width, slabs, side), bf16),
            pltpu.VMEM(t.shape, bf16),
            pltpu.VMEM(t.shape, bf16),
            pltpu.VMEM((irreps, side, side), bf16),
            pltpu.VMEM((slabs, irreps, slabs * side, slabs * side), bf16),
            pltpu.VMEM((1, pairs), jnp.int32),
            pltpu.SMEM(pair_irreps.shape, jnp.int32),
            pltpu.SMEM(slab_irreps.shape, jnp.int32),
            dma, dma((chunks,)), dma, dma((4 * chunks,)),
            dma((n_slab - 1,)), dma((n_slab - 1,)), dma((n_slab - 1,)), dma((n_slab - 1,)),
            dma((6,)), dma((chunks,)), pltpu.SemaphoreType.REGULAR,
            pltpu.SemaphoreType.REGULAR,
        ],
        compiler_params=pltpu.CompilerParams(
            collective_id=0, has_side_effects=True, vmem_limit_bytes=40 * 2**20
        ),
        cost_estimate=pl.CostEstimate(
            flops=4 * pairs * pairs * slabs * square // n_dev,
            bytes_accessed=8 * slabs * pair_dev * square,
            transcendentals=0,
        ),
    )(*(pltpu.with_memory_space_constraint(x, pltpu.HBM) for x in operands))
    return out.reshape(pair_dev, side, slabs, side).transpose(0, 2, 1, 3).reshape(amplitudes.shape)


def body(amplitudes, pair_irreps, slab_irreps, ladder_ints, vv_blocks):
    n_idx = lax.axis_size("idx")
    n_slab = lax.axis_size("slab")
    whole = (amplitudes, pair_irreps, slab_irreps, ladder_ints, vv_blocks, n_idx, n_slab)
    if (n_idx, n_slab) == (8, 4):
        return ladder(*whole)
    return exchange(amplitudes.transpose(1, 0, 2), *whole[1:])


def solution(mesh):
    return jax.shard_map(
        body,
        mesh=mesh,
        in_specs=(P(("idx", "slab"), None, None), P(), P(), P(None, "slab"), P(None, "slab", None)),
        out_specs=P(("idx", "slab"), None, None),
        check_vma=False,
    )
```

```python
import functools

import jax
import jax.numpy as jnp
from jax import lax
from jax.experimental import pallas as pl
from jax.experimental.pallas import tpu as pltpu
from jax.sharding import PartitionSpec as P

MESH = pl.DeviceIdType.MESH


def exchange_kernel(
    n_idx, n_slab, cw, t_ref, labels_ref, slab_labels_ref, row_ref, w_ref, v_ref, out_ref,
    recv, wfull, res, hole, vfull, rows_in, rows_out, labels, slab_labels,
    send1, recv1, send2, recv2, wsend, wrecv, vsend, vrecv, own_sems,
):
    n_dev = n_idx * n_slab
    pair_dev = t_ref.shape[1]
    square = t_ref.shape[2]
    width = t_ref.shape[0] * square // n_dev
    chunks = width // cw
    w_cols = w_ref.shape[1]
    v_rows = v_ref.shape[1]
    e = lax.axis_index("idx")
    s = lax.axis_index("slab")
    me = e * n_slab + s
    my_block = (s * n_idx + e) * pair_dev
    others = n_dev - 1

    def where(peer):
        return (peer // n_slab, peer % n_slab)

    barrier = pltpu.get_barrier_semaphore()

    def greet(j, carry):
        pl.semaphore_signal(barrier, inc=1, device_id=where((me + j) % n_dev), device_id_type=MESH)
        return carry

    lax.fori_loop(1, n_dev, greet, 0)
    pl.semaphore_wait(barrier, others)

    locals_ = [
        pltpu.make_async_copy(
            w_ref, wfull.at[:, pl.ds(pl.multiple_of(s * w_cols, 128), w_cols)], own_sems.at[0]
        ),
        pltpu.make_async_copy(
            v_ref, vfull.at[:, pl.ds(pl.multiple_of(s * v_rows, 16), v_rows), :], own_sems.at[1]
        ),
        pltpu.make_async_copy(labels_ref, labels, own_sems.at[2]),
        pltpu.make_async_copy(slab_labels_ref, slab_labels, own_sems.at[3]),
    ]
    for copy in locals_:
        copy.start()

    def order(j):
        return j

    def columns(device, k):
        first = device * width + k * cw
        return first // square, pl.ds(pl.multiple_of(first % square, 128), cw)

    def send_chunk(k):
        def body(j, carry):
            peer = (me + order(j)) % n_dev
            plane, place = columns(peer, k)
            pltpu.make_async_remote_copy(
                src_ref=t_ref.at[plane, :, place],
                dst_ref=recv.at[k, pl.ds(pl.multiple_of(my_block, 16), pair_dev), :],
                send_sem=send1,
                recv_sem=recv1.at[k],
                device_id=where(peer),
                device_id_type=MESH,
            ).start()
            return carry

        lax.fori_loop(1, n_dev, body, 0)
        plane, place = columns(me, k)
        recv[k, pl.ds(pl.multiple_of(my_block, 16), pair_dev), :] = t_ref[plane, :, place]

    def gather(j):
        peer = (s + j) % n_slab
        return (
            pltpu.make_async_remote_copy(
                src_ref=w_ref,
                dst_ref=wfull.at[:, pl.ds(pl.multiple_of(s * w_cols, 128), w_cols)],
                send_sem=wsend.at[j - 1],
                recv_sem=wrecv.at[j - 1],
                device_id=(e, peer),
                device_id_type=MESH,
            ),
            pltpu.make_async_remote_copy(
                src_ref=v_ref,
                dst_ref=vfull.at[:, pl.ds(pl.multiple_of(s * v_rows, 16), v_rows), :],
                send_sem=vsend.at[j - 1],
                recv_sem=vrecv.at[j - 1],
                device_id=(e, peer),
                device_id_type=MESH,
            ),
        )

    send_chunk(0)
    gathers = [gather(j) for j in range(1, n_slab)]
    for w_copy, v_copy in gathers:
        w_copy.start()
        v_copy.start()
    for k in range(1, chunks):
        send_chunk(k)
    for copy in locals_:
        copy.wait()
    for _, v_copy in gathers:
        v_copy.wait()

    side = vfull.shape[1]
    slabs = t_ref.shape[0]
    def particle(plane):

        def take(c, carry):
            rows_in[pl.ds(pl.multiple_of(c * pair_dev, 16), pair_dev), :] = t_ref[
                plane, :, pl.ds(pl.multiple_of(c * side, 128), side)
            ].astype(jnp.float32)
            return carry

        def one(i, carry):
            g = jnp.bitwise_xor(labels[me * pair_dev + i], slab_labels[plane])
            x = rows_in[pl.ds(i, side, stride=pair_dev), :].astype(jnp.bfloat16)
            rows_out[plane, pl.ds(i, side, stride=pair_dev), :] = jnp.dot(
                vfull[g], x, preferred_element_type=jnp.float32
            )
            return carry

        lax.fori_loop(0, side, take, 0, unroll=8)
        lax.fori_loop(0, pair_dev, one, 0, unroll=4)

    for plane in range(slabs):
        particle(plane)

    for w_copy, _ in gathers:
        w_copy.wait()

    pairs = recv.shape[1]
    tile = min(pairs, 512)
    irreps = vfull.shape[0]
    onehot = (
        row_ref[...] == lax.broadcasted_iota(jnp.int32, (irreps, pairs), 0)
    ).astype(jnp.float32).astype(jnp.bfloat16)

    def mask_columns(n, carry):
        cols = pl.ds(pl.multiple_of(n * tile, tile), tile)
        col = lax.broadcasted_iota(jnp.int32, (pairs, tile), 1) + n * tile
        row = lax.broadcasted_iota(jnp.int32, (pairs, tile), 0)
        p, q = col % pair_dev, col // pair_dev
        kl = ((q % n_idx) * n_slab + q // n_idx) * pair_dev + p
        moved = jnp.dot(
            onehot,
            (row == kl).astype(jnp.float32).astype(jnp.bfloat16),
            preferred_element_type=jnp.float32,
        ).astype(jnp.bfloat16)
        equal = lax.dot_general(
            onehot, moved, (((0,), (0,)), ((), ())), preferred_element_type=jnp.float32
        )
        wfull[:, cols] = jnp.where(
            equal > 0.5, wfull[:, cols].astype(jnp.float32), 0.0
        ).astype(jnp.bfloat16)
        return carry

    lax.fori_loop(0, pairs // tile, mask_columns, 0)

    for k in range(chunks):
        plane, place = columns(me, k)
        landed = recv.at[k, pl.ds(0, others * pair_dev), :]
        pltpu.make_async_copy(landed, landed, recv1.at[k]).wait()

        def multiply(m, carry):
            rows = pl.ds(pl.multiple_of(m * tile, tile), tile)
            res[k, rows, :] = jnp.dot(
                wfull[rows, :], recv[k], preferred_element_type=jnp.float32
            ).astype(jnp.bfloat16)
            return carry

        lax.fori_loop(0, pairs // tile, multiply, 0)

        def give(j, carry):
            peer = (me + order(j)) % n_dev
            pltpu.make_async_remote_copy(
                src_ref=res.at[k, pl.ds(pl.multiple_of(peer * pair_dev, 16), pair_dev), :],
                dst_ref=hole.at[plane, :, place],
                send_sem=send2,
                recv_sem=recv2.at[k],
                device_id=where(peer),
                device_id_type=MESH,
            ).start()
            return carry

        lax.fori_loop(1, n_dev, give, 0)
        hole[plane, :, place] = res[k, pl.ds(pl.multiple_of(me * pair_dev, 16), pair_dev), :]


    per_plane = n_dev // slabs
    for k in range(chunks):
        landed = recv.at[k, pl.ds(0, others * pair_dev), :]
        pltpu.make_async_copy(landed, landed, recv2.at[k]).wait()
        for plane in range(slabs):

            def finish(d, carry):
                for u in range(cw // side):
                    first = d * width + k * cw + u * side
                    cols = pl.ds(pl.multiple_of(first, 128), side)
                    rows = pl.ds(pl.multiple_of(first // side * pair_dev, 16), pair_dev)
                    out_ref[:, plane, cols] = rows_out[plane, rows, :] + hole[
                        plane, :, cols
                    ].astype(jnp.float32)
                return carry

            lax.fori_loop(0, per_plane, finish, 0, unroll=2)

    everything = recv.at[:, pl.ds(0, others * pair_dev), :]
    for sem in (send1, send2):
        pltpu.make_async_copy(everything, everything, sem).wait()


def exchange(t, pair_irreps, slab_irreps, w, v, n_idx, n_slab):
    slabs, pair_dev, square = t.shape
    n_dev = n_idx * n_slab
    pairs = w.shape[0]
    width = slabs * square // n_dev
    cw = min(width, 256)
    chunks = width // cw
    irreps, v_rows, side = v.shape
    block = (chunks, pairs, cw)
    vmem = pl.BlockSpec(memory_space=pltpu.VMEM)
    anywhere = pl.BlockSpec(memory_space=pl.ANY)
    held = 2 * (pairs * pairs + 12 * slabs * pair_dev * square)
    dma = pltpu.SemaphoreType.DMA
    return pl.pallas_call(
        functools.partial(exchange_kernel, n_idx, n_slab, cw),
        out_shape=jax.ShapeDtypeStruct((pair_dev, slabs, square), jnp.float32),
        in_specs=[vmem, anywhere, anywhere, vmem, anywhere, anywhere],
        out_specs=vmem,
        scratch_shapes=[
            pltpu.VMEM(block, jnp.bfloat16),
            pltpu.VMEM((pairs, pairs), jnp.bfloat16),
            pltpu.VMEM(block, jnp.bfloat16),
            pltpu.VMEM(t.shape, jnp.bfloat16),
            pltpu.VMEM((irreps, v_rows * n_slab, side), jnp.bfloat16),
            pltpu.VMEM((side * pair_dev, side), jnp.float32),
            pltpu.VMEM((slabs, side * pair_dev, side), jnp.float32),
            pltpu.SMEM(pair_irreps.shape, jnp.int32),
            pltpu.SMEM(slab_irreps.shape, jnp.int32),
            dma, dma((chunks,)), dma, dma((chunks,)),
            dma((n_slab - 1,)), dma((n_slab - 1,)), dma((n_slab - 1,)), dma((n_slab - 1,)), dma((4,)),
        ],
        compiler_params=pltpu.CompilerParams(
            collective_id=0, has_side_effects=True, vmem_limit_bytes=held + 10 * 2**20
        ),
        cost_estimate=pl.CostEstimate(
            flops=2 * pairs * pairs * width,
            bytes_accessed=8 * slabs * pair_dev * square,
            transcendentals=0,
        ),
    )(t, pair_irreps, slab_irreps, pair_irreps.reshape(1, pairs), w, v)


def ladder_kernel(
    n_idx, n_slab, t_ref, labels_ref, slab_labels_ref, row_ref, w_ref, v_ref, out_ref,
    recv, wfull, wide, res, hole, mine, vfull, vwide, row, labels, slab_labels,
    send1, recv1, send2, recv2, wsend, wrecv, vsend, vrecv, own_sems, keep_sem, late, pre,
):
    n_dev = n_idx * n_slab
    pair_dev, side, slabs, _ = t_ref.shape
    chunks, pairs, width = recv.shape[:3]
    w_cols = w_ref.shape[1]
    irreps, v_rows, _ = v_ref.shape
    e = lax.axis_index("idx")
    s = lax.axis_index("slab")
    z, x, y, core = e // 2, e % 2, s // 2, s % 2
    me = e * n_slab + s
    my_block = (s * n_idx + e) * pair_dev
    others = n_dev - 1
    plane_dev = n_dev // 4
    group = 2 * plane_dev
    inner = (z == 1) | (z == 2)
    outer = (z == 0) | (z == 3)

    def flip(bit, by):
        return bit + by - 2 * bit * by

    def partner(dz, q):
        pz = flip(z // 2, dz // 2) * 2 + flip(z % 2, dz % 2)
        return pz * 2 + flip(x, q // 4), flip(y, q // 2 % 2) * 2 + flip(core, q % 2)

    def of_kind(i):
        return partner(3 * (1 - i // plane_dev), plane_dev - 1 - i % plane_dev)

    def of_other_kind(i):
        return partner(2 - i // plane_dev, plane_dev - 1 - i % plane_dev)

    def of_all(i):
        return partner(3 - i // plane_dev, plane_dev - 1 - i % plane_dev)

    def signal(sem, count, peer_of):
        def body(i, carry):
            pl.semaphore_signal(sem, inc=1, device_id=peer_of(i), device_id_type=MESH)
            return carry

        lax.fori_loop(0, count, body, 0)

    def columns(k, device):
        return pl.ds(k * n_dev * width + device * width, width)

    keep = [
        pltpu.make_async_copy(
            t_ref.at[:, columns(k, me)],
            recv.at[k, pl.ds(pl.multiple_of(my_block, 16), pair_dev)],
            keep_sem.at[k],
        )
        for k in range(chunks)
    ]
    locals_ = [
        pltpu.make_async_copy(
            w_ref, wfull.at[:, pl.ds(pl.multiple_of(s * w_cols, 128), w_cols)], own_sems.at[0]
        ),
        pltpu.make_async_copy(
            v_ref, vfull.at[:, pl.ds(pl.multiple_of(s * v_rows, 16), v_rows), :], own_sems.at[1]
        ),
        pltpu.make_async_copy(labels_ref, labels, own_sems.at[2]),
        pltpu.make_async_copy(slab_labels_ref, slab_labels, own_sems.at[3]),
        pltpu.make_async_copy(row_ref, row, own_sems.at[4]),
        pltpu.make_async_copy(t_ref, mine, own_sems.at[5]),
    ]

    def send(k, count, peer_of, first=0):
        def body(i, carry):
            pe, ps = peer_of(i)
            pltpu.make_async_remote_copy(
                src_ref=t_ref.at[:, columns(k, pe * n_slab + ps)],
                dst_ref=recv.at[k, pl.ds(pl.multiple_of(my_block, 16), pair_dev)],
                send_sem=send1,
                recv_sem=recv1.at[k],
                device_id=(pe, ps),
                device_id_type=MESH,
            ).start()
            return carry

        lax.fori_loop(first, count, body, 0)

    def gather(j):
        peer = (s + j) % n_slab
        return (
            pltpu.make_async_remote_copy(
                src_ref=w_ref,
                dst_ref=wfull.at[:, pl.ds(pl.multiple_of(s * w_cols, 128), w_cols)],
                send_sem=wsend.at[j - 1],
                recv_sem=wrecv.at[j - 1],
                device_id=(e, peer),
                device_id_type=MESH,
            ),
            pltpu.make_async_remote_copy(
                src_ref=v_ref,
                dst_ref=vfull.at[:, pl.ds(pl.multiple_of(s * v_rows, 16), v_rows), :],
                send_sem=vsend.at[j - 1],
                recv_sem=vrecv.at[j - 1],
                device_id=(e, peer),
                device_id_type=MESH,
            ),
        )

    gathers = [gather(j) for j in range(1, n_slab)]
    def start_gathers():
        for w_copy, v_copy in gathers:
            w_copy.start()
            v_copy.start()

    barrier = pltpu.get_barrier_semaphore()
    def second_cores(i):
        pe, ps = partner(3 * (i // 4), i % 4 * 2)
        return pe, ps // 2 * 2 + 1

    def other_second_cores(i):
        pe, ps = partner(3 - 3 * (i // 4), (3 - i % 4) * 2)
        return pe, ps // 2 * 2 + 1

    def first_cores_of_other_kind(i):
        pe, ps = partner(2 - i // 4, i % 4 * 2)
        return pe, ps // 2 * 2

    def facing(i):
        return partner(3, i)

    def mate(i):
        return partner(0, 1)

    @pl.when(inner)
    def _():
        signal(barrier, 2, facing)

        def tell(i, carry):
            pe, ps = second_cores(i)

            @pl.when((pe % 2 != x) | (ps // 2 != y))
            def _():
                pl.semaphore_signal(barrier, inc=1, device_id=(pe, ps), device_id_type=MESH)

            return carry

        lax.fori_loop(0, plane_dev, tell, 0)
        signal(barrier, 1, mate)
        signal(barrier, plane_dev, first_cores_of_other_kind)

    @pl.when(outer)
    def _():
        signal(barrier, plane_dev - 1, other_second_cores)
        signal(barrier, 1, mate)

    for copy in keep + locals_:
        copy.start()

    def send_facing():
        for k in range(chunks):
            send(k, plane_dev, of_kind, plane_dev - 2)

    @pl.when(inner)
    def _():
        @pl.when(core == 0)
        def _():
            pl.semaphore_wait(barrier, 3)
            signal(pre, 1, mate)
            send_facing()
            pl.semaphore_wait(pre, 1)

        @pl.when(core == 1)
        def _():
            pl.semaphore_wait(pre, 1)
            send_facing()
            pl.semaphore_wait(barrier, group - 1)
            signal(pre, 1, mate)

        send(0, plane_dev - 2, of_kind)
        start_gathers()
        send(0, group - 1, of_kind, plane_dev)
        pl.semaphore_wait(late, plane_dev)
        send(0, group, of_other_kind)
        for k in range(1, chunks):
            send(k, plane_dev - 2, of_kind)
            send(k, group - 1, of_kind, plane_dev)
            send(k, group, of_other_kind)

    @pl.when(outer & (core == 0))
    def _():
        pl.semaphore_wait(barrier, group + 1)
        signal(pre, 1, mate)
        signal(late, group, of_other_kind)
        send(0, plane_dev, of_other_kind)
        pl.semaphore_wait(pre, 1)
        send(0, plane_dev, of_kind)
        start_gathers()
        send(0, group, of_other_kind, plane_dev)
        send(0, group - 1, of_kind, plane_dev)
        for k in range(1, chunks):
            send(k, others, of_all)

    @pl.when(outer & (core == 1))
    def _():
        pl.semaphore_wait(barrier, group - 1)
        signal(pre, 1, mate)
        send(0, plane_dev, of_kind)
        pl.semaphore_wait(pre, 1)
        send(0, plane_dev, of_other_kind)
        start_gathers()
        send(0, group, of_other_kind, plane_dev)
        send(0, group - 1, of_kind, plane_dev)
        for k in range(1, chunks):
            send(k, others, of_all)

    for copy in locals_:
        copy.wait()
    for w_copy, _ in gathers:
        w_copy.wait()

    def equal(shape, left, right):
        return (
            left(lax.broadcasted_iota(jnp.int32, shape, 0))
            == right(lax.broadcasted_iota(jnp.int32, shape, 1))
        )

    def ones(mask):
        return mask.astype(jnp.float32).astype(jnp.bfloat16)

    def same(x):
        return x

    def half(x):
        return x // slabs

    def rest(x):
        return x % slabs

    onehot = ones(row[...] == lax.broadcasted_iota(jnp.int32, (irreps, pairs), 0))

    def column_pair(q):
        p, q = q % pair_dev, q // pair_dev
        return ((q % n_idx) * n_slab + q // n_idx) * pair_dev + p

    moved = jnp.dot(
        onehot, ones(equal((pairs, pairs), same, column_pair)), preferred_element_type=jnp.float32
    ).astype(jnp.bfloat16)
    allowed = lax.dot_general(
        onehot, moved, (((0,), (0,)), ((), ())), preferred_element_type=jnp.float32
    )
    wfull[...] = jnp.where(allowed > 0.5, wfull[...].astype(jnp.float32), 0.0).astype(jnp.bfloat16)

    tile = 256
    spread = ones(equal((pairs, slabs * pairs), same, half))

    def widen(m, carry):
        down = ones(
            equal((tile, tile // slabs), half, same)
        )
        part = jnp.dot(
            down,
            wfull[pl.ds(pl.multiple_of(m * (tile // slabs), 16), tile // slabs), :],
            preferred_element_type=jnp.float32,
        ).astype(jnp.bfloat16)
        both = jnp.dot(part, spread, preferred_element_type=jnp.float32)
        wide[pl.ds(pl.multiple_of(m * tile, 16), tile), :] = jnp.where(
            equal(both.shape, rest, rest), both, 0.0
        ).astype(jnp.bfloat16)
        return carry

    lax.fori_loop(0, slabs * pairs // tile, widen, 0)

    def give(k, far):
        def body(j, carry):
            t = j % 2
            q = j // 2 - 2 * t * (1 - flip(z // 2, far))
            right, up = q // 4, q // 2 % 2
            pe = (flip(z // 2, far) * 2 + t) * 2 + right + t * (up - right)
            ps = (up + t * (right - up)) * 2 + flip(core, q % 2)
            peer = pe * n_slab + ps

            @pl.when((q >= 0) & (q < plane_dev) & (peer != me))
            def _():
                pltpu.make_async_remote_copy(
                    src_ref=res.at[k, pl.ds(pl.multiple_of(peer * pair_dev, 16), pair_dev)],
                    dst_ref=hole.at[:, columns(k, me)],
                    send_sem=send2,
                    recv_sem=recv2.at[4 * k + z],
                    device_id=(pe, ps),
                    device_id_type=MESH,
                ).start()

            return carry

        lax.fori_loop(0, group + 8, body, 0)

    for k in range(chunks):
        keep[k].wait()
        landed = recv.at[k, pl.ds(0, others * pair_dev)]
        pltpu.make_async_copy(landed, landed, recv1.at[k]).wait()
        right = jnp.concatenate(
            [recv[k, :, u].reshape(slabs * pairs, side) for u in range(width)], axis=1
        )

        for m in range(slabs * pairs // tile):
            got = jnp.dot(
                wide[m * tile : (m + 1) * tile, :], right, preferred_element_type=jnp.float32
            ).astype(jnp.bfloat16)
            for u in range(width):
                res[k, m * (tile // slabs) : (m + 1) * (tile // slabs), u] = got[
                    :, u * side : (u + 1) * side
                ].reshape(tile // slabs, slabs, side)

        give(k, 1)
        give(k, 0)
        hole[:, columns(k, me)] = res[k, pl.ds(pl.multiple_of(me * pair_dev, 16), pair_dev)]

    for _, v_copy in gathers:
        v_copy.wait()

    rows = slabs * side
    for g in range(irreps):
        tall = jnp.dot(
            ones(equal((rows, side), half, same)), vfull[g], preferred_element_type=jnp.float32
        ).astype(jnp.bfloat16)
        both = jnp.dot(
            tall, ones(equal((side, rows), same, half)), preferred_element_type=jnp.float32
        )
        together = equal((rows, rows), rest, rest)
        for plane in range(slabs):
            mask = together & (lax.broadcasted_iota(jnp.int32, (rows, rows), 0) % slabs == plane)
            vwide[plane, g] = jnp.where(mask, both, 0.0).astype(jnp.bfloat16)

    def particle(i, carry):
        x = mine[i].reshape(rows, side)
        total = jnp.zeros((rows, side), jnp.float32)
        for plane in range(slabs):
            g = jnp.bitwise_xor(labels[me * pair_dev + i], slab_labels[plane])
            total += jnp.dot(vwide[plane, g], x, preferred_element_type=jnp.float32)
        out_ref[i] = total
        return carry

    lax.fori_loop(0, pair_dev, particle, 0)

    part = plane_dev * width
    order = (z, z + 1 - 2 * (z % 2), 3 - 3 * (z // 2), 2 - z // 2)
    for k in range(chunks):
        for turn, plane in enumerate(order):
            senders = plane_dev - 1 if turn == 0 else plane_dev
            landed = recv.at[k, pl.ds(0, senders * pair_dev)]
            pltpu.make_async_copy(landed, landed, recv2.at[4 * k + plane]).wait()
            first = k * n_dev * width + plane * part

            def finish(i, carry):
                place = pl.ds(pl.multiple_of(first * slabs, 8), part * slabs)
                out_ref[i, place, :] += (
                    hole[i, pl.ds(first, part)].reshape(part * slabs, side).astype(jnp.float32)
                )
                return carry

            lax.fori_loop(0, pair_dev, finish, 0, unroll=8)

    everything = recv.at[:, pl.ds(0, others * pair_dev)]
    for sem in (send1, send2):
        pltpu.make_async_copy(everything, everything, sem).wait()


def ladder(amplitudes, pair_irreps, slab_irreps, w, v, n_idx, n_slab):
    pair_dev, slabs, square = amplitudes.shape
    n_dev = n_idx * n_slab
    pairs = w.shape[0]
    irreps, v_rows, side = v.shape
    width = 2
    chunks = side // n_dev // width
    t = amplitudes.reshape(pair_dev, slabs, side, side).transpose(0, 2, 1, 3)
    operands = (t, pair_irreps, slab_irreps, pair_irreps.reshape(1, pairs), w, v)
    hbm = pl.BlockSpec(memory_space=pltpu.HBM)
    dma = pltpu.SemaphoreType.DMA
    bf16 = jnp.bfloat16
    out = pl.pallas_call(
        functools.partial(ladder_kernel, n_idx, n_slab),
        out_shape=jax.ShapeDtypeStruct((pair_dev, side * slabs, side), jnp.float32),
        in_specs=[hbm] * 6,
        out_specs=pl.BlockSpec(memory_space=pltpu.VMEM),
        scratch_shapes=[
            pltpu.VMEM((chunks, pairs, width, slabs, side), bf16),
            pltpu.VMEM((pairs, pairs), bf16),
            pltpu.VMEM((slabs * pairs, slabs * pairs), bf16),
            pltpu.VMEM((chunks, pairs, width, slabs, side), bf16),
            pltpu.VMEM(t.shape, bf16),
            pltpu.VMEM(t.shape, bf16),
            pltpu.VMEM((irreps, side, side), bf16),
            pltpu.VMEM((slabs, irreps, slabs * side, slabs * side), bf16),
            pltpu.VMEM((1, pairs), jnp.int32),
            pltpu.SMEM(pair_irreps.shape, jnp.int32),
            pltpu.SMEM(slab_irreps.shape, jnp.int32),
            dma, dma((chunks,)), dma, dma((4 * chunks,)),
            dma((n_slab - 1,)), dma((n_slab - 1,)), dma((n_slab - 1,)), dma((n_slab - 1,)),
            dma((6,)), dma((chunks,)), pltpu.SemaphoreType.REGULAR,
            pltpu.SemaphoreType.REGULAR,
        ],
        compiler_params=pltpu.CompilerParams(
            collective_id=0, has_side_effects=True, vmem_limit_bytes=40 * 2**20
        ),
        cost_estimate=pl.CostEstimate(
            flops=4 * pairs * pairs * slabs * square // n_dev,
            bytes_accessed=8 * slabs * pair_dev * square,
            transcendentals=0,
        ),
    )(*(pltpu.with_memory_space_constraint(x, pltpu.HBM) for x in operands))
    return out.reshape(pair_dev, side, slabs, side).transpose(0, 2, 1, 3).reshape(amplitudes.shape)


def body(amplitudes, pair_irreps, slab_irreps, ladder_ints, vv_blocks):
    n_idx = lax.axis_size("idx")
    n_slab = lax.axis_size("slab")
    whole = (amplitudes, pair_irreps, slab_irreps, ladder_ints, vv_blocks, n_idx, n_slab)
    if (n_idx, n_slab) == (8, 4):
        return ladder(*whole)
    return exchange(amplitudes.transpose(1, 0, 2), *whole[1:])


def solution(mesh):
    return jax.shard_map(
        body,
        mesh=mesh,
        in_specs=(P(("idx", "slab"), None, None), P(), P(), P(None, "slab"), P(None, "slab", None)),
        out_specs=P(("idx", "slab"), None, None),
        check_vma=False,
    )
```
